32 devices in a mesh: gx: 2 (over y), gy: 4 (over z), gz: 4 (over x, core).
Axes of the slice: x: 2, y: 2, z: 4, core: 2. Of those that a mesh axis runs over, the one named last changes fastest.
Arguments:
- right_side: float32 [8, 8, 2048], P('gx', 'gy', 'gz'), may hold values from -24 to 24
- element_class: int32 [8, 8, 32], P('gx', 'gy', 'gz'), may hold values from 0 to 15
- class_blocks: float32 [16, 64, 64], replicated, may hold values from -0.05 to 11, as said below
- class_shift: float32 [16], replicated, may hold values from 0.5 to 4
- face_weights: float32 [3], replicated, may hold values from 0.4 to 0.9
Outputs:
- solution_field: float32 [8, 8, 2048], P('gx', 'gy', 'gz')
- residual: float32 [8, 8, 2048], P('gx', 'gy', 'gz')
The draws below stay inside these ranges and needn't reach their ends.
Inputs may be any that keep to these rules, and one draw needn't show every extreme that they name: `class_blocks`: each block is symmetric, and each diagonal entry exceeds the sum of magnitudes of the other entries of its row by 3 or more.
All inputs are finite; a program needn't handle non-finite values.
Results may differ from the reference program's by a relative error of at most 0.00027.
Values sent between devices are 32-bit elements; how exact they have to be, the bound alone decides.
A program may use at most 64 MiB of HBM per device.

```python
import math
import jax
import jax.numpy as jnp
from jax import lax

CX = 4
CY = 2
CZ = 8
P_SIZE = 64
K = 16
SWEEPS = 4
NX = 8
NY = 8
NZ = 32
N_GX = 2
N_GY = 4
N_GZ = 4


def draw_class_blocks(key, part):
    key = jax.random.fold_in(key, 11)
    first_key, second_key = jax.random.split(key)
    raw_entries = jax.random.uniform(first_key, (K, P_SIZE, P_SIZE), jnp.float32, -0.05, 0.05)
    symmetric = 0.5 * (raw_entries + jnp.swapaxes(raw_entries, 1, 2))
    identity = jnp.eye(P_SIZE, dtype=jnp.float32)
    margin = jax.random.uniform(second_key, (K, P_SIZE), jnp.float32, 1.0, 4.0)
    diagonal = 0.05 * (P_SIZE - 1) + 3.0 + margin
    return symmetric * (1.0 - identity) + identity * diagonal[:, :, None]


def plant(entries, rng, least, largest):
    longest = entries.shape.index(max(entries.shape))
    spots = []
    for shift in (0, 1):
        where = [jax.random.randint(jax.random.fold_in(rng, axis), (), 0, length) for axis, length in enumerate(entries.shape)]
        where[longest] = (where[longest] + shift) % entries.shape[longest]
        spots.append(tuple(where))
    return entries.at[spots[0]].set(least).at[spots[1]].set(largest)


def block_levels(own_key, dims, cuts, low, top_value):
    gain, own = 1.0, jax.random.fold_in(own_key, 6)
    for axis_at, shards_of in cuts:
        steps = jnp.exp(jax.random.uniform(jax.random.fold_in(own, axis_at), (shards_of,), jnp.float32, low / len(cuts), top_value / len(cuts)))
        gain = gain * jnp.repeat(steps, dims[axis_at] // shards_of).reshape([-1 if axis == axis_at else 1 for axis in range(len(dims))])
    return gain


def noise(key, shape, scale, bound, pieces=(), kind=jnp.bfloat16):
    array = jax.random.normal(key, shape, jnp.float32) * scale
    if len(pieces) > 0:
        array = block_levels(key, shape, pieces, -0.22, 0.18) * array
    return jnp.clip(array, min=-bound, max=bound).astype(kind)


def setup_inputs(seed: int = 0) -> dict:
    keys = jax.random.split(jax.random.key(seed), 6)
    return {
        "right_side": noise(keys[0], (NX, NY, NZ * P_SIZE), 4.0, 24.0, ((0, 2), (1, 4), (2, 4)), jnp.float32),
        "element_class": plant(jax.random.randint(keys[1], (NX, NY, NZ), 0, K), jax.random.fold_in(keys[1], 1), 0, K - 1).astype(jnp.int32),
        "class_blocks": draw_class_blocks(jax.random.fold_in(keys[5], 71), 0),
        "class_shift": jnp.clip(jnp.exp(jax.random.uniform(keys[3], (K,), jnp.float32, math.log(0.5), math.log(4.0))), 0.5, 4.0),
        "face_weights": jnp.clip(jax.random.uniform(keys[4], (3,), jnp.float32, 0.4, 0.9), 0.4, 0.9),
    }


highest = lax.Precision.HIGHEST
relax_weight = 0.6


def couple(padded, face_weights):
    middle = padded[1:-1, 1:-1, 1:-1]
    result = jnp.zeros(middle.shape, jnp.float32)
    result = result.at[:, :, :, 3].add(face_weights[0] * padded[2:, 1:-1, 1:-1, 0])
    result = result.at[:, :, :, 0].add(face_weights[0] * padded[:-2, 1:-1, 1:-1, 3])
    result = result.at[:, :, :, :, 3].add(face_weights[1] * padded[1:-1, 2:, 1:-1, :, 0])
    result = result.at[:, :, :, :, 0].add(face_weights[1] * padded[1:-1, :-2, 1:-1, :, 3])
    result = result.at[:, :, :, :, :, 3].add(face_weights[2] * padded[1:-1, 1:-1, 2:, :, :, 0])
    result = result.at[:, :, :, :, :, 0].add(face_weights[2] * padded[1:-1, 1:-1, :-2, :, :, 3])
    return result


def coarsen(values):
    size_x, size_y, size_z = values.shape
    return values.reshape(size_x // 2, 2, size_y // 2, 2, size_z // 2, 2).sum(axis=(1, 3, 5))


def refine(values):
    return jnp.repeat(jnp.repeat(jnp.repeat(values, 2, axis=0), 2, axis=1), 2, axis=2)


def section_apply(values, shift, extent):
    size_x, size_y, size_z = values.shape
    ext_x, ext_y, ext_z = extent
    blocked = values.reshape(size_x // ext_x, ext_x, size_y // ext_y, ext_y, size_z // ext_z, ext_z)
    padded = jnp.pad(blocked, ((0, 0), (1, 1), (0, 0), (1, 1), (0, 0), (1, 1)))
    beside = padded[:, 2:, :, 1:-1, :, 1:-1] + padded[:, :-2, :, 1:-1, :, 1:-1]
    beside = beside + padded[:, 1:-1, :, 2:, :, 1:-1] + padded[:, 1:-1, :, :-2, :, 1:-1]
    beside = beside + padded[:, 1:-1, :, 1:-1, :, 2:] + padded[:, 1:-1, :, 1:-1, :, :-2]
    return (6.0 + shift) * values - beside.reshape(size_x, size_y, size_z)


def extents(depth):
    factor = 2 ** depth
    return (CX * min(N_GX, factor) // factor, CY * min(N_GY, factor) // factor, CZ * min(N_GZ, factor) // factor)


def fine_apply(field, element_class, class_blocks, face_weights):
    elements = field.reshape(NX, NY, NZ, P_SIZE)

    def one_slab(pair):
        slab, marks = pair
        chosen = class_blocks[marks]
        return jnp.einsum("yznm,yzm->yzn", chosen, slab, precision=highest)

    local_part = lax.map(one_slab, (elements, element_class))
    padded = jnp.pad(elements.reshape(NX, NY, NZ, 4, 4, 4), ((1, 1), (1, 1), (1, 1), (0, 0), (0, 0), (0, 0)))
    nearby = couple(padded, face_weights).reshape(NX, NY, NZ, P_SIZE)
    return (local_part - nearby).reshape(NX, NY, NZ * P_SIZE)


def section_cycle(source, shift, depth):
    extent = extents(depth)
    diagonal = 6.0 + shift
    if depth == 3:
        iterate = jnp.zeros_like(source)
        for sweep_index in range(SWEEPS):
            iterate = iterate + relax_weight * (source - section_apply(iterate, shift, extent)) / diagonal
        return iterate
    iterate = relax_weight * source / diagonal
    remainder = source - section_apply(iterate, shift, extent)
    coarse = section_cycle(0.25 * coarsen(remainder), 0.125 * coarsen(shift), depth + 1)
    iterate = iterate + refine(coarse)
    return iterate + relax_weight * (source - section_apply(iterate, shift, extent)) / diagonal


def precondition(source, element_class, class_blocks, face_weights, fine_diagonal, shift_cells):
    iterate = relax_weight * source / fine_diagonal
    remainder = source - fine_apply(iterate, element_class, class_blocks, face_weights)
    sums = remainder.reshape(NX, NY, NZ, P_SIZE).sum(axis=3)
    coarse = section_cycle(coarsen(sums) / float(P_SIZE), 0.125 * coarsen(shift_cells), 1)
    iterate = iterate + jnp.repeat(refine(coarse), P_SIZE, axis=2)
    update = source - fine_apply(iterate, element_class, class_blocks, face_weights)
    return iterate + relax_weight * update / fine_diagonal


def reference(right_side, element_class, class_blocks, class_shift, face_weights):
    table = jnp.diagonal(class_blocks, axis1=1, axis2=2)
    fine_diagonal = table[element_class].reshape(NX, NY, NZ * P_SIZE)
    shift_cells = class_shift[element_class]
    residual = right_side
    smoothed = precondition(residual, element_class, class_blocks, face_weights, fine_diagonal, shift_cells)
    gamma_now = jnp.sum(residual * smoothed)
    direction = smoothed
    image = fine_apply(direction, element_class, class_blocks, face_weights)
    step_size = gamma_now / jnp.sum(direction * image)
    solution_field = step_size * direction
    residual = residual - step_size * image
    smoothed = precondition(residual, element_class, class_blocks, face_weights, fine_diagonal, shift_cells)
    gamma_next = jnp.sum(residual * smoothed)
    direction = smoothed + (gamma_next / gamma_now) * direction
    image = fine_apply(direction, element_class, class_blocks, face_weights)
    step_size = gamma_next / jnp.sum(direction * image)
    solution_field = solution_field + step_size * direction
    residual = residual - step_size * image
    return solution_field, residual
```

```python
import jax
import jax.numpy as jnp
import numpy as np
from jax import lax
from jax.experimental import pallas as pl
from jax.experimental.pallas import tpu as pltpu
from jax.sharding import PartitionSpec as P

P_SIZE = 64
SWEEPS = 4


highest = lax.Precision.HIGHEST
relax_weight = 0.6


def with_halo(x, sides, width):
    for axis, dim in sides:
        size, length = (lax.axis_size(axis), x.shape[dim])
        up = [(i, (i + 1) % size) for i in range(size - 1)]
        down = [(j, i) for i, j in up]
        last = lax.slice_in_dim(x, length - width, length, axis=dim)
        first = lax.slice_in_dim(x, 0, width, axis=dim)
        before = lax.ppermute(last, axis, up)
        after = lax.ppermute(first, axis, down)
        x = jnp.concatenate([before, x, after], axis=dim)
    return x


def partner_2(x, axis, bit):
    return lax.ppermute(x, axis, [(i, i ^ 1 << bit) for i in range(lax.axis_size(axis))])


def face_tables():
    node_ids = np.arange(P_SIZE)
    digits = (node_ids // 16, node_ids // 4 % 4, node_ids % 4)
    strides = (48, 12, 3)
    lower_sets = [node_ids[digits[axis_dim] == 0] for axis_dim in range(3)]
    return (lower_sets, strides)


def full_matrix(face_weights):
    lower_sets, strides = face_tables()
    pieces = []
    for axis_dim in range(3):
        lower_ids = lower_sets[axis_dim]
        upper_ids = lower_ids + strides[axis_dim]
        from_next = np.zeros((P_SIZE, P_SIZE), np.float32)
        from_next[lower_ids, upper_ids] = 1.0
        from_prev = np.zeros((P_SIZE, P_SIZE), np.float32)
        from_prev[upper_ids, lower_ids] = 1.0
        pieces.append(face_weights[axis_dim] * jnp.asarray(from_next))
        pieces.append(face_weights[axis_dim] * jnp.asarray(from_prev))
    return jnp.concatenate(pieces, axis=0)


def couple_full(cubes, face_weights):
    count = cubes.shape[0] * cubes.shape[1] * cubes.shape[2]
    padded = with_halo(cubes, (("gx", 0), ("gy", 1), ("gz", 2)), 1)
    views = [
        padded[2:, 1:-1, 1:-1],
        padded[:-2, 1:-1, 1:-1],
        padded[1:-1, 2:, 1:-1],
        padded[1:-1, :-2, 1:-1],
        padded[1:-1, 1:-1, 2:],
        padded[1:-1, 1:-1, :-2],
    ]
    stacked = jnp.concatenate(views, axis=3).reshape(count, 6 * P_SIZE)
    return jnp.dot(stacked, full_matrix(face_weights), precision=highest)


def coarsen(values):
    size_x, size_y, size_z = values.shape
    return values.reshape(size_x // 2, 2, size_y // 2, 2, size_z // 2, 2).sum(axis=(1, 3, 5))


def refine(values):
    return jnp.repeat(jnp.repeat(jnp.repeat(values, 2, axis=0), 2, axis=1), 2, axis=2)


def section_apply(values, shift):
    padded = jnp.pad(values, ((1, 1), (1, 1), (1, 1)))
    beside = padded[2:, 1:-1, 1:-1] + padded[:-2, 1:-1, 1:-1]
    beside = beside + padded[1:-1, 2:, 1:-1] + padded[1:-1, :-2, 1:-1]
    beside = beside + padded[1:-1, 1:-1, 2:] + padded[1:-1, 1:-1, :-2]
    return (6.0 + shift) * values - beside


def assemble(stacked, depth, layout):
    undo_list = []
    for axis_dim, axis_count, bit_offset, my_index in layout:
        if axis_count >= 2**depth:
            partner = partner_2(stacked, ("gx", "gy", "gz"), bit_offset + depth - 1)
            upper_half = my_index >> depth - 1 & 1 == 1
            half_size = stacked.shape[axis_dim + 1]
            low_first = jnp.concatenate([stacked, partner], axis_dim + 1)
            high_first = jnp.concatenate([partner, stacked], axis_dim + 1)
            stacked = jnp.where(upper_half, high_first, low_first)
            undo_list.append((axis_dim, upper_half, half_size))
    return (stacked, undo_list)


def unpick(values, undo_list):
    for axis_dim, upper_half, half_size in reversed(undo_list):
        values = lax.dynamic_slice_in_dim(
            values, upper_half.astype(jnp.int32) * half_size, half_size, axis_dim
        )
    return values


def fine_apply(field, operator):
    onehot, wide_blocks, face_weights = operator
    size_x, size_y, width = field.shape
    size_z = width // P_SIZE
    count = size_x * size_y * size_z
    classes = onehot.shape[1]
    flat = field.reshape(count, P_SIZE)
    products = jnp.dot(flat, wide_blocks, precision=highest).reshape(count, classes, P_SIZE)
    local_part = jnp.einsum("ekn,ek->en", products, onehot, precision=highest)
    cubes = field.reshape(size_x, size_y, size_z, P_SIZE)
    nearby = couple_full(cubes, face_weights)
    return (local_part - nearby).reshape(size_x, size_y, width)


def section_cycle(source, shift, depth, layout):
    diagonal = 6.0 + shift
    if depth == 3:
        iterate = jnp.zeros_like(source)
        for sweep_index in range(SWEEPS):
            iterate = iterate + relax_weight * (source - section_apply(iterate, shift)) / diagonal
        return iterate
    iterate = relax_weight * source / diagonal
    remainder = source - section_apply(iterate, shift)
    gathered, undo_list = assemble(
        jnp.stack([0.25 * coarsen(remainder), 0.125 * coarsen(shift)]), depth + 1, layout
    )
    coarse = section_cycle(gathered[0], gathered[1], depth + 1, layout)
    iterate = iterate + refine(unpick(coarse, undo_list))
    return iterate + relax_weight * (source - section_apply(iterate, shift)) / diagonal


def precondition(source, context):
    operator, fine_diagonal, shift_cells, row_totals, layout = context
    iterate = relax_weight * source / fine_diagonal
    remainder = source - fine_apply(iterate, operator)
    size_x, size_y, width = source.shape
    sums = remainder.reshape(size_x, size_y, width // P_SIZE, P_SIZE).sum(axis=3)
    gathered, undo_list = assemble(
        jnp.stack([coarsen(sums) / float(P_SIZE), 0.125 * coarsen(shift_cells)]), 1, layout
    )
    coarse = section_cycle(gathered[0], gathered[1], 1, layout)
    correction = refine(unpick(coarse, undo_list))
    iterate = iterate + jnp.repeat(correction, P_SIZE, axis=2)
    update = source - fine_apply(iterate, operator)
    return iterate + relax_weight * update / fine_diagonal


def total(terms):
    return lax.psum(terms, ("gx", "gy", "gz"))


def per_device(right_side, element_class, class_blocks, class_shift, face_weights):
    size_x, size_y, width = right_side.shape
    size_z = width // P_SIZE
    classes = class_blocks.shape[0]
    element_count = size_x * size_y * size_z
    onehot = (
        element_class.reshape(element_count, 1) == jnp.arange(classes, dtype=jnp.int32)[None, :]
    ).astype(jnp.float32)
    wide_blocks = jnp.transpose(class_blocks, (2, 0, 1)).reshape(P_SIZE, classes * P_SIZE)
    operator = (onehot, wide_blocks, face_weights)
    diag_table = jnp.diagonal(class_blocks, axis1=1, axis2=2)
    fine_diagonal = jnp.dot(onehot, diag_table, precision=highest).reshape(size_x, size_y, width)
    shift_cells = jnp.dot(onehot, class_shift[:, None], precision=highest).reshape(
        size_x, size_y, size_z
    )
    row_totals = None
    bits_z = lax.axis_size("gz").bit_length() - 1
    bits_y = lax.axis_size("gy").bit_length() - 1
    layout = (
        (0, lax.axis_size("gx"), bits_z + bits_y, lax.axis_index("gx")),
        (1, lax.axis_size("gy"), bits_z, lax.axis_index("gy")),
        (2, lax.axis_size("gz"), 0, lax.axis_index("gz")),
    )
    context = (operator, fine_diagonal, shift_cells, row_totals, layout)
    residual = right_side
    smoothed = precondition(residual, context)
    gamma_now = total((jnp.sum(residual * smoothed),))[0]
    direction = smoothed
    image = fine_apply(direction, operator)
    step_size = gamma_now / total((jnp.sum(direction * image),))[0]
    solution_field = step_size * direction
    residual = residual - step_size * image
    smoothed = precondition(residual, context)
    gamma_next = total((jnp.sum(residual * smoothed),))[0]
    direction = smoothed + gamma_next / gamma_now * direction
    image = fine_apply(direction, operator)
    step_size = gamma_next / total((jnp.sum(direction * image),))[0]
    solution_field = solution_field + step_size * direction
    residual = residual - step_size * image
    return (solution_field, residual)


AXES = (2, 4, 4)
DEVICES = 32
CELLS = 256
MESSAGE = 384
HALO_ROUNDS = 4
MESH = pl.DeviceIdType.MESH
f32 = jnp.float32


def iota(shape, dim):
    return lax.broadcasted_iota(jnp.int32, shape, dim)


def exact_dot(a, b):
    return jnp.dot(a, b, precision=highest, preferred_element_type=f32)


def neighbours(count, bits_y, bits_z, section_y, section_z):
    i, j = iota((count, count), 0), iota((count, count), 1)

    def split(k):
        return k >> bits_y + bits_z, k >> bits_z & (1 << bits_y) - 1, k & (1 << bits_z) - 1

    (xi, yi, zi), (xj, yj, zj) = split(i), split(j)
    apart = jnp.abs(xi - xj) + jnp.abs(yi - yj) + jnp.abs(zi - zj)
    same = ((yi >> section_y) == (yj >> section_y)) & ((zi >> section_z) == (zj >> section_z))
    return jnp.where((apart == 1) & same, 1.0, 0.0).astype(f32)


def coarse_matrix(shift_row):
    i, j = iota((CELLS, CELLS), 0), iota((CELLS, CELLS), 1)
    eye = jnp.where(i == j, 1.0, 0.0).astype(f32)
    beside_1 = neighbours(CELLS, 2, 4, 1, 3)
    beside_2 = neighbours(32, 1, 3, 1, 3)
    j2, cell = iota((32, CELLS), 0), iota((32, CELLS), 1)
    parent = (cell >> 7) * 16 + (cell >> 5 & 1) * 8 + (cell >> 1 & 7)
    down_1 = jnp.where(parent == j2, 1.0, 0.0).astype(f32)
    ci, cj = iota((CELLS, 32), 0), iota((CELLS, 32), 1)
    up_1 = jnp.where((ci >> 7) * 16 + (ci >> 5 & 1) * 8 + (ci >> 1 & 7) == cj, 1.0, 0.0).astype(f32)
    j3, k3 = iota((8, 32), 0), iota((8, 32), 1)
    down_2 = jnp.where((k3 >> 1 & 3) == j3, 1.0, 0.0).astype(f32)
    k2, i2 = iota((32, 8), 0), iota((32, 8), 1)
    up_2 = jnp.where((k2 >> 1 & 3) == i2, 1.0, 0.0).astype(f32)
    d1_row = 6.0 + shift_row
    d1 = jnp.sum(eye * d1_row, axis=1, keepdims=True)
    d2 = 6.0 + 0.125 * jnp.sum(down_1 * shift_row, axis=1, keepdims=True)
    j3w, cellw = iota((8, CELLS), 0), iota((8, CELLS), 1)
    d3 = 6.0 + 0.015625 * jnp.sum(
        jnp.where((cellw >> 2 & 3) == j3w, shift_row, 0.0), axis=1, keepdims=True
    )
    q2 = 0.25 * exact_dot(down_1, 0.4 * eye + 0.6 * beside_1 / d1_row)
    x2 = 0.6 * q2 / d2
    q3 = 0.25 * exact_dot(down_2, 0.4 * q2 + exact_dot(beside_2, x2))
    x3 = 0.6 * q3 / d3
    row = iota((8, CELLS), 0)
    for _ in range(SWEEPS - 1):
        after = jnp.where(row < 3, pltpu.roll(x3, 7, 0), 0.0)
        before = jnp.where((row > 0) & (row < 4), pltpu.roll(x3, 1, 0), 0.0)
        x3 = 0.4 * x3 + 0.6 * (q3 + after + before) / d3
    x2 = x2 + exact_dot(up_2, x3)
    x2 = 0.4 * x2 + 0.6 * (q2 + exact_dot(beside_2, x2)) / d2
    x1 = 0.6 * eye / d1 + exact_dot(up_1, x2)
    return 0.4 * x1 + 0.6 * (eye + exact_dot(beside_1, x1)) / d1


def pick_cells(gx, gy, gz):
    rows = []
    s, cell = iota((8, CELLS), 0), iota((8, CELLS), 1)
    x, y = s >> 1, s & 1
    cx, cy, cz = cell >> 6, cell >> 4 & 3, cell & 15
    for dx, dy, zs in ((0, 0, range(-1, 5)), (1, 0, range(4)), (-1, 0, range(4)), (0, 1, range(4)), (0, -1, range(4))):
        at_x = (gx * 4 + x + dx) >> 1
        at_y = (gy * 2 + y + dy) >> 1
        for z in zs:
            hit = (cx == at_x) & (cy == at_y) & (cz == gz * 4 + z)
            rows.append(jnp.where(hit, 1.0, 0.0).astype(f32))
    return jnp.concatenate(rows, axis=0)


def fused(
    r_ref, class_ref, blocks_ref, shift_ref, weight_ref, x_out, r_out,
    halo_out, halo_in, note_out, note_in, w_hi, w_lo, cells_ref,
    halo_send, halo_recv, note_send, note_recv,
):
    gx, gy, gz = lax.axis_index("gx"), lax.axis_index("gy"), lax.axis_index("gz")
    me = gx * 16 + gy * 4 + gz

    def others(act):
        def step(k, carry):
            to = lax.rem(me + k, DEVICES)
            act((to // 16, lax.rem(to // 4, 4), lax.rem(to, 4)))
            return carry

        lax.fori_loop(1, DEVICES, step, 0)

    barrier = pltpu.get_barrier_semaphore()
    halo_in[...] = jnp.zeros_like(halo_in)
    others(lambda to: pl.semaphore_signal(barrier, inc=1, device_id=to, device_id_type=MESH))

    lane = iota((8, 128), 1)
    sub = iota((8, 128), 0)
    low = lane < 64
    ni, nj, nk = lane >> 4 & 3, lane >> 2 & 3, lane & 3
    weights = [weight_ref[d] for d in range(3)]
    upper = [jnp.where(n == 3, w, 0.0) for n, w in zip((ni, nj, nk), weights)]
    lower = [jnp.where(n == 0, w, 0.0) for n, w in zip((ni, nj, nk), weights)]

    def widen(blocks):
        out = []
        for j in range(4):
            turned = pltpu.roll(blocks[j], 64, 1)
            out += [jnp.where(low, blocks[j], turned), jnp.where(low, turned, blocks[j])]
        return out

    def halves(u):
        return [jnp.where(low, u[2 * j], u[2 * j + 1]) for j in range(4)]

    flat = jnp.concatenate([r_ref[x] for x in range(4)], axis=0)
    right = widen([flat[:, 128 * j : 128 * j + 128] for j in range(4)])
    marks = jnp.concatenate([class_ref[x] for x in range(4)], axis=0)
    mark = [jnp.broadcast_to(marks[:, z : z + 1], (8, 128)) for z in range(8)]

    diagonal = [jnp.zeros((8, 128), f32) for _ in range(8)]
    totals = [jnp.zeros((8, 128), f32) for _ in range(8)]
    shifts = [jnp.zeros((8, 128), f32) for _ in range(8)]
    eye = iota((64, 128), 0) == (iota((64, 128), 1) & 63)
    for k in range(16):
        block = blocks_ref[k]
        block = jnp.concatenate([block, block], axis=1)
        diag_row = jnp.sum(jnp.where(eye, block, 0.0), axis=0, keepdims=True)
        total_row = jnp.sum(block, axis=0, keepdims=True)
        rest = jnp.where(eye, 0.0, block)
        rest_hi = rest.astype(jnp.bfloat16)
        w_hi[64 * k : 64 * k + 64, :] = rest_hi
        w_lo[64 * k : 64 * k + 64, :] = (rest - rest_hi.astype(f32)).astype(jnp.bfloat16)
        for z in range(8):
            here = mark[z] == k
            diagonal[z] = jnp.where(here, diag_row, diagonal[z])
            totals[z] = jnp.where(here, total_row, totals[z])
            shifts[z] = jnp.where(here, shift_ref[k], shifts[z])
    inverse = [1.0 / d for d in diagonal]

    wide_cell = iota((8, CELLS), 1)
    wide_sub = iota((8, CELLS), 0)
    own_cell = (gx * 2 + (wide_sub >> 2)) * 64 + gy * 16 + gz * 4

    def cell_row(columns, scale):
        row = jnp.zeros((8, CELLS), f32)
        for j in range(4):
            row = row + jnp.where(wide_cell == own_cell + j, columns[j], 0.0)
        return scale * jnp.sum(row, axis=0, keepdims=True)

    note_lane = iota((1, 128), 1)

    def dots(*pairs):
        row = jnp.zeros((1, 128), f32)
        for at, (a, b) in enumerate(pairs):
            acc = a[0] * b[0]
            for z in range(1, 8):
                acc = acc + a[z] * b[z]
            acc = jnp.sum(jnp.sum(acc, axis=0, keepdims=True), axis=1, keepdims=True)
            row = row + jnp.where(note_lane == at, 0.5 * acc, 0.0)
        return row

    def tell(at, message):
        note_out[at] = message
        note_in[at, me] = message
        others(
            lambda to: pltpu.make_async_remote_copy(
                src_ref=note_out.at[at], dst_ref=note_in.at[at, me],
                send_sem=note_send.at[at], recv_sem=note_recv.at[at],
                device_id=to, device_id_type=MESH,
            ).start()
        )

    def hear(at):
        span = note_in.at[at, pl.ds(0, DEVICES - 1)]
        pltpu.make_async_copy(span, span, note_recv.at[at]).wait()
        return jnp.sum(note_in[at], axis=0)

    def end_tell(at):
        span = note_in.at[at, pl.ds(0, DEVICES - 1)]
        pltpu.make_async_copy(span, span, note_send.at[at]).wait()

    routes = (
        (0, 1, gx < AXES[0] - 1, gx > 0, (gx + 1, gy, gz)),
        (1, 1, gx > 0, gx < AXES[0] - 1, (gx - 1, gy, gz)),
        (2, 2, gy < AXES[1] - 1, gy > 0, (gx, gy + 1, gz)),
        (4, 2, gy > 0, gy < AXES[1] - 1, (gx, gy - 1, gz)),
        (6, 1, gz < AXES[2] - 1, gz > 0, (gx, gy, gz + 1)),
        (7, 1, gz > 0, gz < AXES[2] - 1, (gx, gy, gz - 1)),
    )

    def halo_copy(at, way):
        tile, count, _, _, to = routes[way]
        return pltpu.make_async_remote_copy(
            src_ref=halo_out.at[at, pl.ds(tile, count)], dst_ref=halo_in.at[at, pl.ds(tile, count)],
            send_sem=halo_send.at[at, way], recv_sem=halo_recv.at[at, way],
            device_id=to, device_id_type=MESH,
        )

    odd = (sub & 1) == 1

    def send_halo(at, u):
        half = halves(u)
        up, down = half[3], half[0]
        up = jnp.where(sub >= 6, up, 0.0)
        down = jnp.where(sub < 2, down, 0.0)
        for m in range(3):
            up = jnp.where((sub >> 1) == m, pltpu.roll(half[m], (2 * m + 2) % 8, 0), up)
        for m in range(1, 4):
            down = jnp.where((sub >> 1) == m, pltpu.roll(half[m], 2 * m, 0), down)
        halo_out[at, 0] = up
        halo_out[at, 1] = down
        for j in range(2):
            halo_out[at, 2 + j] = jnp.where(odd, half[2 * j], pltpu.roll(half[2 * j + 1], 7, 0))
            halo_out[at, 4 + j] = jnp.where(odd, pltpu.roll(half[2 * j + 1], 1, 0), half[2 * j])
        halo_out[at, 6] = u[7]
        halo_out[at, 7] = u[0]
        for way in range(6):
            @pl.when(routes[way][2])
            def _():
                halo_copy(at, way).start()

    def wait_halo(at):
        for way in range(6):
            @pl.when(routes[way][3])
            def _():
                halo_copy(at, way).wait_recv()

    def end_halo(at):
        for way in range(6):
            @pl.when(routes[way][2])
            def _():
                halo_copy(at, way).wait_send()

    def turn(tile, by):
        return pltpu.roll(tile, by % 8, 0) if by % 8 else tile

    def unpack_x(packed, row):
        return widen([turn(packed, row - 2 * m) for m in range(4)])

    def local_part(u):
        top = jnp.concatenate(u, axis=0)
        top_hi = top.astype(jnp.bfloat16).astype(f32)
        top_lo = top - top_hi
        classes = jnp.concatenate(mark, axis=0)
        kind = classes - (iota((64, 128), 1) >> 6)
        his, los = [], []
        for p in range(8):
            here = kind == 2 * p
            his.append(jnp.where(here, top_hi, 0.0).astype(jnp.bfloat16))
            los.append(jnp.where(here, top_lo, 0.0).astype(jnp.bfloat16))
        hi, lo = jnp.concatenate(his, axis=1), jnp.concatenate(los, axis=1)
        out = jnp.dot(hi, w_hi[...], preferred_element_type=f32)
        out = out + jnp.dot(lo, w_hi[...], preferred_element_type=f32)
        out = out + jnp.dot(hi, w_lo[...], preferred_element_type=f32)
        return [out[8 * z : 8 * z + 8] + diagonal[z] * u[z] for z in range(8)]

    def couple(u, at):
        got = [halo_in[at, t] for t in range(8)]
        x_before, x_after = unpack_x(got[0], 0), unpack_x(got[1], 6)
        y_before = widen([pltpu.roll(got[2], 7, 0), got[2], pltpu.roll(got[3], 7, 0), got[3]])
        y_after = widen([pltpu.roll(got[4], 1, 0), got[4], pltpu.roll(got[5], 1, 0), got[5]])
        out = []
        for z in range(8):
            x_next = jnp.where(sub >= 6, x_after[z], pltpu.roll(u[z], 6, 0))
            x_last = jnp.where(sub < 2, x_before[z], pltpu.roll(u[z], 2, 0))
            y_next = jnp.where(odd, y_after[z], pltpu.roll(u[z], 7, 0))
            y_last = jnp.where(odd, pltpu.roll(u[z], 1, 0), y_before[z])
            z_next = u[z + 1] if z < 7 else got[7]
            z_last = u[z - 1] if z > 0 else got[6]
            acc = upper[0] * pltpu.roll(x_next, 48, 1) + lower[0] * pltpu.roll(x_last, 80, 1)
            acc = acc + upper[1] * pltpu.roll(y_next, 12, 1) + lower[1] * pltpu.roll(y_last, 116, 1)
            acc = acc + upper[2] * pltpu.roll(z_next, 3, 1) + lower[2] * pltpu.roll(z_last, 125, 1)
            out.append(acc)
        return out

    def apply(u, at):
        send_halo(at, u)
        own = local_part(u)
        wait_halo(at)
        return [a - b for a, b in zip(own, couple(u, at))]

    def tell_cells(at, left, extra):
        sums = [jnp.sum(left[2 * j] + left[2 * j + 1], axis=1, keepdims=True) for j in range(4)]
        tell(at, jnp.concatenate([cell_row(sums, 1.0 / 128.0), extra], axis=1))

    def correct(q, iterate, left):
        picked = jnp.sum(cells_ref[...] * q, axis=1, keepdims=True)
        tiles = [jnp.broadcast_to(picked[8 * t : 8 * t + 8], (8, 128)) for t in range(22)]
        own, x_up, x_down, y_up, y_down = tiles[:6], tiles[6:10], tiles[10:14], tiles[14:18], tiles[18:22]
        out = []
        for z in range(8):
            j = z // 2
            image = totals[z] * own[j + 1]
            image = image - upper[0] * x_up[j] - lower[0] * x_down[j]
            image = image - upper[1] * y_up[j] - lower[1] * y_down[j]
            image = image - upper[2] * own[(z + 1) // 2 + 1] - lower[2] * own[(z - 1) // 2 + 1]
            out.append(iterate[z] + own[j + 1] + 0.6 * (left[z] - image) * inverse[z])
        return out

    nothing = jnp.zeros((1, 128), f32)
    first = [0.6 * a * b for a, b in zip(right, inverse)]
    pl.semaphore_wait(barrier, DEVICES - 1)
    columns = [(shifts[2 * j] + shifts[2 * j + 1])[:, :1] for j in range(4)]
    tell(0, jnp.concatenate([cell_row(columns, 0.125), nothing], axis=1))
    left = [a - b for a, b in zip(right, apply(first, 0))]
    tell_cells(1, left, nothing)
    shift_row = hear(0)[:, :CELLS]
    cells_ref[...] = exact_dot(pick_cells(gx, gy, gz), coarse_matrix(shift_row))
    z0 = correct(hear(1)[:, :CELLS], first, left)
    w0 = apply(z0, 1)

    start = [0.6 * a * b for a, b in zip(w0, inverse)]
    left = [a - b for a, b in zip(w0, apply(start, 2))]
    tell_cells(2, left, dots((right, z0), (z0, w0)))
    heard = hear(2)
    gamma, curve = heard[:, 256:257], heard[:, 257:258]
    alpha = gamma / curve
    u = correct(heard[:, :CELLS], start, left)
    z1 = [a - alpha * b for a, b in zip(z0, u)]
    w1 = apply(z1, 3)
    r1 = [a - alpha * b for a, b in zip(right, w0)]
    tell(3, jnp.concatenate([jnp.zeros((1, CELLS), f32), dots((r1, z1), (z1, w1), (z1, w0), (z0, w1))], axis=1))
    heard = hear(3)
    gamma_2 = heard[:, 256:257]
    beta = gamma_2 / gamma
    curve_2 = heard[:, 257:258] + beta * (heard[:, 258:259] + heard[:, 259:260]) + beta * beta * curve
    alpha_2 = gamma_2 / curve_2
    field = [alpha * a + alpha_2 * (b + beta * a) for a, b in zip(z0, z1)]
    rest = [a - alpha_2 * (b + beta * c) for a, b, c in zip(r1, w1, w0)]
    for ref, tiles in ((x_out, field), (r_out, rest)):
        whole = jnp.concatenate(halves(tiles), axis=1)
        for x in range(4):
            ref[x] = whole[2 * x : 2 * x + 2, :]
    for at in range(HALO_ROUNDS):
        end_halo(at)
        end_tell(at)


def per_device_fused(right_side, element_class, class_blocks, class_shift, face_weights):
    vmem, smem = pl.BlockSpec(memory_space=pltpu.VMEM), pl.BlockSpec(memory_space=pltpu.SMEM)
    shape = jax.ShapeDtypeStruct(right_side.shape, f32)
    return pl.pallas_call(
        fused,
        out_shape=(shape, shape),
        in_specs=[vmem, vmem, vmem, smem, smem],
        out_specs=(vmem, vmem),
        scratch_shapes=[
            pltpu.VMEM((HALO_ROUNDS, 8, 8, 128), f32),
            pltpu.VMEM((HALO_ROUNDS, 8, 8, 128), f32),
            pltpu.VMEM((HALO_ROUNDS, 1, MESSAGE), f32),
            pltpu.VMEM((HALO_ROUNDS, DEVICES, 1, MESSAGE), f32),
            pltpu.VMEM((1024, 128), jnp.bfloat16),
            pltpu.VMEM((1024, 128), jnp.bfloat16),
            pltpu.VMEM((176, CELLS), f32),
            pltpu.SemaphoreType.DMA((HALO_ROUNDS, 6)),
            pltpu.SemaphoreType.DMA((HALO_ROUNDS, 6)),
            pltpu.SemaphoreType.DMA((HALO_ROUNDS,)),
            pltpu.SemaphoreType.DMA((HALO_ROUNDS,)),
        ],
        compiler_params=pltpu.CompilerParams(
            collective_id=0, has_side_effects=True, vmem_limit_bytes=32 * 1024 * 1024
        ),
    )(right_side, element_class, class_blocks, class_shift, face_weights)


def solution(mesh):
    in_specs = (P("gx", "gy", "gz"), P("gx", "gy", "gz"), P(), P(), P())
    out_specs = (P("gx", "gy", "gz"), P("gx", "gy", "gz"))
    small = tuple(mesh.shape[axis] for axis in ("gx", "gy", "gz")) == AXES
    body = per_device_fused if small else per_device
    return jax.shard_map(
        body, mesh=mesh, in_specs=in_specs, out_specs=out_specs, check_vma=False
    )
```

```python
import jax
import jax.numpy as jnp
import numpy as np
from jax import lax
from jax.experimental import pallas as pl
from jax.experimental.pallas import tpu as pltpu
from jax.sharding import PartitionSpec as P

P_SIZE = 64
SWEEPS = 4


highest = lax.Precision.HIGHEST
relax_weight = 0.6


def with_halo(x, sides, width):
    for axis, dim in sides:
        size, length = (lax.axis_size(axis), x.shape[dim])
        up = [(i, (i + 1) % size) for i in range(size - 1)]
        down = [(j, i) for i, j in up]
        last = lax.slice_in_dim(x, length - width, length, axis=dim)
        first = lax.slice_in_dim(x, 0, width, axis=dim)
        before = lax.ppermute(last, axis, up)
        after = lax.ppermute(first, axis, down)
        x = jnp.concatenate([before, x, after], axis=dim)
    return x


def partner_2(x, axis, bit):
    return lax.ppermute(x, axis, [(i, i ^ 1 << bit) for i in range(lax.axis_size(axis))])


def face_tables():
    node_ids = np.arange(P_SIZE)
    digits = (node_ids // 16, node_ids // 4 % 4, node_ids % 4)
    strides = (48, 12, 3)
    lower_sets = [node_ids[digits[axis_dim] == 0] for axis_dim in range(3)]
    return (lower_sets, strides)


def full_matrix(face_weights):
    lower_sets, strides = face_tables()
    pieces = []
    for axis_dim in range(3):
        lower_ids = lower_sets[axis_dim]
        upper_ids = lower_ids + strides[axis_dim]
        from_next = np.zeros((P_SIZE, P_SIZE), np.float32)
        from_next[lower_ids, upper_ids] = 1.0
        from_prev = np.zeros((P_SIZE, P_SIZE), np.float32)
        from_prev[upper_ids, lower_ids] = 1.0
        pieces.append(face_weights[axis_dim] * jnp.asarray(from_next))
        pieces.append(face_weights[axis_dim] * jnp.asarray(from_prev))
    return jnp.concatenate(pieces, axis=0)


def couple_full(cubes, face_weights):
    count = cubes.shape[0] * cubes.shape[1] * cubes.shape[2]
    padded = with_halo(cubes, (("gx", 0), ("gy", 1), ("gz", 2)), 1)
    views = [
        padded[2:, 1:-1, 1:-1],
        padded[:-2, 1:-1, 1:-1],
        padded[1:-1, 2:, 1:-1],
        padded[1:-1, :-2, 1:-1],
        padded[1:-1, 1:-1, 2:],
        padded[1:-1, 1:-1, :-2],
    ]
    stacked = jnp.concatenate(views, axis=3).reshape(count, 6 * P_SIZE)
    return jnp.dot(stacked, full_matrix(face_weights), precision=highest)


def coarsen(values):
    size_x, size_y, size_z = values.shape
    return values.reshape(size_x // 2, 2, size_y // 2, 2, size_z // 2, 2).sum(axis=(1, 3, 5))


def refine(values):
    return jnp.repeat(jnp.repeat(jnp.repeat(values, 2, axis=0), 2, axis=1), 2, axis=2)


def section_apply(values, shift):
    padded = jnp.pad(values, ((1, 1), (1, 1), (1, 1)))
    beside = padded[2:, 1:-1, 1:-1] + padded[:-2, 1:-1, 1:-1]
    beside = beside + padded[1:-1, 2:, 1:-1] + padded[1:-1, :-2, 1:-1]
    beside = beside + padded[1:-1, 1:-1, 2:] + padded[1:-1, 1:-1, :-2]
    return (6.0 + shift) * values - beside


def assemble(stacked, depth, layout):
    undo_list = []
    for axis_dim, axis_count, bit_offset, my_index in layout:
        if axis_count >= 2**depth:
            partner = partner_2(stacked, ("gx", "gy", "gz"), bit_offset + depth - 1)
            upper_half = my_index >> depth - 1 & 1 == 1
            half_size = stacked.shape[axis_dim + 1]
            low_first = jnp.concatenate([stacked, partner], axis_dim + 1)
            high_first = jnp.concatenate([partner, stacked], axis_dim + 1)
            stacked = jnp.where(upper_half, high_first, low_first)
            undo_list.append((axis_dim, upper_half, half_size))
    return (stacked, undo_list)


def unpick(values, undo_list):
    for axis_dim, upper_half, half_size in reversed(undo_list):
        values = lax.dynamic_slice_in_dim(
            values, upper_half.astype(jnp.int32) * half_size, half_size, axis_dim
        )
    return values


def fine_apply(field, operator):
    onehot, wide_blocks, face_weights = operator
    size_x, size_y, width = field.shape
    size_z = width // P_SIZE
    count = size_x * size_y * size_z
    classes = onehot.shape[1]
    flat = field.reshape(count, P_SIZE)
    products = jnp.dot(flat, wide_blocks, precision=highest).reshape(count, classes, P_SIZE)
    local_part = jnp.einsum("ekn,ek->en", products, onehot, precision=highest)
    cubes = field.reshape(size_x, size_y, size_z, P_SIZE)
    nearby = couple_full(cubes, face_weights)
    return (local_part - nearby).reshape(size_x, size_y, width)


def section_cycle(source, shift, depth, layout):
    diagonal = 6.0 + shift
    if depth == 3:
        iterate = jnp.zeros_like(source)
        for sweep_index in range(SWEEPS):
            iterate = iterate + relax_weight * (source - section_apply(iterate, shift)) / diagonal
        return iterate
    iterate = relax_weight * source / diagonal
    remainder = source - section_apply(iterate, shift)
    gathered, undo_list = assemble(
        jnp.stack([0.25 * coarsen(remainder), 0.125 * coarsen(shift)]), depth + 1, layout
    )
    coarse = section_cycle(gathered[0], gathered[1], depth + 1, layout)
    iterate = iterate + refine(unpick(coarse, undo_list))
    return iterate + relax_weight * (source - section_apply(iterate, shift)) / diagonal


def precondition(source, context):
    operator, fine_diagonal, shift_cells, row_totals, layout = context
    iterate = relax_weight * source / fine_diagonal
    remainder = source - fine_apply(iterate, operator)
    size_x, size_y, width = source.shape
    sums = remainder.reshape(size_x, size_y, width // P_SIZE, P_SIZE).sum(axis=3)
    gathered, undo_list = assemble(
        jnp.stack([coarsen(sums) / float(P_SIZE), 0.125 * coarsen(shift_cells)]), 1, layout
    )
    coarse = section_cycle(gathered[0], gathered[1], 1, layout)
    correction = refine(unpick(coarse, undo_list))
    iterate = iterate + jnp.repeat(correction, P_SIZE, axis=2)
    update = source - fine_apply(iterate, operator)
    return iterate + relax_weight * update / fine_diagonal


def total(terms):
    return lax.psum(terms, ("gx", "gy", "gz"))


def per_device(right_side, element_class, class_blocks, class_shift, face_weights):
    size_x, size_y, width = right_side.shape
    size_z = width // P_SIZE
    classes = class_blocks.shape[0]
    element_count = size_x * size_y * size_z
    onehot = (
        element_class.reshape(element_count, 1) == jnp.arange(classes, dtype=jnp.int32)[None, :]
    ).astype(jnp.float32)
    wide_blocks = jnp.transpose(class_blocks, (2, 0, 1)).reshape(P_SIZE, classes * P_SIZE)
    operator = (onehot, wide_blocks, face_weights)
    diag_table = jnp.diagonal(class_blocks, axis1=1, axis2=2)
    fine_diagonal = jnp.dot(onehot, diag_table, precision=highest).reshape(size_x, size_y, width)
    shift_cells = jnp.dot(onehot, class_shift[:, None], precision=highest).reshape(
        size_x, size_y, size_z
    )
    row_totals = None
    bits_z = lax.axis_size("gz").bit_length() - 1
    bits_y = lax.axis_size("gy").bit_length() - 1
    layout = (
        (0, lax.axis_size("gx"), bits_z + bits_y, lax.axis_index("gx")),
        (1, lax.axis_size("gy"), bits_z, lax.axis_index("gy")),
        (2, lax.axis_size("gz"), 0, lax.axis_index("gz")),
    )
    context = (operator, fine_diagonal, shift_cells, row_totals, layout)
    residual = right_side
    smoothed = precondition(residual, context)
    gamma_now = total((jnp.sum(residual * smoothed),))[0]
    direction = smoothed
    image = fine_apply(direction, operator)
    step_size = gamma_now / total((jnp.sum(direction * image),))[0]
    solution_field = step_size * direction
    residual = residual - step_size * image
    smoothed = precondition(residual, context)
    gamma_next = total((jnp.sum(residual * smoothed),))[0]
    direction = smoothed + gamma_next / gamma_now * direction
    image = fine_apply(direction, operator)
    step_size = gamma_next / total((jnp.sum(direction * image),))[0]
    solution_field = solution_field + step_size * direction
    residual = residual - step_size * image
    return (solution_field, residual)


AXES = (2, 4, 4)
DEVICES = 32
CELLS = 256
MESSAGE = 384
HALO_ROUNDS = 4
MESH = pl.DeviceIdType.MESH
f32 = jnp.float32


def iota(shape, dim):
    return lax.broadcasted_iota(jnp.int32, shape, dim)


def exact_dot(a, b):
    a = a.astype(jnp.bfloat16)
    total_dot = None
    for _ in range(3):
        part = b.astype(jnp.bfloat16)
        b = b - part.astype(f32)
        term = jnp.dot(a, part, preferred_element_type=f32)
        total_dot = term if total_dot is None else total_dot + term
    return total_dot


def neighbours(count, bits_y, bits_z, section_y, section_z):
    i, j = iota((count, count), 0), iota((count, count), 1)

    def split(k):
        return k >> bits_y + bits_z, k >> bits_z & (1 << bits_y) - 1, k & (1 << bits_z) - 1

    (xi, yi, zi), (xj, yj, zj) = split(i), split(j)
    apart = jnp.abs(xi - xj) + jnp.abs(yi - yj) + jnp.abs(zi - zj)
    same = ((yi >> section_y) == (yj >> section_y)) & ((zi >> section_z) == (zj >> section_z))
    return jnp.where((apart == 1) & same, 1.0, 0.0).astype(f32)


def coarse_matrix(shift_row):
    i, j = iota((CELLS, CELLS), 0), iota((CELLS, CELLS), 1)
    eye = jnp.where(i == j, 1.0, 0.0).astype(f32)
    beside_1 = neighbours(CELLS, 2, 4, 1, 3)
    beside_2 = neighbours(32, 1, 3, 1, 3)
    j2, cell = iota((32, CELLS), 0), iota((32, CELLS), 1)
    parent = (cell >> 7) * 16 + (cell >> 5 & 1) * 8 + (cell >> 1 & 7)
    down_1 = jnp.where(parent == j2, 1.0, 0.0).astype(f32)
    ci, cj = iota((CELLS, 32), 0), iota((CELLS, 32), 1)
    up_1 = jnp.where((ci >> 7) * 16 + (ci >> 5 & 1) * 8 + (ci >> 1 & 7) == cj, 1.0, 0.0).astype(f32)
    j3, k3 = iota((8, 32), 0), iota((8, 32), 1)
    down_2 = jnp.where((k3 >> 1 & 3) == j3, 1.0, 0.0).astype(f32)
    k2, i2 = iota((32, 8), 0), iota((32, 8), 1)
    up_2 = jnp.where((k2 >> 1 & 3) == i2, 1.0, 0.0).astype(f32)
    d1_row = 6.0 + shift_row
    d1 = jnp.sum(eye * d1_row, axis=1, keepdims=True)
    d2 = 6.0 + 0.125 * jnp.sum(down_1 * shift_row, axis=1, keepdims=True)
    j3w, cellw = iota((8, CELLS), 0), iota((8, CELLS), 1)
    d3 = 6.0 + 0.015625 * jnp.sum(
        jnp.where((cellw >> 2 & 3) == j3w, shift_row, 0.0), axis=1, keepdims=True
    )
    q2 = 0.25 * exact_dot(down_1, 0.4 * eye + 0.6 * beside_1 / d1_row)
    x2 = 0.6 * q2 / d2
    q3 = 0.25 * exact_dot(down_2, 0.4 * q2 + exact_dot(beside_2, x2))
    x3 = 0.6 * q3 / d3
    row = iota((8, CELLS), 0)
    for _ in range(SWEEPS - 1):
        after = jnp.where(row < 3, pltpu.roll(x3, 7, 0), 0.0)
        before = jnp.where((row > 0) & (row < 4), pltpu.roll(x3, 1, 0), 0.0)
        x3 = 0.4 * x3 + 0.6 * (q3 + after + before) / d3
    x2 = x2 + exact_dot(up_2, x3)
    x2 = 0.4 * x2 + 0.6 * (q2 + exact_dot(beside_2, x2)) / d2
    x1 = 0.6 * eye / d1 + exact_dot(up_1, x2)
    return 0.4 * x1 + 0.6 * (eye + exact_dot(beside_1, x1)) / d1


def pick_cells(gx, gy, gz):
    rows = []
    s, cell = iota((8, CELLS), 0), iota((8, CELLS), 1)
    cx, cy, cz = cell >> 6, cell >> 4 & 3, cell & 15

    def pick(x, y, z):
        hit = (cx == ((gx * 4 + x) >> 1)) & (cy == ((gy * 2 + y) >> 1)) & (cz == gz * 4 + z)
        rows.append(jnp.where(hit, 1.0, 0.0).astype(f32))

    x, y = s >> 1, s & 1
    for dx, dy, zs in ((0, 0, range(-1, 5)), (1, 0, range(4)), (-1, 0, range(4)), (0, 1, range(4)), (0, -1, range(4))):
        for z in zs:
            pick(x + dx, y + dy, z)
    pairs = ((-1, y, s >> 1), (4, y, s >> 1))
    pairs += ((x, -1, 1 - y), (x, -1, 3 - y), (x, 2, y), (x, 2, y + 2), (x, y, -1), (x, y, 4))
    for gone_x, gone_y, gone_z in pairs:
        pick(gone_x, gone_y, gone_z)
        for dx, dy, dz in ((1, 0, 0), (-1, 0, 0), (0, 1, 0), (0, -1, 0), (0, 0, 1), (0, 0, -1)):
            pick(gone_x + dx, gone_y + dy, gone_z + dz)
    return jnp.concatenate(rows, axis=0)


def fused(
    r_hbm, class_hbm, blocks_hbm, shift_hbm, weight_hbm, x_out, r_out,
    r_ref, class_ref, blocks_ref, shift_ref, weight_ref,
    halo_out, halo_in, note_out, note_in, w_hi, w_lo, cells_ref,
    load_sem, halo_send, halo_recv, note_send, note_recv,
):
    loads = (
        (blocks_hbm, blocks_ref), (r_hbm, r_ref), (class_hbm, class_ref),
        (shift_hbm, shift_ref), (weight_hbm, weight_ref),
    )
    loads = [pltpu.make_async_copy(a, b, load_sem.at[i]) for i, (a, b) in enumerate(loads)]
    for load in loads:
        load.start()
    gx, gy, gz = lax.axis_index("gx"), lax.axis_index("gy"), lax.axis_index("gz")
    me = gx * 16 + gy * 4 + gz

    def others(act):
        def step(k, carry):
            to = lax.rem(me + k, DEVICES)
            act((to // 16, lax.rem(to // 4, 4), lax.rem(to, 4)))
            return carry

        lax.fori_loop(1, DEVICES, step, 0)

    barrier = pltpu.get_barrier_semaphore()
    halo_in[...] = jnp.zeros_like(halo_in)
    others(lambda to: pl.semaphore_signal(barrier, inc=1, device_id=to, device_id_type=MESH))

    for load in loads:
        load.wait()

    lane = iota((8, 128), 1)
    sub = iota((8, 128), 0)
    low = lane < 64
    ni, nj, nk = lane >> 4 & 3, lane >> 2 & 3, lane & 3
    weights = [weight_ref[d] for d in range(3)]
    upper = [jnp.where(n == 3, w, 0.0) for n, w in zip((ni, nj, nk), weights)]
    lower = [jnp.where(n == 0, w, 0.0) for n, w in zip((ni, nj, nk), weights)]

    def widen(blocks):
        out = []
        for j in range(4):
            turned = pltpu.roll(blocks[j], 64, 1)
            out += [jnp.where(low, blocks[j], turned), jnp.where(low, turned, blocks[j])]
        return out

    def halves(u):
        return [jnp.where(low, u[2 * j], u[2 * j + 1]) for j in range(4)]

    flat = jnp.concatenate([r_ref[x] for x in range(4)], axis=0)
    right = widen([flat[:, 128 * j : 128 * j + 128] for j in range(4)])
    marks = jnp.concatenate([class_ref[x] for x in range(4)], axis=0)
    mark = [jnp.broadcast_to(marks[:, z : z + 1], (8, 128)) for z in range(8)]

    diagonal = [jnp.zeros((8, 128), f32) for _ in range(8)]
    totals = [jnp.zeros((8, 128), f32) for _ in range(8)]
    shifts = [jnp.zeros((8, 128), f32) for _ in range(8)]
    eye = iota((64, 128), 0) == (iota((64, 128), 1) & 63)
    for k in range(16):
        block = blocks_ref[k]
        block = jnp.concatenate([block, block], axis=1)
        diag_row = jnp.sum(jnp.where(eye, block, 0.0), axis=0, keepdims=True)
        total_row = jnp.sum(block, axis=0, keepdims=True)
        rest = jnp.where(eye, 0.0, block)
        rest_hi = rest.astype(jnp.bfloat16)
        w_hi[64 * k : 64 * k + 64, :] = rest_hi
        w_lo[64 * k : 64 * k + 64, :] = (rest - rest_hi.astype(f32)).astype(jnp.bfloat16)
        for z in range(8):
            here = mark[z] == k
            diagonal[z] = jnp.where(here, diag_row, diagonal[z])
            totals[z] = jnp.where(here, total_row, totals[z])
            shifts[z] = jnp.where(here, shift_ref[k], shifts[z])
    inverse = [1.0 / d for d in diagonal]

    wide_cell = iota((8, CELLS), 1)
    wide_sub = iota((8, CELLS), 0)
    own_cell = (gx * 2 + (wide_sub >> 2)) * 64 + gy * 16 + gz * 4

    def cell_row(columns, scale):
        row = jnp.zeros((8, CELLS), f32)
        for j in range(4):
            row = row + jnp.where(wide_cell == own_cell + j, columns[j], 0.0)
        return scale * jnp.sum(row, axis=0, keepdims=True)

    note_lane = iota((1, 128), 1)

    def dots(*pairs):
        row = jnp.zeros((1, 128), f32)
        for at, (a, b) in enumerate(pairs):
            acc = a[0] * b[0]
            for z in range(1, 8):
                acc = acc + a[z] * b[z]
            acc = jnp.sum(jnp.sum(acc, axis=0, keepdims=True), axis=1, keepdims=True)
            row = row + jnp.where(note_lane == at, 0.5 * acc, 0.0)
        return row

    def tell(at, message):
        note_out[at] = message
        note_in[at, me] = message
        others(
            lambda to: pltpu.make_async_remote_copy(
                src_ref=note_out.at[at], dst_ref=note_in.at[at, me],
                send_sem=note_send.at[at], recv_sem=note_recv.at[at],
                device_id=to, device_id_type=MESH,
            ).start()
        )

    def hear(at):
        span = note_in.at[at, pl.ds(0, DEVICES - 1)]
        pltpu.make_async_copy(span, span, note_recv.at[at]).wait()
        return jnp.sum(note_in[at], axis=0)

    def end_tell(at):
        span = note_in.at[at, pl.ds(0, DEVICES - 1)]
        pltpu.make_async_copy(span, span, note_send.at[at]).wait()

    routes = (
        (0, 1, gx < AXES[0] - 1, gx > 0, (gx + 1, gy, gz)),
        (1, 1, gx > 0, gx < AXES[0] - 1, (gx - 1, gy, gz)),
        (2, 2, gy < AXES[1] - 1, gy > 0, (gx, gy + 1, gz)),
        (4, 2, gy > 0, gy < AXES[1] - 1, (gx, gy - 1, gz)),
        (6, 1, gz < AXES[2] - 1, gz > 0, (gx, gy, gz + 1)),
        (7, 1, gz > 0, gz < AXES[2] - 1, (gx, gy, gz - 1)),
    )

    def halo_copy(at, way):
        tile, count, _, _, to = routes[way]
        span = pl.ds(3 * tile, 3 * count if at == 0 else count)
        return pltpu.make_async_remote_copy(
            src_ref=halo_out.at[at, span], dst_ref=halo_in.at[at, span],
            send_sem=halo_send.at[at, way], recv_sem=halo_recv.at[at, way],
            device_id=to, device_id_type=MESH,
        )

    odd = (sub & 1) == 1

    places = [(0, 1, 0), (1, 1, 0), (2, 2, 0), (2, 2, 1), (4, 2, 0), (4, 2, 1), (6, 1, 0), (7, 1, 0)]

    def send_halo(at, *fields):
        for f, u in enumerate(fields):
            half = halves(u)
            up = jnp.where(sub >= 6, half[3], 0.0)
            down = jnp.where(sub < 2, half[0], 0.0)
            for m in range(3):
                up = jnp.where((sub >> 1) == m, pltpu.roll(half[m], (2 * m + 2) % 8, 0), up)
            for m in range(1, 4):
                down = jnp.where((sub >> 1) == m, pltpu.roll(half[m], 2 * m, 0), down)
            tiles = [up, down]
            tiles += [jnp.where(odd, half[2 * j], pltpu.roll(half[2 * j + 1], 7, 0)) for j in range(2)]
            tiles += [jnp.where(odd, pltpu.roll(half[2 * j + 1], 1, 0), half[2 * j]) for j in range(2)]
            tiles += [u[7], u[0]]
            for (tile, count, j), value in zip(places, tiles):
                halo_out[at, 3 * tile + f * count + j] = value
        for way in range(6):
            @pl.when(routes[way][2])
            def _():
                halo_copy(at, way).start()

    def ghosts(at, f=0):
        return [halo_in[at, 3 * tile + f * count + j] for tile, count, j in places]

    def wait_halo(at):
        for way in range(6):
            @pl.when(routes[way][3])
            def _():
                halo_copy(at, way).wait_recv()

    def end_halo(at):
        for way in range(6):
            @pl.when(routes[way][2])
            def _():
                halo_copy(at, way).wait_send()

    def turn(tile, by):
        return pltpu.roll(tile, by % 8, 0) if by % 8 else tile

    def unpack_x(packed, row):
        return widen([turn(packed, row - 2 * m) for m in range(4)])

    def local_part(u):
        top = jnp.concatenate(u, axis=0)
        top_hi = top.astype(jnp.bfloat16).astype(f32)
        top_lo = top - top_hi
        classes = jnp.concatenate(mark, axis=0)
        kind = classes - (iota((64, 128), 1) >> 6)
        his, los = [], []
        for p in range(8):
            here = kind == 2 * p
            his.append(jnp.where(here, top_hi, 0.0).astype(jnp.bfloat16))
            los.append(jnp.where(here, top_lo, 0.0).astype(jnp.bfloat16))
        hi, lo = jnp.concatenate(his, axis=1), jnp.concatenate(los, axis=1)
        out = jnp.dot(hi, w_hi[...], preferred_element_type=f32)
        out = out + jnp.dot(lo, w_hi[...], preferred_element_type=f32)
        out = out + jnp.dot(hi, w_lo[...], preferred_element_type=f32)
        return [out[8 * z : 8 * z + 8] + diagonal[z] * u[z] for z in range(8)]

    def couple(u, got):
        x_before, x_after = unpack_x(got[0], 0), unpack_x(got[1], 6)
        y_before = widen([pltpu.roll(got[2], 7, 0), got[2], pltpu.roll(got[3], 7, 0), got[3]])
        y_after = widen([pltpu.roll(got[4], 1, 0), got[4], pltpu.roll(got[5], 1, 0), got[5]])
        out = []
        for z in range(8):
            x_next = jnp.where(sub >= 6, x_after[z], pltpu.roll(u[z], 6, 0))
            x_last = jnp.where(sub < 2, x_before[z], pltpu.roll(u[z], 2, 0))
            y_next = jnp.where(odd, y_after[z], pltpu.roll(u[z], 7, 0))
            y_last = jnp.where(odd, pltpu.roll(u[z], 1, 0), y_before[z])
            z_next = u[z + 1] if z < 7 else got[7]
            z_last = u[z - 1] if z > 0 else got[6]
            acc = upper[0] * pltpu.roll(x_next, 48, 1) + lower[0] * pltpu.roll(x_last, 80, 1)
            acc = acc + upper[1] * pltpu.roll(y_next, 12, 1) + lower[1] * pltpu.roll(y_last, 116, 1)
            acc = acc + upper[2] * pltpu.roll(z_next, 3, 1) + lower[2] * pltpu.roll(z_last, 125, 1)
            out.append(acc)
        return out

    def minus(a, b):
        return [p - q for p, q in zip(a, b)]

    def tell_cells(at, left, extra):
        sums = [jnp.sum(left[2 * j] + left[2 * j + 1], axis=1, keepdims=True) for j in range(4)]
        tell(at, jnp.concatenate([cell_row(sums, 1.0 / 128.0), extra], axis=1))

    def correct(q, source, iterate, left, at):
        picked = jnp.sum(cells_ref[...] * q, axis=1, keepdims=True)
        tiles = [jnp.broadcast_to(picked[8 * t : 8 * t + 8], (8, 128)) for t in range(78)]
        own, x_up, x_down, y_up, y_down = tiles[:6], tiles[6:10], tiles[10:14], tiles[14:18], tiles[18:22]
        rest, scaled = [], []
        for z in range(8):
            j = z // 2
            image = totals[z] * own[j + 1]
            image = image - upper[0] * x_up[j] - lower[0] * x_down[j]
            image = image - upper[1] * y_up[j] - lower[1] * y_down[j]
            image = image - upper[2] * own[(z + 1) // 2 + 1] - lower[2] * own[(z - 1) // 2 + 1]
            rest.append(left[z] - image)
            scaled.append(rest[z] * inverse[z])
        own_part = local_part(scaled)
        wait_halo(at)
        got = []
        for g, (sent, inv, tot) in enumerate(zip(ghosts(at), ghosts(0, 1), ghosts(0, 2))):
            mid, xu, xd, yu, yd, zu, zd = tiles[22 + 7 * g : 29 + 7 * g]
            if g < 6:
                zu, zd = jnp.where(low, mid, zu), jnp.where(low, zd, mid)
            pull = upper[0] * xu + lower[0] * xd + upper[1] * yu + lower[1] * yd
            pull = pull + upper[2] * zu + lower[2] * zd
            got.append(sent - tot * mid + inv * pull)
        near = couple(scaled, got)
        result = [iterate[z] + own[z // 2 + 1] + 0.6 * scaled[z] for z in range(8)]
        image = [source[z] - rest[z] + 0.6 * (own_part[z] - near[z]) for z in range(8)]
        return result, image

    def descend(source, at, *fields):
        iterate = [0.6 * a * b for a, b in zip(source, inverse)]
        send_halo(at, iterate, *fields)
        own_part = local_part(iterate)
        wait_halo(at)
        left = minus(source, minus(own_part, couple(iterate, ghosts(at))))
        send_halo(at + 1, [a * b for a, b in zip(left, inverse)])
        return iterate, left

    nothing = jnp.zeros((1, 128), f32)
    pl.semaphore_wait(barrier, DEVICES - 1)
    columns = [(shifts[2 * j] + shifts[2 * j + 1])[:, :1] for j in range(4)]
    tell(0, jnp.concatenate([cell_row(columns, 0.125), nothing], axis=1))
    ratio = [a * b for a, b in zip(totals, inverse)]
    first, left = descend(right, 0, inverse, ratio)
    tell_cells(1, left, nothing)
    shift_row = hear(0)[:, :CELLS]
    cells_ref[...] = exact_dot(pick_cells(gx, gy, gz), coarse_matrix(shift_row))
    z0, w0 = correct(hear(1)[:, :CELLS], right, first, left, 1)

    start, left = descend(w0, 2)
    tell_cells(2, left, dots((right, z0), (z0, w0)))
    heard = hear(2)
    gamma, curve = heard[:, 256:257], heard[:, 257:258]
    alpha = gamma / curve
    u, v = correct(heard[:, :CELLS], w0, start, left, 3)
    z1 = [a - alpha * b for a, b in zip(z0, u)]
    w1 = [a - alpha * b for a, b in zip(w0, v)]
    r1 = [a - alpha * b for a, b in zip(right, w0)]
    tell(3, jnp.concatenate([jnp.zeros((1, CELLS), f32), dots((r1, z1), (z1, w1), (z1, w0), (z0, w1))], axis=1))
    heard = hear(3)
    gamma_2 = heard[:, 256:257]
    beta = gamma_2 / gamma
    curve_2 = heard[:, 257:258] + beta * (heard[:, 258:259] + heard[:, 259:260]) + beta * beta * curve
    alpha_2 = gamma_2 / curve_2
    field = [alpha * a + alpha_2 * (b + beta * a) for a, b in zip(z0, z1)]
    rest = [a - alpha_2 * (b + beta * c) for a, b, c in zip(r1, w1, w0)]
    for ref, tiles in ((x_out, field), (r_out, rest)):
        whole = jnp.concatenate(halves(tiles), axis=1)
        for x in range(4):
            ref[x] = whole[2 * x : 2 * x + 2, :]
    for at in range(HALO_ROUNDS):
        end_halo(at)
        end_tell(at)


def per_device_fused(right_side, element_class, class_blocks, class_shift, face_weights):
    vmem, hbm = pl.BlockSpec(memory_space=pltpu.VMEM), pl.BlockSpec(memory_space=pltpu.HBM)
    shape = jax.ShapeDtypeStruct(right_side.shape, f32)
    return pl.pallas_call(
        fused,
        out_shape=(shape, shape),
        in_specs=[hbm] * 5,
        out_specs=(vmem, vmem),
        scratch_shapes=[
            pltpu.VMEM(right_side.shape, f32),
            pltpu.VMEM(element_class.shape, jnp.int32),
            pltpu.VMEM(class_blocks.shape, f32),
            pltpu.SMEM(class_shift.shape, f32),
            pltpu.SMEM(face_weights.shape, f32),
            pltpu.VMEM((HALO_ROUNDS, 24, 8, 128), f32),
            pltpu.VMEM((HALO_ROUNDS, 24, 8, 128), f32),
            pltpu.VMEM((HALO_ROUNDS, 1, MESSAGE), f32),
            pltpu.VMEM((HALO_ROUNDS, DEVICES, 1, MESSAGE), f32),
            pltpu.VMEM((1024, 128), jnp.bfloat16),
            pltpu.VMEM((1024, 128), jnp.bfloat16),
            pltpu.VMEM((624, CELLS), f32),
            pltpu.SemaphoreType.DMA((5,)),
            pltpu.SemaphoreType.DMA((HALO_ROUNDS, 6)),
            pltpu.SemaphoreType.DMA((HALO_ROUNDS, 6)),
            pltpu.SemaphoreType.DMA((HALO_ROUNDS,)),
            pltpu.SemaphoreType.DMA((HALO_ROUNDS,)),
        ],
        compiler_params=pltpu.CompilerParams(
            collective_id=0, has_side_effects=True, vmem_limit_bytes=32 * 1024 * 1024
        ),
    )(right_side, element_class, class_blocks, class_shift, face_weights)


def solution(mesh):
    in_specs = (P("gx", "gy", "gz"), P("gx", "gy", "gz"), P(), P(), P())
    out_specs = (P("gx", "gy", "gz"), P("gx", "gy", "gz"))
    small = tuple(mesh.shape[axis] for axis in ("gx", "gy", "gz")) == AXES
    body = per_device_fused if small else per_device
    return jax.shard_map(
        body, mesh=mesh, in_specs=in_specs, out_specs=out_specs, check_vma=False
    )
```

```python
import jax
import jax.numpy as jnp
import numpy as np
from jax import lax
from jax.experimental import pallas as pl
from jax.experimental.pallas import tpu as pltpu
from jax.sharding import PartitionSpec as P

P_SIZE = 64
SWEEPS = 4


highest = lax.Precision.HIGHEST
relax_weight = 0.6


def with_halo(x, sides, width):
    for axis, dim in sides:
        size, length = (lax.axis_size(axis), x.shape[dim])
        up = [(i, (i + 1) % size) for i in range(size - 1)]
        down = [(j, i) for i, j in up]
        last = lax.slice_in_dim(x, length - width, length, axis=dim)
        first = lax.slice_in_dim(x, 0, width, axis=dim)
        before = lax.ppermute(last, axis, up)
        after = lax.ppermute(first, axis, down)
        x = jnp.concatenate([before, x, after], axis=dim)
    return x


def partner_2(x, axis, bit):
    return lax.ppermute(x, axis, [(i, i ^ 1 << bit) for i in range(lax.axis_size(axis))])


def face_tables():
    node_ids = np.arange(P_SIZE)
    digits = (node_ids // 16, node_ids // 4 % 4, node_ids % 4)
    strides = (48, 12, 3)
    lower_sets = [node_ids[digits[axis_dim] == 0] for axis_dim in range(3)]
    return (lower_sets, strides)


def full_matrix(face_weights):
    lower_sets, strides = face_tables()
    pieces = []
    for axis_dim in range(3):
        lower_ids = lower_sets[axis_dim]
        upper_ids = lower_ids + strides[axis_dim]
        from_next = np.zeros((P_SIZE, P_SIZE), np.float32)
        from_next[lower_ids, upper_ids] = 1.0
        from_prev = np.zeros((P_SIZE, P_SIZE), np.float32)
        from_prev[upper_ids, lower_ids] = 1.0
        pieces.append(face_weights[axis_dim] * jnp.asarray(from_next))
        pieces.append(face_weights[axis_dim] * jnp.asarray(from_prev))
    return jnp.concatenate(pieces, axis=0)


def couple_full(cubes, face_weights):
    count = cubes.shape[0] * cubes.shape[1] * cubes.shape[2]
    padded = with_halo(cubes, (("gx", 0), ("gy", 1), ("gz", 2)), 1)
    views = [
        padded[2:, 1:-1, 1:-1],
        padded[:-2, 1:-1, 1:-1],
        padded[1:-1, 2:, 1:-1],
        padded[1:-1, :-2, 1:-1],
        padded[1:-1, 1:-1, 2:],
        padded[1:-1, 1:-1, :-2],
    ]
    stacked = jnp.concatenate(views, axis=3).reshape(count, 6 * P_SIZE)
    return jnp.dot(stacked, full_matrix(face_weights), precision=highest)


def coarsen(values):
    size_x, size_y, size_z = values.shape
    return values.reshape(size_x // 2, 2, size_y // 2, 2, size_z // 2, 2).sum(axis=(1, 3, 5))


def refine(values):
    return jnp.repeat(jnp.repeat(jnp.repeat(values, 2, axis=0), 2, axis=1), 2, axis=2)


def section_apply(values, shift):
    padded = jnp.pad(values, ((1, 1), (1, 1), (1, 1)))
    beside = padded[2:, 1:-1, 1:-1] + padded[:-2, 1:-1, 1:-1]
    beside = beside + padded[1:-1, 2:, 1:-1] + padded[1:-1, :-2, 1:-1]
    beside = beside + padded[1:-1, 1:-1, 2:] + padded[1:-1, 1:-1, :-2]
    return (6.0 + shift) * values - beside


def assemble(stacked, depth, layout):
    undo_list = []
    for axis_dim, axis_count, bit_offset, my_index in layout:
        if axis_count >= 2**depth:
            partner = partner_2(stacked, ("gx", "gy", "gz"), bit_offset + depth - 1)
            upper_half = my_index >> depth - 1 & 1 == 1
            half_size = stacked.shape[axis_dim + 1]
            low_first = jnp.concatenate([stacked, partner], axis_dim + 1)
            high_first = jnp.concatenate([partner, stacked], axis_dim + 1)
            stacked = jnp.where(upper_half, high_first, low_first)
            undo_list.append((axis_dim, upper_half, half_size))
    return (stacked, undo_list)


def unpick(values, undo_list):
    for axis_dim, upper_half, half_size in reversed(undo_list):
        values = lax.dynamic_slice_in_dim(
            values, upper_half.astype(jnp.int32) * half_size, half_size, axis_dim
        )
    return values


def fine_apply(field, operator):
    onehot, wide_blocks, face_weights = operator
    size_x, size_y, width = field.shape
    size_z = width // P_SIZE
    count = size_x * size_y * size_z
    classes = onehot.shape[1]
    flat = field.reshape(count, P_SIZE)
    products = jnp.dot(flat, wide_blocks, precision=highest).reshape(count, classes, P_SIZE)
    local_part = jnp.einsum("ekn,ek->en", products, onehot, precision=highest)
    cubes = field.reshape(size_x, size_y, size_z, P_SIZE)
    nearby = couple_full(cubes, face_weights)
    return (local_part - nearby).reshape(size_x, size_y, width)


def section_cycle(source, shift, depth, layout):
    diagonal = 6.0 + shift
    if depth == 3:
        iterate = jnp.zeros_like(source)
        for sweep_index in range(SWEEPS):
            iterate = iterate + relax_weight * (source - section_apply(iterate, shift)) / diagonal
        return iterate
    iterate = relax_weight * source / diagonal
    remainder = source - section_apply(iterate, shift)
    gathered, undo_list = assemble(
        jnp.stack([0.25 * coarsen(remainder), 0.125 * coarsen(shift)]), depth + 1, layout
    )
    coarse = section_cycle(gathered[0], gathered[1], depth + 1, layout)
    iterate = iterate + refine(unpick(coarse, undo_list))
    return iterate + relax_weight * (source - section_apply(iterate, shift)) / diagonal


def precondition(source, context):
    operator, fine_diagonal, shift_cells, row_totals, layout = context
    iterate = relax_weight * source / fine_diagonal
    remainder = source - fine_apply(iterate, operator)
    size_x, size_y, width = source.shape
    sums = remainder.reshape(size_x, size_y, width // P_SIZE, P_SIZE).sum(axis=3)
    gathered, undo_list = assemble(
        jnp.stack([coarsen(sums) / float(P_SIZE), 0.125 * coarsen(shift_cells)]), 1, layout
    )
    coarse = section_cycle(gathered[0], gathered[1], 1, layout)
    correction = refine(unpick(coarse, undo_list))
    iterate = iterate + jnp.repeat(correction, P_SIZE, axis=2)
    update = source - fine_apply(iterate, operator)
    return iterate + relax_weight * update / fine_diagonal


def total(terms):
    return lax.psum(terms, ("gx", "gy", "gz"))


def per_device(right_side, element_class, class_blocks, class_shift, face_weights):
    size_x, size_y, width = right_side.shape
    size_z = width // P_SIZE
    classes = class_blocks.shape[0]
    element_count = size_x * size_y * size_z
    onehot = (
        element_class.reshape(element_count, 1) == jnp.arange(classes, dtype=jnp.int32)[None, :]
    ).astype(jnp.float32)
    wide_blocks = jnp.transpose(class_blocks, (2, 0, 1)).reshape(P_SIZE, classes * P_SIZE)
    operator = (onehot, wide_blocks, face_weights)
    diag_table = jnp.diagonal(class_blocks, axis1=1, axis2=2)
    fine_diagonal = jnp.dot(onehot, diag_table, precision=highest).reshape(size_x, size_y, width)
    shift_cells = jnp.dot(onehot, class_shift[:, None], precision=highest).reshape(
        size_x, size_y, size_z
    )
    row_totals = None
    bits_z = lax.axis_size("gz").bit_length() - 1
    bits_y = lax.axis_size("gy").bit_length() - 1
    layout = (
        (0, lax.axis_size("gx"), bits_z + bits_y, lax.axis_index("gx")),
        (1, lax.axis_size("gy"), bits_z, lax.axis_index("gy")),
        (2, lax.axis_size("gz"), 0, lax.axis_index("gz")),
    )
    context = (operator, fine_diagonal, shift_cells, row_totals, layout)
    residual = right_side
    smoothed = precondition(residual, context)
    gamma_now = total((jnp.sum(residual * smoothed),))[0]
    direction = smoothed
    image = fine_apply(direction, operator)
    step_size = gamma_now / total((jnp.sum(direction * image),))[0]
    solution_field = step_size * direction
    residual = residual - step_size * image
    smoothed = precondition(residual, context)
    gamma_next = total((jnp.sum(residual * smoothed),))[0]
    direction = smoothed + gamma_next / gamma_now * direction
    image = fine_apply(direction, operator)
    step_size = gamma_next / total((jnp.sum(direction * image),))[0]
    solution_field = solution_field + step_size * direction
    residual = residual - step_size * image
    return (solution_field, residual)


AXES = (2, 4, 4)
CELLS = 256
MESSAGE = 384
HALO_ROUNDS = 4
MESH = pl.DeviceIdType.MESH
f32 = jnp.float32


def iota(shape, dim):
    return lax.broadcasted_iota(jnp.int32, shape, dim)


def exact_dot(a, b):
    a = a.astype(jnp.bfloat16)
    total_dot = None
    for _ in range(3):
        part = b.astype(jnp.bfloat16)
        b = b - part.astype(f32)
        term = jnp.dot(a, part, preferred_element_type=f32)
        total_dot = term if total_dot is None else total_dot + term
    return total_dot


def neighbours(count, bits_y, bits_z, section_y, section_z):
    i, j = iota((count, count), 0), iota((count, count), 1)

    def split(k):
        return k >> bits_y + bits_z, k >> bits_z & (1 << bits_y) - 1, k & (1 << bits_z) - 1

    (xi, yi, zi), (xj, yj, zj) = split(i), split(j)
    apart = jnp.abs(xi - xj) + jnp.abs(yi - yj) + jnp.abs(zi - zj)
    same = ((yi >> section_y) == (yj >> section_y)) & ((zi >> section_z) == (zj >> section_z))
    return jnp.where((apart == 1) & same, 1.0, 0.0).astype(f32)


def coarse_matrix(shift_row, beside_1):
    i, j = iota((CELLS, CELLS), 0), iota((CELLS, CELLS), 1)
    eye = jnp.where(i == j, 1.0, 0.0).astype(f32)
    beside_2 = neighbours(32, 1, 3, 1, 3)
    j2, cell = iota((32, CELLS), 0), iota((32, CELLS), 1)
    parent = (cell >> 7) * 16 + (cell >> 5 & 1) * 8 + (cell >> 1 & 7)
    down_1 = jnp.where(parent == j2, 1.0, 0.0).astype(f32)
    ci, cj = iota((CELLS, 32), 0), iota((CELLS, 32), 1)
    up_1 = jnp.where((ci >> 7) * 16 + (ci >> 5 & 1) * 8 + (ci >> 1 & 7) == cj, 1.0, 0.0).astype(f32)
    j3, k3 = iota((8, 32), 0), iota((8, 32), 1)
    down_2 = jnp.where((k3 >> 1 & 3) == j3, 1.0, 0.0).astype(f32)
    k2, i2 = iota((32, 8), 0), iota((32, 8), 1)
    up_2 = jnp.where((k2 >> 1 & 3) == i2, 1.0, 0.0).astype(f32)
    d1_row = 6.0 + shift_row
    d1 = jnp.sum(eye * d1_row, axis=1, keepdims=True)
    d2 = 6.0 + 0.125 * jnp.sum(down_1 * shift_row, axis=1, keepdims=True)
    j3w, cellw = iota((8, CELLS), 0), iota((8, CELLS), 1)
    d3 = 6.0 + 0.015625 * jnp.sum(
        jnp.where((cellw >> 2 & 3) == j3w, shift_row, 0.0), axis=1, keepdims=True
    )
    q2 = 0.25 * exact_dot(down_1, 0.4 * eye + 0.6 * beside_1.astype(f32) / d1_row)
    x2 = 0.6 * q2 / d2
    q3 = 0.25 * exact_dot(down_2, 0.4 * q2 + exact_dot(beside_2, x2))
    x3 = 0.6 * q3 / d3
    row = iota((8, CELLS), 0)
    for _ in range(SWEEPS - 1):
        after = jnp.where(row < 3, pltpu.roll(x3, 7, 0), 0.0)
        before = jnp.where((row > 0) & (row < 4), pltpu.roll(x3, 1, 0), 0.0)
        x3 = 0.4 * x3 + 0.6 * (q3 + after + before) / d3
    x2 = x2 + exact_dot(up_2, x3)
    x2 = 0.4 * x2 + 0.6 * (q2 + exact_dot(beside_2, x2)) / d2
    x1 = 0.6 * eye / d1 + exact_dot(up_1, x2)
    return 0.4 * x1 + 0.6 * (eye + exact_dot(beside_1, x1)) / d1


def pick_cells(gx, gy, gz):
    rows = []
    s, cell = iota((8, CELLS), 0), iota((8, CELLS), 1)
    cx, cy, cz = cell >> 6, cell >> 4 & 3, cell & 15

    def pick(x, y, z):
        hit = (cx == ((gx * 4 + x) >> 1)) & (cy == ((gy * 2 + y) >> 1)) & (cz == gz * 4 + z)
        rows.append(jnp.where(hit, 1.0, 0.0).astype(f32))

    x, y = s >> 1, s & 1
    for dx, dy, zs in ((0, 0, range(-1, 5)), (1, 0, range(4)), (-1, 0, range(4)), (0, 1, range(4)), (0, -1, range(4))):
        for z in zs:
            pick(x + dx, y + dy, z)
    pairs = ((-1, y, s >> 1), (4, y, s >> 1))
    pairs += ((x, -1, 1 - y), (x, -1, 3 - y), (x, 2, y), (x, 2, y + 2), (x, y, -1), (x, y, 4))
    for gone_x, gone_y, gone_z in pairs:
        pick(gone_x, gone_y, gone_z)
        for dx, dy, dz in ((1, 0, 0), (-1, 0, 0), (0, 1, 0), (0, -1, 0), (0, 0, 1), (0, 0, -1)):
            pick(gone_x + dx, gone_y + dy, gone_z + dz)
    return jnp.concatenate(rows, axis=0)


def fused(
    r_hbm, class_hbm, blocks_hbm, shift_hbm, weight_hbm, x_out, r_out,
    r_ref, class_ref, blocks_ref, shift_ref, weight_ref,
    halo_out, halo_in, note_out, note_in, w_hi, w_lo, cells_ref, pick_ref, beside_ref,
    load_sem, halo_send, halo_recv, note_send, note_recv,
):
    loads = (
        (blocks_hbm, blocks_ref), (r_hbm, r_ref), (class_hbm, class_ref),
        (shift_hbm, shift_ref), (weight_hbm, weight_ref),
    )
    loads = [pltpu.make_async_copy(a, b, load_sem.at[i]) for i, (a, b) in enumerate(loads)]
    for load in loads:
        load.start()
    gx, gy, gz = lax.axis_index("gx"), lax.axis_index("gy"), lax.axis_index("gz")

    plane = gx * 4 + gy
    along = [(gx, gy, lax.rem(gz + k, 4)) for k in range(1, 4)]
    across = [lax.rem(plane + k, 8) for k in range(1, 8)]
    across = [(to // 4, lax.rem(to, 4), gz) for to in across]

    barrier = pltpu.get_barrier_semaphore()
    halo_in[...] = jnp.zeros_like(halo_in)
    for to in along + across:
        pl.semaphore_signal(barrier, inc=1, device_id=to, device_id_type=MESH)
    pick_ref[...] = pick_cells(gx, gy, gz).astype(jnp.bfloat16)
    beside_ref[...] = neighbours(CELLS, 2, 4, 1, 3).astype(jnp.bfloat16)

    for load in loads:
        load.wait()

    lane = iota((8, 128), 1)
    sub = iota((8, 128), 0)
    low = lane < 64
    ni, nj, nk = lane >> 4 & 3, lane >> 2 & 3, lane & 3
    weights = [weight_ref[d] for d in range(3)]
    upper = [jnp.where(n == 3, w, 0.0) for n, w in zip((ni, nj, nk), weights)]
    lower = [jnp.where(n == 0, w, 0.0) for n, w in zip((ni, nj, nk), weights)]

    def widen(blocks):
        out = []
        for j in range(4):
            turned = pltpu.roll(blocks[j], 64, 1)
            out += [jnp.where(low, blocks[j], turned), jnp.where(low, turned, blocks[j])]
        return out

    def halves(u):
        return [jnp.where(low, u[2 * j], u[2 * j + 1]) for j in range(4)]

    flat = jnp.concatenate([r_ref[x] for x in range(4)], axis=0)
    right = widen([flat[:, 128 * j : 128 * j + 128] for j in range(4)])
    marks = jnp.concatenate([class_ref[x] for x in range(4)], axis=0)
    mark = [jnp.broadcast_to(marks[:, z : z + 1], (8, 128)) for z in range(8)]

    diagonal = [jnp.zeros((8, 128), f32) for _ in range(8)]
    totals = [jnp.zeros((8, 128), f32) for _ in range(8)]
    shifts = [jnp.zeros((8, 128), f32) for _ in range(8)]
    eye = iota((64, 128), 0) == (iota((64, 128), 1) & 63)
    for k in range(16):
        block = blocks_ref[k]
        block = jnp.concatenate([block, block], axis=1)
        diag_row = jnp.sum(jnp.where(eye, block, 0.0), axis=0, keepdims=True)
        total_row = jnp.sum(block, axis=0, keepdims=True)
        rest = jnp.where(eye, 0.0, block)
        rest_hi = rest.astype(jnp.bfloat16)
        w_hi[64 * k : 64 * k + 64, :] = rest_hi
        w_lo[64 * k : 64 * k + 64, :] = (rest - rest_hi.astype(f32)).astype(jnp.bfloat16)
        for z in range(8):
            here = mark[z] == k
            diagonal[z] = jnp.where(here, diag_row, diagonal[z])
            totals[z] = jnp.where(here, total_row, totals[z])
            shifts[z] = jnp.where(here, shift_ref[k], shifts[z])
    inverse = [1.0 / d for d in diagonal]

    wide_cell = iota((8, CELLS), 1)
    wide_sub = iota((8, CELLS), 0)
    own_cell = (gx * 2 + (wide_sub >> 2)) * 64 + gy * 16 + gz * 4

    def cell_row(columns, scale):
        row = jnp.zeros((8, CELLS), f32)
        for j in range(4):
            row = row + jnp.where(wide_cell == own_cell + j, columns[j], 0.0)
        return scale * jnp.sum(row, axis=0, keepdims=True)

    note_lane = iota((1, 128), 1)

    def dots(*pairs):
        row = jnp.zeros((1, 128), f32)
        for at, (a, b) in enumerate(pairs):
            acc = a[0] * b[0]
            for z in range(1, 8):
                acc = acc + a[z] * b[z]
            acc = jnp.sum(jnp.sum(acc, axis=0, keepdims=True), axis=1, keepdims=True)
            row = row + jnp.where(note_lane == at, 0.5 * acc, 0.0)
        return row

    def tell(at, step, message):
        base, me, partners = ((0, gz, along), (4, plane, across))[step]
        note_out[at, step] = message
        note_in[at, base + me] = message
        for to in partners:
            pltpu.make_async_remote_copy(
                src_ref=note_out.at[at, step], dst_ref=note_in.at[at, base + me],
                send_sem=note_send.at[at, step], recv_sem=note_recv.at[at, step],
                device_id=to, device_id_type=MESH,
            ).start()

    def hear(at, step):
        base, count = ((0, 4), (4, 8))[step]
        span = note_in.at[at, pl.ds(base, count - 1)]
        pltpu.make_async_copy(span, span, note_recv.at[at, step]).wait()
        return jnp.sum(note_in[at, base : base + count], axis=0)

    def relay(at):
        tell(at, 1, hear(at, 0))

    def end_tell(at):
        for step, count in ((0, 3), (1, 7)):
            span = note_in.at[at, pl.ds(0, count)]
            pltpu.make_async_copy(span, span, note_send.at[at, step]).wait()

    routes = (
        (0, 1, gx < AXES[0] - 1, gx > 0, (gx + 1, gy, gz)),
        (1, 1, gx > 0, gx < AXES[0] - 1, (gx - 1, gy, gz)),
        (2, 2, gy < AXES[1] - 1, gy > 0, (gx, gy + 1, gz)),
        (4, 2, gy > 0, gy < AXES[1] - 1, (gx, gy - 1, gz)),
        (6, 1, gz < AXES[2] - 1, gz > 0, (gx, gy, gz + 1)),
        (7, 1, gz > 0, gz < AXES[2] - 1, (gx, gy, gz - 1)),
    )

    def halo_copy(at, way):
        tile, count, _, _, to = routes[way]
        span = pl.ds(3 * tile, 3 * count if at == 0 else count)
        return pltpu.make_async_remote_copy(
            src_ref=halo_out.at[at, span], dst_ref=halo_in.at[at, span],
            send_sem=halo_send.at[at, way], recv_sem=halo_recv.at[at, way],
            device_id=to, device_id_type=MESH,
        )

    odd = (sub & 1) == 1

    places = [(0, 1, 0), (1, 1, 0), (2, 2, 0), (2, 2, 1), (4, 2, 0), (4, 2, 1), (6, 1, 0), (7, 1, 0)]

    def send_halo(at, *fields):
        for f, u in enumerate(fields):
            half = halves(u)
            up = jnp.where(sub >= 6, half[3], 0.0)
            down = jnp.where(sub < 2, half[0], 0.0)
            for m in range(3):
                up = jnp.where((sub >> 1) == m, pltpu.roll(half[m], (2 * m + 2) % 8, 0), up)
            for m in range(1, 4):
                down = jnp.where((sub >> 1) == m, pltpu.roll(half[m], 2 * m, 0), down)
            tiles = [up, down]
            tiles += [jnp.where(odd, half[2 * j], pltpu.roll(half[2 * j + 1], 7, 0)) for j in range(2)]
            tiles += [jnp.where(odd, pltpu.roll(half[2 * j + 1], 1, 0), half[2 * j]) for j in range(2)]
            tiles += [u[7], u[0]]
            for (tile, count, j), value in zip(places, tiles):
                halo_out[at, 3 * tile + f * count + j] = value
        for way in range(6):
            @pl.when(routes[way][2])
            def _():
                halo_copy(at, way).start()

    def ghosts(at, f=0):
        return [halo_in[at, 3 * tile + f * count + j] for tile, count, j in places]

    def wait_halo(at):
        for way in range(6):
            @pl.when(routes[way][3])
            def _():
                halo_copy(at, way).wait_recv()

    def end_halo(at):
        for way in range(6):
            @pl.when(routes[way][2])
            def _():
                halo_copy(at, way).wait_send()

    def turn(tile, by):
        return pltpu.roll(tile, by % 8, 0) if by % 8 else tile

    def unpack_x(packed, row):
        return widen([turn(packed, row - 2 * m) for m in range(4)])

    def local_part(u):
        top = jnp.concatenate(u, axis=0)
        top_hi = top.astype(jnp.bfloat16).astype(f32)
        top_lo = top - top_hi
        classes = jnp.concatenate(mark, axis=0)
        kind = classes - (iota((64, 128), 1) >> 6)
        his, los = [], []
        for p in range(8):
            here = kind == 2 * p
            his.append(jnp.where(here, top_hi, 0.0).astype(jnp.bfloat16))
            los.append(jnp.where(here, top_lo, 0.0).astype(jnp.bfloat16))
        hi, lo = jnp.concatenate(his, axis=1), jnp.concatenate(los, axis=1)
        out = jnp.dot(hi, w_hi[...], preferred_element_type=f32)
        out = out + jnp.dot(lo, w_hi[...], preferred_element_type=f32)
        out = out + jnp.dot(hi, w_lo[...], preferred_element_type=f32)
        return [out[8 * z : 8 * z + 8] + diagonal[z] * u[z] for z in range(8)]

    def couple(u, got):
        x_before, x_after = unpack_x(got[0], 0), unpack_x(got[1], 6)
        y_before = widen([pltpu.roll(got[2], 7, 0), got[2], pltpu.roll(got[3], 7, 0), got[3]])
        y_after = widen([pltpu.roll(got[4], 1, 0), got[4], pltpu.roll(got[5], 1, 0), got[5]])
        out = []
        for z in range(8):
            x_next = jnp.where(sub >= 6, x_after[z], pltpu.roll(u[z], 6, 0))
            x_last = jnp.where(sub < 2, x_before[z], pltpu.roll(u[z], 2, 0))
            y_next = jnp.where(odd, y_after[z], pltpu.roll(u[z], 7, 0))
            y_last = jnp.where(odd, pltpu.roll(u[z], 1, 0), y_before[z])
            z_next = u[z + 1] if z < 7 else got[7]
            z_last = u[z - 1] if z > 0 else got[6]
            acc = upper[0] * pltpu.roll(x_next, 48, 1) + lower[0] * pltpu.roll(x_last, 80, 1)
            acc = acc + upper[1] * pltpu.roll(y_next, 12, 1) + lower[1] * pltpu.roll(y_last, 116, 1)
            acc = acc + upper[2] * pltpu.roll(z_next, 3, 1) + lower[2] * pltpu.roll(z_last, 125, 1)
            out.append(acc)
        return out

    def minus(a, b):
        return [p - q for p, q in zip(a, b)]

    def tell_cells(at, left, extra):
        sums = [jnp.sum(left[2 * j] + left[2 * j + 1], axis=1, keepdims=True) for j in range(4)]
        tell(at, 0, jnp.concatenate([cell_row(sums, 1.0 / 128.0), extra], axis=1))

    def correct(q, source, iterate, left, at):
        picked = jnp.sum(cells_ref[...] * q, axis=1, keepdims=True)
        tiles = [jnp.broadcast_to(picked[8 * t : 8 * t + 8], (8, 128)) for t in range(78)]
        own, x_up, x_down, y_up, y_down = tiles[:6], tiles[6:10], tiles[10:14], tiles[14:18], tiles[18:22]
        rest, scaled = [], []
        for z in range(8):
            j = z // 2
            image = totals[z] * own[j + 1]
            image = image - upper[0] * x_up[j] - lower[0] * x_down[j]
            image = image - upper[1] * y_up[j] - lower[1] * y_down[j]
            image = image - upper[2] * own[(z + 1) // 2 + 1] - lower[2] * own[(z - 1) // 2 + 1]
            rest.append(left[z] - image)
            scaled.append(rest[z] * inverse[z])
        own_part = local_part(scaled)
        wait_halo(at)
        got = []
        for g, (sent, inv, tot) in enumerate(zip(ghosts(at), ghosts(0, 1), ghosts(0, 2))):
            mid, xu, xd, yu, yd, zu, zd = tiles[22 + 7 * g : 29 + 7 * g]
            if g < 6:
                zu, zd = jnp.where(low, mid, zu), jnp.where(low, zd, mid)
            pull = upper[0] * xu + lower[0] * xd + upper[1] * yu + lower[1] * yd
            pull = pull + upper[2] * zu + lower[2] * zd
            got.append(sent - tot * mid + inv * pull)
        near = couple(scaled, got)
        result = [iterate[z] + own[z // 2 + 1] + 0.6 * scaled[z] for z in range(8)]
        image = [source[z] - rest[z] + 0.6 * (own_part[z] - near[z]) for z in range(8)]
        return result, image

    def descend(source, at, *fields, between=None):
        iterate = [0.6 * a * b for a, b in zip(source, inverse)]
        send_halo(at, iterate, *fields)
        if between is not None:
            between()
        own_part = local_part(iterate)
        wait_halo(at)
        left = minus(source, minus(own_part, couple(iterate, ghosts(at))))
        send_halo(at + 1, [a * b for a, b in zip(left, inverse)])
        return iterate, left

    nothing = jnp.zeros((1, 128), f32)
    pl.semaphore_wait(barrier, 10)
    columns = [(shifts[2 * j] + shifts[2 * j + 1])[:, :1] for j in range(4)]
    ratio = [a * b for a, b in zip(totals, inverse)]
    shift_message = jnp.concatenate([cell_row(columns, 0.125), nothing], axis=1)
    first, left = descend(right, 0, inverse, ratio, between=lambda: tell(0, 0, shift_message))
    relay(0)
    tell_cells(1, left, nothing)
    coarse = coarse_matrix(hear(0, 1)[:, :CELLS], beside_ref[...])
    relay(1)
    cells_ref[...] = exact_dot(pick_ref[...], coarse)
    z0, w0 = correct(hear(1, 1)[:, :CELLS], right, first, left, 1)

    start, left = descend(w0, 2)
    tell_cells(2, left, dots((right, z0), (z0, w0)))
    relay(2)
    heard = hear(2, 1)
    gamma, curve = heard[:, 256:257], heard[:, 257:258]
    alpha = gamma / curve
    u, v = correct(heard[:, :CELLS], w0, start, left, 3)
    z1 = [a - alpha * b for a, b in zip(z0, u)]
    w1 = [a - alpha * b for a, b in zip(w0, v)]
    r1 = [a - alpha * b for a, b in zip(right, w0)]
    tell(3, 0, jnp.concatenate([jnp.zeros((1, CELLS), f32), dots((r1, z1), (z1, w1), (z1, w0), (z0, w1))], axis=1))
    relay(3)
    heard = hear(3, 1)
    gamma_2 = heard[:, 256:257]
    beta = gamma_2 / gamma
    curve_2 = heard[:, 257:258] + beta * (heard[:, 258:259] + heard[:, 259:260]) + beta * beta * curve
    alpha_2 = gamma_2 / curve_2
    field = [alpha * a + alpha_2 * (b + beta * a) for a, b in zip(z0, z1)]
    rest = [a - alpha_2 * (b + beta * c) for a, b, c in zip(r1, w1, w0)]
    for ref, tiles in ((x_out, field), (r_out, rest)):
        whole = jnp.concatenate(halves(tiles), axis=1)
        for x in range(4):
            ref[x] = whole[2 * x : 2 * x + 2, :]
    for at in range(HALO_ROUNDS):
        end_halo(at)
        end_tell(at)


def per_device_fused(right_side, element_class, class_blocks, class_shift, face_weights):
    vmem, hbm = pl.BlockSpec(memory_space=pltpu.VMEM), pl.BlockSpec(memory_space=pltpu.HBM)
    shape = jax.ShapeDtypeStruct(right_side.shape, f32)
    return pl.pallas_call(
        fused,
        out_shape=(shape, shape),
        in_specs=[hbm] * 5,
        out_specs=(vmem, vmem),
        scratch_shapes=[
            pltpu.VMEM(right_side.shape, f32),
            pltpu.VMEM(element_class.shape, jnp.int32),
            pltpu.VMEM(class_blocks.shape, f32),
            pltpu.SMEM(class_shift.shape, f32),
            pltpu.SMEM(face_weights.shape, f32),
            pltpu.VMEM((HALO_ROUNDS, 24, 8, 128), f32),
            pltpu.VMEM((HALO_ROUNDS, 24, 8, 128), f32),
            pltpu.VMEM((HALO_ROUNDS, 2, 1, MESSAGE), f32),
            pltpu.VMEM((HALO_ROUNDS, 12, 1, MESSAGE), f32),
            pltpu.VMEM((1024, 128), jnp.bfloat16),
            pltpu.VMEM((1024, 128), jnp.bfloat16),
            pltpu.VMEM((624, CELLS), f32),
            pltpu.VMEM((624, CELLS), jnp.bfloat16),
            pltpu.VMEM((CELLS, CELLS), jnp.bfloat16),
            pltpu.SemaphoreType.DMA((5,)),
            pltpu.SemaphoreType.DMA((HALO_ROUNDS, 6)),
            pltpu.SemaphoreType.DMA((HALO_ROUNDS, 6)),
            pltpu.SemaphoreType.DMA((HALO_ROUNDS, 2)),
            pltpu.SemaphoreType.DMA((HALO_ROUNDS, 2)),
        ],
        compiler_params=pltpu.CompilerParams(
            collective_id=0, has_side_effects=True
        ),
    )(right_side, element_class, class_blocks, class_shift, face_weights)


def solution(mesh):
    in_specs = (P("gx", "gy", "gz"), P("gx", "gy", "gz"), P(), P(), P())
    out_specs = (P("gx", "gy", "gz"), P("gx", "gy", "gz"))
    small = tuple(mesh.shape[axis] for axis in ("gx", "gy", "gz")) == AXES
    body = per_device_fused if small else per_device
    return jax.shard_map(
        body, mesh=mesh, in_specs=in_specs, out_specs=out_specs, check_vma=False
    )
```

```python
import jax
import jax.numpy as jnp
import numpy as np
from jax import lax
from jax.experimental import pallas as pl
from jax.experimental.pallas import tpu as pltpu
from jax.sharding import PartitionSpec as P

P_SIZE = 64
SWEEPS = 4


highest = lax.Precision.HIGHEST
relax_weight = 0.6


def with_halo(x, sides, width):
    for axis, dim in sides:
        size, length = (lax.axis_size(axis), x.shape[dim])
        up = [(i, (i + 1) % size) for i in range(size - 1)]
        down = [(j, i) for i, j in up]
        last = lax.slice_in_dim(x, length - width, length, axis=dim)
        first = lax.slice_in_dim(x, 0, width, axis=dim)
        before = lax.ppermute(last, axis, up)
        after = lax.ppermute(first, axis, down)
        x = jnp.concatenate([before, x, after], axis=dim)
    return x


def partner_2(x, axis, bit):
    return lax.ppermute(x, axis, [(i, i ^ 1 << bit) for i in range(lax.axis_size(axis))])


def face_tables():
    node_ids = np.arange(P_SIZE)
    digits = (node_ids // 16, node_ids // 4 % 4, node_ids % 4)
    strides = (48, 12, 3)
    lower_sets = [node_ids[digits[axis_dim] == 0] for axis_dim in range(3)]
    return (lower_sets, strides)


def full_matrix(face_weights):
    lower_sets, strides = face_tables()
    pieces = []
    for axis_dim in range(3):
        lower_ids = lower_sets[axis_dim]
        upper_ids = lower_ids + strides[axis_dim]
        from_next = np.zeros((P_SIZE, P_SIZE), np.float32)
        from_next[lower_ids, upper_ids] = 1.0
        from_prev = np.zeros((P_SIZE, P_SIZE), np.float32)
        from_prev[upper_ids, lower_ids] = 1.0
        pieces.append(face_weights[axis_dim] * jnp.asarray(from_next))
        pieces.append(face_weights[axis_dim] * jnp.asarray(from_prev))
    return jnp.concatenate(pieces, axis=0)


def couple_full(cubes, face_weights):
    count = cubes.shape[0] * cubes.shape[1] * cubes.shape[2]
    padded = with_halo(cubes, (("gx", 0), ("gy", 1), ("gz", 2)), 1)
    views = [
        padded[2:, 1:-1, 1:-1],
        padded[:-2, 1:-1, 1:-1],
        padded[1:-1, 2:, 1:-1],
        padded[1:-1, :-2, 1:-1],
        padded[1:-1, 1:-1, 2:],
        padded[1:-1, 1:-1, :-2],
    ]
    stacked = jnp.concatenate(views, axis=3).reshape(count, 6 * P_SIZE)
    return jnp.dot(stacked, full_matrix(face_weights), precision=highest)


def coarsen(values):
    size_x, size_y, size_z = values.shape
    return values.reshape(size_x // 2, 2, size_y // 2, 2, size_z // 2, 2).sum(axis=(1, 3, 5))


def refine(values):
    return jnp.repeat(jnp.repeat(jnp.repeat(values, 2, axis=0), 2, axis=1), 2, axis=2)


def section_apply(values, shift):
    padded = jnp.pad(values, ((1, 1), (1, 1), (1, 1)))
    beside = padded[2:, 1:-1, 1:-1] + padded[:-2, 1:-1, 1:-1]
    beside = beside + padded[1:-1, 2:, 1:-1] + padded[1:-1, :-2, 1:-1]
    beside = beside + padded[1:-1, 1:-1, 2:] + padded[1:-1, 1:-1, :-2]
    return (6.0 + shift) * values - beside


def assemble(stacked, depth, layout):
    undo_list = []
    for axis_dim, axis_count, bit_offset, my_index in layout:
        if axis_count >= 2**depth:
            partner = partner_2(stacked, ("gx", "gy", "gz"), bit_offset + depth - 1)
            upper_half = my_index >> depth - 1 & 1 == 1
            half_size = stacked.shape[axis_dim + 1]
            low_first = jnp.concatenate([stacked, partner], axis_dim + 1)
            high_first = jnp.concatenate([partner, stacked], axis_dim + 1)
            stacked = jnp.where(upper_half, high_first, low_first)
            undo_list.append((axis_dim, upper_half, half_size))
    return (stacked, undo_list)


def unpick(values, undo_list):
    for axis_dim, upper_half, half_size in reversed(undo_list):
        values = lax.dynamic_slice_in_dim(
            values, upper_half.astype(jnp.int32) * half_size, half_size, axis_dim
        )
    return values


def fine_apply(field, operator):
    onehot, wide_blocks, face_weights = operator
    size_x, size_y, width = field.shape
    size_z = width // P_SIZE
    count = size_x * size_y * size_z
    classes = onehot.shape[1]
    flat = field.reshape(count, P_SIZE)
    products = jnp.dot(flat, wide_blocks, precision=highest).reshape(count, classes, P_SIZE)
    local_part = jnp.einsum("ekn,ek->en", products, onehot, precision=highest)
    cubes = field.reshape(size_x, size_y, size_z, P_SIZE)
    nearby = couple_full(cubes, face_weights)
    return (local_part - nearby).reshape(size_x, size_y, width)


def section_cycle(source, shift, depth, layout):
    diagonal = 6.0 + shift
    if depth == 3:
        iterate = jnp.zeros_like(source)
        for sweep_index in range(SWEEPS):
            iterate = iterate + relax_weight * (source - section_apply(iterate, shift)) / diagonal
        return iterate
    iterate = relax_weight * source / diagonal
    remainder = source - section_apply(iterate, shift)
    gathered, undo_list = assemble(
        jnp.stack([0.25 * coarsen(remainder), 0.125 * coarsen(shift)]), depth + 1, layout
    )
    coarse = section_cycle(gathered[0], gathered[1], depth + 1, layout)
    iterate = iterate + refine(unpick(coarse, undo_list))
    return iterate + relax_weight * (source - section_apply(iterate, shift)) / diagonal


def precondition(source, context):
    operator, fine_diagonal, shift_cells, row_totals, layout = context
    iterate = relax_weight * source / fine_diagonal
    remainder = source - fine_apply(iterate, operator)
    size_x, size_y, width = source.shape
    sums = remainder.reshape(size_x, size_y, width // P_SIZE, P_SIZE).sum(axis=3)
    gathered, undo_list = assemble(
        jnp.stack([coarsen(sums) / float(P_SIZE), 0.125 * coarsen(shift_cells)]), 1, layout
    )
    coarse = section_cycle(gathered[0], gathered[1], 1, layout)
    correction = refine(unpick(coarse, undo_list))
    iterate = iterate + jnp.repeat(correction, P_SIZE, axis=2)
    update = source - fine_apply(iterate, operator)
    return iterate + relax_weight * update / fine_diagonal


def total(terms):
    return lax.psum(terms, ("gx", "gy", "gz"))


def per_device(right_side, element_class, class_blocks, class_shift, face_weights):
    size_x, size_y, width = right_side.shape
    size_z = width // P_SIZE
    classes = class_blocks.shape[0]
    element_count = size_x * size_y * size_z
    onehot = (
        element_class.reshape(element_count, 1) == jnp.arange(classes, dtype=jnp.int32)[None, :]
    ).astype(jnp.float32)
    wide_blocks = jnp.transpose(class_blocks, (2, 0, 1)).reshape(P_SIZE, classes * P_SIZE)
    operator = (onehot, wide_blocks, face_weights)
    diag_table = jnp.diagonal(class_blocks, axis1=1, axis2=2)
    fine_diagonal = jnp.dot(onehot, diag_table, precision=highest).reshape(size_x, size_y, width)
    shift_cells = jnp.dot(onehot, class_shift[:, None], precision=highest).reshape(
        size_x, size_y, size_z
    )
    row_totals = None
    bits_z = lax.axis_size("gz").bit_length() - 1
    bits_y = lax.axis_size("gy").bit_length() - 1
    layout = (
        (0, lax.axis_size("gx"), bits_z + bits_y, lax.axis_index("gx")),
        (1, lax.axis_size("gy"), bits_z, lax.axis_index("gy")),
        (2, lax.axis_size("gz"), 0, lax.axis_index("gz")),
    )
    context = (operator, fine_diagonal, shift_cells, row_totals, layout)
    residual = right_side
    smoothed = precondition(residual, context)
    gamma_now = total((jnp.sum(residual * smoothed),))[0]
    direction = smoothed
    image = fine_apply(direction, operator)
    step_size = gamma_now / total((jnp.sum(direction * image),))[0]
    solution_field = step_size * direction
    residual = residual - step_size * image
    smoothed = precondition(residual, context)
    gamma_next = total((jnp.sum(residual * smoothed),))[0]
    direction = smoothed + gamma_next / gamma_now * direction
    image = fine_apply(direction, operator)
    step_size = gamma_next / total((jnp.sum(direction * image),))[0]
    solution_field = solution_field + step_size * direction
    residual = residual - step_size * image
    return (solution_field, residual)


AXES = (2, 4, 4)
CELLS = 256
DEVICES = 32
MESSAGE = 256
HALO_ROUNDS = 4
MESH = pl.DeviceIdType.MESH
f32 = jnp.float32


def iota(shape, dim):
    return lax.broadcasted_iota(jnp.int32, shape, dim)


def exact_dot(a, b):
    a = a.astype(jnp.bfloat16)
    total_dot = None
    for _ in range(3):
        part = b.astype(jnp.bfloat16)
        b = b - part.astype(f32)
        term = jnp.dot(a, part, preferred_element_type=f32)
        total_dot = term if total_dot is None else total_dot + term
    return total_dot


def neighbours(count, bits_y, bits_z, section_y, section_z):
    i, j = iota((count, count), 0), iota((count, count), 1)

    def split(k):
        return k >> bits_y + bits_z, k >> bits_z & (1 << bits_y) - 1, k & (1 << bits_z) - 1

    (xi, yi, zi), (xj, yj, zj) = split(i), split(j)
    apart = jnp.abs(xi - xj) + jnp.abs(yi - yj) + jnp.abs(zi - zj)
    same = ((yi >> section_y) == (yj >> section_y)) & ((zi >> section_z) == (zj >> section_z))
    return jnp.where((apart == 1) & same, 1.0, 0.0).astype(f32)


def coarse_matrix(shift_row, beside_1):
    i, j = iota((CELLS, CELLS), 0), iota((CELLS, CELLS), 1)
    eye = jnp.where(i == j, 1.0, 0.0).astype(f32)
    beside_2 = neighbours(32, 1, 3, 1, 3)
    j2, cell = iota((32, CELLS), 0), iota((32, CELLS), 1)
    parent = (cell >> 7) * 16 + (cell >> 5 & 1) * 8 + (cell >> 1 & 7)
    down_1 = jnp.where(parent == j2, 1.0, 0.0).astype(f32)
    ci, cj = iota((CELLS, 32), 0), iota((CELLS, 32), 1)
    up_1 = jnp.where((ci >> 7) * 16 + (ci >> 5 & 1) * 8 + (ci >> 1 & 7) == cj, 1.0, 0.0).astype(f32)
    j3, k3 = iota((8, 32), 0), iota((8, 32), 1)
    down_2 = jnp.where((k3 >> 1 & 3) == j3, 1.0, 0.0).astype(f32)
    k2, i2 = iota((32, 8), 0), iota((32, 8), 1)
    up_2 = jnp.where((k2 >> 1 & 3) == i2, 1.0, 0.0).astype(f32)
    d1_row = 6.0 + shift_row
    d1 = jnp.sum(eye * d1_row, axis=1, keepdims=True)
    d2 = 6.0 + 0.125 * jnp.sum(down_1 * shift_row, axis=1, keepdims=True)
    j3w, cellw = iota((8, CELLS), 0), iota((8, CELLS), 1)
    d3 = 6.0 + 0.015625 * jnp.sum(
        jnp.where((cellw >> 2 & 3) == j3w, shift_row, 0.0), axis=1, keepdims=True
    )
    q2 = 0.25 * exact_dot(down_1, 0.4 * eye + 0.6 * beside_1.astype(f32) / d1_row)
    x2 = 0.6 * q2 / d2
    q3 = 0.25 * exact_dot(down_2, 0.4 * q2 + exact_dot(beside_2, x2))
    x3 = 0.6 * q3 / d3
    row = iota((8, CELLS), 0)
    for _ in range(SWEEPS - 1):
        after = jnp.where(row < 3, pltpu.roll(x3, 7, 0), 0.0)
        before = jnp.where((row > 0) & (row < 4), pltpu.roll(x3, 1, 0), 0.0)
        x3 = 0.4 * x3 + 0.6 * (q3 + after + before) / d3
    x2 = x2 + exact_dot(up_2, x3)
    x2 = 0.4 * x2 + 0.6 * (q2 + exact_dot(beside_2, x2)) / d2
    x1 = 0.6 * eye / d1 + exact_dot(up_1, x2)
    return 0.4 * x1 + 0.6 * (eye + exact_dot(beside_1, x1)) / d1


def pick_cells(gx, gy, gz):
    rows = []
    s, cell = iota((8, CELLS), 0), iota((8, CELLS), 1)
    cx, cy, cz = cell >> 6, cell >> 4 & 3, cell & 15

    def pick(x, y, z):
        hit = (cx == ((gx * 4 + x) >> 1)) & (cy == ((gy * 2 + y) >> 1)) & (cz == gz * 4 + z)
        rows.append(jnp.where(hit, 1.0, 0.0).astype(f32))

    x, y = s >> 1, s & 1
    for dx, dy, zs in ((0, 0, range(-1, 5)), (1, 0, range(4)), (-1, 0, range(4)), (0, 1, range(4)), (0, -1, range(4))):
        for z in zs:
            pick(x + dx, y + dy, z)
    pairs = ((-1, y, s >> 1), (4, y, s >> 1))
    pairs += ((x, -1, 1 - y), (x, -1, 3 - y), (x, 2, y), (x, 2, y + 2), (x, y, -1), (x, y, 4))
    for gone_x, gone_y, gone_z in pairs:
        pick(gone_x, gone_y, gone_z)
        for dx, dy, dz in ((1, 0, 0), (-1, 0, 0), (0, 1, 0), (0, -1, 0), (0, 0, 1), (0, 0, -1)):
            pick(gone_x + dx, gone_y + dy, gone_z + dz)
    return jnp.concatenate(rows, axis=0)


def fused(
    r_hbm, class_hbm, blocks_hbm, shift_hbm, weight_hbm, x_out, r_out,
    r_ref, class_ref, blocks_ref, shift_ref, weight_ref,
    halo_out, halo_in, note_out, note_in, w_ref, cells_ref, pick_ref, beside_ref,
    load_sem, halo_send, halo_recv, note_send, note_recv,
):
    loads = (
        (blocks_hbm, blocks_ref), (r_hbm, r_ref), (class_hbm, class_ref),
        (shift_hbm, shift_ref), (weight_hbm, weight_ref),
    )
    loads = [pltpu.make_async_copy(a, b, load_sem.at[i]) for i, (a, b) in enumerate(loads)]
    for load in loads:
        load.start()
    gx, gy, gz = lax.axis_index("gx"), lax.axis_index("gy"), lax.axis_index("gz")

    me = gx * 16 + gy * 4 + gz
    ring_y = [gy] + [lax.rem(gy + k, 4) for k in range(1, 4)]
    ring_z = [gz] + [lax.rem(gz + k, 4) for k in range(1, 4)]
    others = [(x, y, z) for y in ring_y for x in (gx, 1 - gx) for z in ring_z][:0:-1]
    barrier = pltpu.get_barrier_semaphore()
    halo_in[...] = jnp.zeros_like(halo_in)
    for to in others:
        pl.semaphore_signal(barrier, inc=1, device_id=to, device_id_type=MESH)
    pick_ref[...] = pick_cells(gx, gy, gz).astype(jnp.bfloat16)
    beside_ref[...] = neighbours(CELLS, 2, 4, 1, 3).astype(jnp.bfloat16)

    for load in loads:
        load.wait()

    lane = iota((8, 128), 1)
    sub = iota((8, 128), 0)
    low = lane < 64
    ni, nj, nk = lane >> 4 & 3, lane >> 2 & 3, lane & 3
    weights = [weight_ref[d] for d in range(3)]
    upper = [jnp.where(n == 3, w, 0.0) for n, w in zip((ni, nj, nk), weights)]
    lower = [jnp.where(n == 0, w, 0.0) for n, w in zip((ni, nj, nk), weights)]

    def widen(blocks):
        out = []
        for j in range(4):
            turned = pltpu.roll(blocks[j], 64, 1)
            out += [jnp.where(low, blocks[j], turned), jnp.where(low, turned, blocks[j])]
        return out

    def halves(u):
        return [jnp.where(low, u[2 * j], u[2 * j + 1]) for j in range(4)]

    flat = jnp.concatenate([r_ref[x] for x in range(4)], axis=0)
    right = widen([flat[:, 128 * j : 128 * j + 128] for j in range(4)])
    marks = jnp.concatenate([class_ref[x] for x in range(4)], axis=0)
    mark = [jnp.broadcast_to(marks[:, z : z + 1], (8, 128)) for z in range(8)]

    diagonal = [jnp.zeros((8, 128), f32) for _ in range(8)]
    totals = [jnp.zeros((8, 128), f32) for _ in range(8)]
    shifts = [jnp.zeros((8, 128), f32) for _ in range(8)]
    eye = iota((64, 64), 0) == iota((64, 64), 1)
    for k in range(16):
        block = blocks_ref[k]
        rest = jnp.where(eye, 0.0, block)
        rest_hi = rest.astype(jnp.bfloat16).astype(f32)
        both = jnp.concatenate([rest_hi, rest - rest_hi], axis=1)
        w_ref[64 * k : 64 * k + 64, :] = both.astype(jnp.bfloat16)
        rest_row = jnp.sum(rest, axis=0, keepdims=True)
        diag_row = jnp.sum(block - rest, axis=0, keepdims=True)
        diag_row = jnp.concatenate([diag_row, diag_row], axis=1)
        total_row = jnp.concatenate([rest_row, rest_row], axis=1) + diag_row
        for z in range(8):
            here = mark[z] == k
            diagonal[z] = jnp.where(here, diag_row, diagonal[z])
            totals[z] = jnp.where(here, total_row, totals[z])
            shifts[z] = jnp.where(here, shift_ref[k], shifts[z])
    inverse = [1.0 / d for d in diagonal]

    own_cell = (sub >> 2) * 64 + gy * 16 + gz * 4

    def cell_row(columns, scale):
        row = jnp.zeros((8, 128), f32)
        for j in range(4):
            row = row + jnp.where(lane == own_cell + j, columns[j], 0.0)
        return scale * jnp.sum(row, axis=0, keepdims=True)

    note_lane = iota((1, 128), 1)

    def dots(*pairs):
        row = jnp.zeros((1, 128), f32)
        for at, (a, b) in enumerate(pairs):
            acc = a[0] * b[0]
            for z in range(1, 8):
                acc = acc + a[z] * b[z]
            acc = jnp.sum(jnp.sum(acc, axis=0, keepdims=True), axis=1, keepdims=True)
            row = row + jnp.where(note_lane == at, 0.5 * acc, 0.0)
        return row

    widths = (128, 128, 256, 128)

    def note(ref, at, slot):
        return ref.at[at, slot, :, pl.ds(0, widths[at])]

    def tell(at, message):
        note_out[at, :, : widths[at]] = message
        note_in[at, me, :, : widths[at]] = message
        for to in others:
            pltpu.make_async_remote_copy(
                src_ref=note_out.at[at, :, pl.ds(0, widths[at])], dst_ref=note(note_in, at, me),
                send_sem=note_send.at[at], recv_sem=note_recv.at[at],
                device_id=to, device_id_type=MESH,
            ).start()

    def hear(at):
        span = note(note_in, at, pl.ds(0, DEVICES - 1))
        pltpu.make_async_copy(span, span, note_recv.at[at]).wait()
        cells = note_in[at, :, :, :128]
        cells = [jnp.sum(cells[:16], axis=0), jnp.sum(cells[16:], axis=0)]
        return jnp.concatenate(cells, axis=1)

    def end_tell(at):
        span = note(note_in, at, pl.ds(0, DEVICES - 1))
        pltpu.make_async_copy(span, span, note_send.at[at]).wait()

    routes = (
        (0, 1, gx < AXES[0] - 1, gx > 0, (gx + 1, gy, gz)),
        (1, 1, gx > 0, gx < AXES[0] - 1, (gx - 1, gy, gz)),
        (2, 2, gy < AXES[1] - 1, gy > 0, (gx, gy + 1, gz)),
        (4, 2, gy > 0, gy < AXES[1] - 1, (gx, gy - 1, gz)),
        (6, 1, gz < AXES[2] - 1, gz > 0, (gx, gy, gz + 1)),
        (7, 1, gz > 0, gz < AXES[2] - 1, (gx, gy, gz - 1)),
    )

    def halo_copy(at, way):
        tile, count, _, _, to = routes[way]
        span = pl.ds(3 * tile, 3 * count if at == 0 else count)
        return pltpu.make_async_remote_copy(
            src_ref=halo_out.at[at, span], dst_ref=halo_in.at[at, span],
            send_sem=halo_send.at[at, way], recv_sem=halo_recv.at[at, way],
            device_id=to, device_id_type=MESH,
        )

    odd = (sub & 1) == 1

    places = [(0, 1, 0), (1, 1, 0), (2, 2, 0), (2, 2, 1), (4, 2, 0), (4, 2, 1), (6, 1, 0), (7, 1, 0)]

    def send_halo(at, *fields):
        for f, u in enumerate(fields):
            half = halves(u)
            up = jnp.where(sub >= 6, half[3], 0.0)
            down = jnp.where(sub < 2, half[0], 0.0)
            for m in range(3):
                up = jnp.where((sub >> 1) == m, pltpu.roll(half[m], (2 * m + 2) % 8, 0), up)
            for m in range(1, 4):
                down = jnp.where((sub >> 1) == m, pltpu.roll(half[m], 2 * m, 0), down)
            tiles = [up, down]
            tiles += [jnp.where(odd, half[2 * j], pltpu.roll(half[2 * j + 1], 7, 0)) for j in range(2)]
            tiles += [jnp.where(odd, pltpu.roll(half[2 * j + 1], 1, 0), half[2 * j]) for j in range(2)]
            tiles += [u[7], u[0]]
            for (tile, count, j), value in zip(places, tiles):
                halo_out[at, 3 * tile + f * count + j] = value
        for way in range(6):
            @pl.when(routes[way][2])
            def _():
                halo_copy(at, way).start()

    def ghosts(at, f=0):
        return [halo_in[at, 3 * tile + f * count + j] for tile, count, j in places]

    def wait_halo(at):
        for way in range(6):
            @pl.when(routes[way][3])
            def _():
                halo_copy(at, way).wait_recv()

    def end_halo(at):
        for way in range(6):
            @pl.when(routes[way][2])
            def _():
                halo_copy(at, way).wait_send()

    def turn(tile, by):
        return pltpu.roll(tile, by % 8, 0) if by % 8 else tile

    def unpack_x(packed, row):
        return widen([turn(packed, row - 2 * m) for m in range(4)])

    def local_part(u):
        top = jnp.concatenate(u, axis=0)
        top_hi = top.astype(jnp.bfloat16).astype(f32)
        top_lo = top - top_hi
        top = jnp.concatenate([top_hi, top_lo], axis=0)
        classes = jnp.concatenate(mark + mark, axis=0)
        kind = classes - (iota((128, 128), 1) >> 6)
        parts = [jnp.where(kind == 2 * p, top, 0.0).astype(jnp.bfloat16) for p in range(8)]
        out = jnp.dot(jnp.concatenate(parts, axis=1), w_ref[...], preferred_element_type=f32)
        out = out[:64] + out[64:]
        out = out + pltpu.roll(out, 64, 1)
        return [out[8 * z : 8 * z + 8] + diagonal[z] * u[z] for z in range(8)]

    def couple(u, got):
        x_before, x_after = unpack_x(got[0], 0), unpack_x(got[1], 6)
        y_before = widen([pltpu.roll(got[2], 7, 0), got[2], pltpu.roll(got[3], 7, 0), got[3]])
        y_after = widen([pltpu.roll(got[4], 1, 0), got[4], pltpu.roll(got[5], 1, 0), got[5]])
        out = []
        for z in range(8):
            x_next = jnp.where(sub >= 6, x_after[z], pltpu.roll(u[z], 6, 0))
            x_last = jnp.where(sub < 2, x_before[z], pltpu.roll(u[z], 2, 0))
            y_next = jnp.where(odd, y_after[z], pltpu.roll(u[z], 7, 0))
            y_last = jnp.where(odd, pltpu.roll(u[z], 1, 0), y_before[z])
            z_next = u[z + 1] if z < 7 else got[7]
            z_last = u[z - 1] if z > 0 else got[6]
            acc = upper[0] * pltpu.roll(x_next, 48, 1) + lower[0] * pltpu.roll(x_last, 80, 1)
            acc = acc + upper[1] * pltpu.roll(y_next, 12, 1) + lower[1] * pltpu.roll(y_last, 116, 1)
            acc = acc + upper[2] * pltpu.roll(z_next, 3, 1) + lower[2] * pltpu.roll(z_last, 125, 1)
            out.append(acc)
        return out

    def minus(a, b):
        return [p - q for p, q in zip(a, b)]

    def tell_cells(at, left, *extra):
        sums = [jnp.sum(left[2 * j] + left[2 * j + 1], axis=1, keepdims=True) for j in range(4)]
        tell(at, jnp.concatenate([cell_row(sums, 1.0 / 128.0), *extra], axis=1))

    def correct(q, source, iterate, left, at):
        picked = jnp.sum(cells_ref[...] * q, axis=1, keepdims=True)
        tiles = [jnp.broadcast_to(picked[8 * t : 8 * t + 8], (8, 128)) for t in range(78)]
        own, x_up, x_down, y_up, y_down = tiles[:6], tiles[6:10], tiles[10:14], tiles[14:18], tiles[18:22]
        rest, scaled = [], []
        for z in range(8):
            j = z // 2
            image = totals[z] * own[j + 1]
            image = image - upper[0] * x_up[j] - lower[0] * x_down[j]
            image = image - upper[1] * y_up[j] - lower[1] * y_down[j]
            image = image - upper[2] * own[(z + 1) // 2 + 1] - lower[2] * own[(z - 1) // 2 + 1]
            rest.append(left[z] - image)
            scaled.append(rest[z] * inverse[z])
        own_part = local_part(scaled)
        wait_halo(at)
        got = []
        for g, (sent, inv, tot) in enumerate(zip(ghosts(at), ghosts(0, 1), ghosts(0, 2))):
            mid, xu, xd, yu, yd, zu, zd = tiles[22 + 7 * g : 29 + 7 * g]
            if g < 6:
                zu, zd = jnp.where(low, mid, zu), jnp.where(low, zd, mid)
            pull = upper[0] * xu + lower[0] * xd + upper[1] * yu + lower[1] * yd
            pull = pull + upper[2] * zu + lower[2] * zd
            got.append(sent - tot * mid + inv * pull)
        near = couple(scaled, got)
        result = [iterate[z] + own[z // 2 + 1] + 0.6 * scaled[z] for z in range(8)]
        image = [source[z] - rest[z] + 0.6 * (own_part[z] - near[z]) for z in range(8)]
        return result, image

    def descend(source, at, *fields, between=None):
        iterate = [0.6 * a * b for a, b in zip(source, inverse)]
        send_halo(at, iterate, *fields)
        if between is not None:
            between()
        own_part = local_part(iterate)
        wait_halo(at)
        left = minus(source, minus(own_part, couple(iterate, ghosts(at))))
        send_halo(at + 1, [a * b for a, b in zip(left, inverse)])
        return iterate, left

    pl.semaphore_wait(barrier, DEVICES - 1)
    columns = [(shifts[2 * j] + shifts[2 * j + 1])[:, :1] for j in range(4)]
    ratio = [a * b for a, b in zip(totals, inverse)]
    shift_message = cell_row(columns, 0.125)
    first, left = descend(right, 0, inverse, ratio, between=lambda: tell(0, shift_message))
    tell_cells(1, left)
    coarse = coarse_matrix(hear(0), beside_ref[...])
    cells_ref[...] = exact_dot(pick_ref[...], coarse)
    z0, w0 = correct(hear(1), right, first, left, 1)

    start, left = descend(w0, 2)
    tell_cells(2, left, dots((right, z0), (z0, w0)))
    heard = hear(2)
    heard_dots = jnp.sum(note_in[2, :, :, 128:], axis=0)
    gamma, curve = heard_dots[:, 0:1], heard_dots[:, 1:2]
    alpha = gamma / curve
    u, v = correct(heard, w0, start, left, 3)
    z1 = [a - alpha * b for a, b in zip(z0, u)]
    w1 = [a - alpha * b for a, b in zip(w0, v)]
    r1 = [a - alpha * b for a, b in zip(right, w0)]
    tell(3, dots((r1, z1), (z1, w1), (z1, w0), (z0, w1)))
    heard = hear(3)
    heard = heard[:, :128] + heard[:, 128:]
    gamma_2 = heard[:, 0:1]
    beta = gamma_2 / gamma
    curve_2 = heard[:, 1:2] + beta * (heard[:, 2:3] + heard[:, 3:4]) + beta * beta * curve
    alpha_2 = gamma_2 / curve_2
    field = [alpha * a + alpha_2 * (b + beta * a) for a, b in zip(z0, z1)]
    rest = [a - alpha_2 * (b + beta * c) for a, b, c in zip(r1, w1, w0)]
    for ref, tiles in ((x_out, field), (r_out, rest)):
        whole = jnp.concatenate(halves(tiles), axis=1)
        for x in range(4):
            ref[x] = whole[2 * x : 2 * x + 2, :]
    for at in range(HALO_ROUNDS):
        end_halo(at)
        end_tell(at)


def per_device_fused(right_side, element_class, class_blocks, class_shift, face_weights):
    vmem, hbm = pl.BlockSpec(memory_space=pltpu.VMEM), pl.BlockSpec(memory_space=pltpu.HBM)
    shape = jax.ShapeDtypeStruct(right_side.shape, f32)
    return pl.pallas_call(
        fused,
        out_shape=(shape, shape),
        in_specs=[hbm] * 5,
        out_specs=(vmem, vmem),
        scratch_shapes=[
            pltpu.VMEM(right_side.shape, f32),
            pltpu.VMEM(element_class.shape, jnp.int32),
            pltpu.VMEM(class_blocks.shape, f32),
            pltpu.SMEM(class_shift.shape, f32),
            pltpu.SMEM(face_weights.shape, f32),
            pltpu.VMEM((HALO_ROUNDS, 24, 8, 128), f32),
            pltpu.VMEM((HALO_ROUNDS, 24, 8, 128), f32),
            pltpu.VMEM((HALO_ROUNDS, 1, MESSAGE), f32),
            pltpu.VMEM((HALO_ROUNDS, DEVICES, 1, MESSAGE), f32),
            pltpu.VMEM((1024, 128), jnp.bfloat16),
            pltpu.VMEM((624, CELLS), f32),
            pltpu.VMEM((624, CELLS), jnp.bfloat16),
            pltpu.VMEM((CELLS, CELLS), jnp.bfloat16),
            pltpu.SemaphoreType.DMA((5,)),
            pltpu.SemaphoreType.DMA((HALO_ROUNDS, 6)),
            pltpu.SemaphoreType.DMA((HALO_ROUNDS, 6)),
            pltpu.SemaphoreType.DMA((HALO_ROUNDS,)),
            pltpu.SemaphoreType.DMA((HALO_ROUNDS,)),
        ],
        compiler_params=pltpu.CompilerParams(
            collective_id=0, has_side_effects=True
        ),
    )(right_side, element_class, class_blocks, class_shift, face_weights)


def solution(mesh):
    in_specs = (P("gx", "gy", "gz"), P("gx", "gy", "gz"), P(), P(), P())
    out_specs = (P("gx", "gy", "gz"), P("gx", "gy", "gz"))
    small = tuple(mesh.shape[axis] for axis in ("gx", "gy", "gz")) == AXES
    body = per_device_fused if small else per_device
    return jax.shard_map(
        body, mesh=mesh, in_specs=in_specs, out_specs=out_specs, check_vma=False
    )
```

```python
import jax
import jax.numpy as jnp
import numpy as np
from jax import lax
from jax.experimental import pallas as pl
from jax.experimental.pallas import tpu as pltpu
from jax.sharding import PartitionSpec as P

P_SIZE = 64
SWEEPS = 4


highest = lax.Precision.HIGHEST
relax_weight = 0.6


def with_halo(x, sides, width):
    for axis, dim in sides:
        size, length = (lax.axis_size(axis), x.shape[dim])
        up = [(i, (i + 1) % size) for i in range(size - 1)]
        down = [(j, i) for i, j in up]
        last = lax.slice_in_dim(x, length - width, length, axis=dim)
        first = lax.slice_in_dim(x, 0, width, axis=dim)
        before = lax.ppermute(last, axis, up)
        after = lax.ppermute(first, axis, down)
        x = jnp.concatenate([before, x, after], axis=dim)
    return x


def partner_2(x, axis, bit):
    return lax.ppermute(x, axis, [(i, i ^ 1 << bit) for i in range(lax.axis_size(axis))])


def face_tables():
    node_ids = np.arange(P_SIZE)
    digits = (node_ids // 16, node_ids // 4 % 4, node_ids % 4)
    strides = (48, 12, 3)
    lower_sets = [node_ids[digits[axis_dim] == 0] for axis_dim in range(3)]
    return (lower_sets, strides)


def full_matrix(face_weights):
    lower_sets, strides = face_tables()
    pieces = []
    for axis_dim in range(3):
        lower_ids = lower_sets[axis_dim]
        upper_ids = lower_ids + strides[axis_dim]
        from_next = np.zeros((P_SIZE, P_SIZE), np.float32)
        from_next[lower_ids, upper_ids] = 1.0
        from_prev = np.zeros((P_SIZE, P_SIZE), np.float32)
        from_prev[upper_ids, lower_ids] = 1.0
        pieces.append(face_weights[axis_dim] * jnp.asarray(from_next))
        pieces.append(face_weights[axis_dim] * jnp.asarray(from_prev))
    return jnp.concatenate(pieces, axis=0)


def couple_full(cubes, face_weights):
    count = cubes.shape[0] * cubes.shape[1] * cubes.shape[2]
    padded = with_halo(cubes, (("gx", 0), ("gy", 1), ("gz", 2)), 1)
    views = [
        padded[2:, 1:-1, 1:-1],
        padded[:-2, 1:-1, 1:-1],
        padded[1:-1, 2:, 1:-1],
        padded[1:-1, :-2, 1:-1],
        padded[1:-1, 1:-1, 2:],
        padded[1:-1, 1:-1, :-2],
    ]
    stacked = jnp.concatenate(views, axis=3).reshape(count, 6 * P_SIZE)
    return jnp.dot(stacked, full_matrix(face_weights), precision=highest)


def coarsen(values):
    size_x, size_y, size_z = values.shape
    return values.reshape(size_x // 2, 2, size_y // 2, 2, size_z // 2, 2).sum(axis=(1, 3, 5))


def refine(values):
    return jnp.repeat(jnp.repeat(jnp.repeat(values, 2, axis=0), 2, axis=1), 2, axis=2)


def section_apply(values, shift):
    padded = jnp.pad(values, ((1, 1), (1, 1), (1, 1)))
    beside = padded[2:, 1:-1, 1:-1] + padded[:-2, 1:-1, 1:-1]
    beside = beside + padded[1:-1, 2:, 1:-1] + padded[1:-1, :-2, 1:-1]
    beside = beside + padded[1:-1, 1:-1, 2:] + padded[1:-1, 1:-1, :-2]
    return (6.0 + shift) * values - beside


def assemble(stacked, depth, layout):
    undo_list = []
    for axis_dim, axis_count, bit_offset, my_index in layout:
        if axis_count >= 2**depth:
            partner = partner_2(stacked, ("gx", "gy", "gz"), bit_offset + depth - 1)
            upper_half = my_index >> depth - 1 & 1 == 1
            half_size = stacked.shape[axis_dim + 1]
            low_first = jnp.concatenate([stacked, partner], axis_dim + 1)
            high_first = jnp.concatenate([partner, stacked], axis_dim + 1)
            stacked = jnp.where(upper_half, high_first, low_first)
            undo_list.append((axis_dim, upper_half, half_size))
    return (stacked, undo_list)


def unpick(values, undo_list):
    for axis_dim, upper_half, half_size in reversed(undo_list):
        values = lax.dynamic_slice_in_dim(
            values, upper_half.astype(jnp.int32) * half_size, half_size, axis_dim
        )
    return values


def fine_apply(field, operator):
    onehot, wide_blocks, face_weights = operator
    size_x, size_y, width = field.shape
    size_z = width // P_SIZE
    count = size_x * size_y * size_z
    classes = onehot.shape[1]
    flat = field.reshape(count, P_SIZE)
    products = jnp.dot(flat, wide_blocks, precision=highest).reshape(count, classes, P_SIZE)
    local_part = jnp.einsum("ekn,ek->en", products, onehot, precision=highest)
    cubes = field.reshape(size_x, size_y, size_z, P_SIZE)
    nearby = couple_full(cubes, face_weights)
    return (local_part - nearby).reshape(size_x, size_y, width)


def section_cycle(source, shift, depth, layout):
    diagonal = 6.0 + shift
    if depth == 3:
        iterate = jnp.zeros_like(source)
        for sweep_index in range(SWEEPS):
            iterate = iterate + relax_weight * (source - section_apply(iterate, shift)) / diagonal
        return iterate
    iterate = relax_weight * source / diagonal
    remainder = source - section_apply(iterate, shift)
    gathered, undo_list = assemble(
        jnp.stack([0.25 * coarsen(remainder), 0.125 * coarsen(shift)]), depth + 1, layout
    )
    coarse = section_cycle(gathered[0], gathered[1], depth + 1, layout)
    iterate = iterate + refine(unpick(coarse, undo_list))
    return iterate + relax_weight * (source - section_apply(iterate, shift)) / diagonal


def precondition(source, context):
    operator, fine_diagonal, shift_cells, row_totals, layout = context
    iterate = relax_weight * source / fine_diagonal
    remainder = source - fine_apply(iterate, operator)
    size_x, size_y, width = source.shape
    sums = remainder.reshape(size_x, size_y, width // P_SIZE, P_SIZE).sum(axis=3)
    gathered, undo_list = assemble(
        jnp.stack([coarsen(sums) / float(P_SIZE), 0.125 * coarsen(shift_cells)]), 1, layout
    )
    coarse = section_cycle(gathered[0], gathered[1], 1, layout)
    correction = refine(unpick(coarse, undo_list))
    iterate = iterate + jnp.repeat(correction, P_SIZE, axis=2)
    update = source - fine_apply(iterate, operator)
    return iterate + relax_weight * update / fine_diagonal


def total(terms):
    return lax.psum(terms, ("gx", "gy", "gz"))


def per_device(right_side, element_class, class_blocks, class_shift, face_weights):
    size_x, size_y, width = right_side.shape
    size_z = width // P_SIZE
    classes = class_blocks.shape[0]
    element_count = size_x * size_y * size_z
    onehot = (
        element_class.reshape(element_count, 1) == jnp.arange(classes, dtype=jnp.int32)[None, :]
    ).astype(jnp.float32)
    wide_blocks = jnp.transpose(class_blocks, (2, 0, 1)).reshape(P_SIZE, classes * P_SIZE)
    operator = (onehot, wide_blocks, face_weights)
    diag_table = jnp.diagonal(class_blocks, axis1=1, axis2=2)
    fine_diagonal = jnp.dot(onehot, diag_table, precision=highest).reshape(size_x, size_y, width)
    shift_cells = jnp.dot(onehot, class_shift[:, None], precision=highest).reshape(
        size_x, size_y, size_z
    )
    row_totals = None
    bits_z = lax.axis_size("gz").bit_length() - 1
    bits_y = lax.axis_size("gy").bit_length() - 1
    layout = (
        (0, lax.axis_size("gx"), bits_z + bits_y, lax.axis_index("gx")),
        (1, lax.axis_size("gy"), bits_z, lax.axis_index("gy")),
        (2, lax.axis_size("gz"), 0, lax.axis_index("gz")),
    )
    context = (operator, fine_diagonal, shift_cells, row_totals, layout)
    residual = right_side
    smoothed = precondition(residual, context)
    gamma_now = total((jnp.sum(residual * smoothed),))[0]
    direction = smoothed
    image = fine_apply(direction, operator)
    step_size = gamma_now / total((jnp.sum(direction * image),))[0]
    solution_field = step_size * direction
    residual = residual - step_size * image
    smoothed = precondition(residual, context)
    gamma_next = total((jnp.sum(residual * smoothed),))[0]
    direction = smoothed + gamma_next / gamma_now * direction
    image = fine_apply(direction, operator)
    step_size = gamma_next / total((jnp.sum(direction * image),))[0]
    solution_field = solution_field + step_size * direction
    residual = residual - step_size * image
    return (solution_field, residual)


AXES = (2, 4, 4)
CELLS = 256
DEVICES = 32
MESSAGE = 256
HALO_ROUNDS = 4
MESH = pl.DeviceIdType.MESH
f32 = jnp.float32


def iota(shape, dim):
    return lax.broadcasted_iota(jnp.int32, shape, dim)


def exact_dot(a, b):
    a = a.astype(jnp.bfloat16)
    total_dot = None
    for _ in range(3):
        part = b.astype(jnp.bfloat16)
        b = b - part.astype(f32)
        term = jnp.dot(a, part, preferred_element_type=f32)
        total_dot = term if total_dot is None else total_dot + term
    return total_dot


def neighbours(count, bits_y, bits_z, section_y, section_z):
    i, j = iota((count, count), 0), iota((count, count), 1)

    def split(k):
        return k >> bits_y + bits_z, k >> bits_z & (1 << bits_y) - 1, k & (1 << bits_z) - 1

    (xi, yi, zi), (xj, yj, zj) = split(i), split(j)
    apart = jnp.abs(xi - xj) + jnp.abs(yi - yj) + jnp.abs(zi - zj)
    same = ((yi >> section_y) == (yj >> section_y)) & ((zi >> section_z) == (zj >> section_z))
    return jnp.where((apart == 1) & same, 1.0, 0.0).astype(f32)


def coarse_matrix(shift_row, beside_1):
    i, j = iota((CELLS, CELLS), 0), iota((CELLS, CELLS), 1)
    eye = jnp.where(i == j, 1.0, 0.0).astype(f32)
    beside_2 = neighbours(32, 1, 3, 1, 3)
    j2, cell = iota((32, CELLS), 0), iota((32, CELLS), 1)
    parent = (cell >> 7) * 16 + (cell >> 5 & 1) * 8 + (cell >> 1 & 7)
    down_1 = jnp.where(parent == j2, 1.0, 0.0).astype(f32)
    ci, cj = iota((CELLS, 32), 0), iota((CELLS, 32), 1)
    up_1 = jnp.where((ci >> 7) * 16 + (ci >> 5 & 1) * 8 + (ci >> 1 & 7) == cj, 1.0, 0.0).astype(f32)
    j3, k3 = iota((8, 32), 0), iota((8, 32), 1)
    down_2 = jnp.where((k3 >> 1 & 3) == j3, 1.0, 0.0).astype(f32)
    k2, i2 = iota((32, 8), 0), iota((32, 8), 1)
    up_2 = jnp.where((k2 >> 1 & 3) == i2, 1.0, 0.0).astype(f32)
    d1_row = 6.0 + shift_row
    d1 = jnp.sum(eye * d1_row, axis=1, keepdims=True)
    d2 = 6.0 + 0.125 * jnp.sum(down_1 * shift_row, axis=1, keepdims=True)
    j3w, cellw = iota((8, CELLS), 0), iota((8, CELLS), 1)
    d3 = 6.0 + 0.015625 * jnp.sum(
        jnp.where((cellw >> 2 & 3) == j3w, shift_row, 0.0), axis=1, keepdims=True
    )
    q2 = 0.25 * exact_dot(down_1, 0.4 * eye + 0.6 * beside_1.astype(f32) / d1_row)
    x2 = 0.6 * q2 / d2
    q3 = 0.25 * exact_dot(down_2, 0.4 * q2 + exact_dot(beside_2, x2))
    x3 = 0.6 * q3 / d3
    row = iota((8, CELLS), 0)
    for _ in range(SWEEPS - 1):
        after = jnp.where(row < 3, pltpu.roll(x3, 7, 0), 0.0)
        before = jnp.where((row > 0) & (row < 4), pltpu.roll(x3, 1, 0), 0.0)
        x3 = 0.4 * x3 + 0.6 * (q3 + after + before) / d3
    x2 = x2 + exact_dot(up_2, x3)
    x2 = 0.4 * x2 + 0.6 * (q2 + exact_dot(beside_2, x2)) / d2
    x1 = 0.6 * eye / d1 + exact_dot(up_1, x2)
    return 0.4 * x1 + 0.6 * (eye + exact_dot(beside_1, x1)) / d1


def pick_cells(gx, gy, gz):
    rows = []
    s, cell = iota((8, CELLS), 0), iota((8, CELLS), 1)
    cx, cy, cz = cell >> 6, cell >> 4 & 3, cell & 15

    def pick(x, y, z):
        hit = (cx == ((gx * 4 + x) >> 1)) & (cy == ((gy * 2 + y) >> 1)) & (cz == gz * 4 + z)
        rows.append(jnp.where(hit, 1.0, 0.0).astype(f32))

    x, y = s >> 1, s & 1
    for dx, dy, zs in ((0, 0, range(-1, 5)), (1, 0, range(4)), (-1, 0, range(4)), (0, 1, range(4)), (0, -1, range(4))):
        for z in zs:
            pick(x + dx, y + dy, z)
    pairs = ((-1, y, s >> 1), (4, y, s >> 1))
    pairs += ((x, -1, 1 - y), (x, -1, 3 - y), (x, 2, y), (x, 2, y + 2), (x, y, -1), (x, y, 4))
    for gone_x, gone_y, gone_z in pairs:
        pick(gone_x, gone_y, gone_z)
        for dx, dy, dz in ((1, 0, 0), (-1, 0, 0), (0, 1, 0), (0, -1, 0), (0, 0, 1), (0, 0, -1)):
            pick(gone_x + dx, gone_y + dy, gone_z + dz)
    return jnp.concatenate(rows, axis=0)


def fused(
    r_hbm, class_hbm, blocks_hbm, shift_hbm, weight_hbm, out_ref,
    r_ref, class_ref, blocks_ref, shift_ref, weight_ref,
    halo_out, halo_in, note_out, note_in, w_ref, cells_ref, pick_ref, beside_ref,
    load_sem, halo_send, halo_recv, note_send, note_recv,
):
    loads = (
        (blocks_hbm, blocks_ref), (r_hbm, r_ref), (class_hbm, class_ref),
        (shift_hbm, shift_ref), (weight_hbm, weight_ref),
    )
    loads = [pltpu.make_async_copy(a, b, load_sem.at[i]) for i, (a, b) in enumerate(loads)]
    for load in loads:
        load.start()
    gx, gy, gz = lax.axis_index("gx"), lax.axis_index("gy"), lax.axis_index("gz")

    me = gx * 16 + gy * 4 + gz
    ring_y = [gy] + [lax.rem(gy + k, 4) for k in range(1, 4)]
    ring_z = [gz] + [lax.rem(gz + k, 4) for k in range(1, 4)]
    others = [(x, y, z) for y in ring_y for x in (gx, 1 - gx) for z in ring_z][:0:-1]
    barrier = pltpu.get_barrier_semaphore()
    halo_in[...] = jnp.zeros_like(halo_in)
    for to in others:
        pl.semaphore_signal(barrier, inc=1, device_id=to, device_id_type=MESH)
    pick_ref[...] = pick_cells(gx, gy, gz).astype(jnp.bfloat16)
    beside_ref[...] = neighbours(CELLS, 2, 4, 1, 3).astype(jnp.bfloat16)

    for load in loads:
        load.wait()

    lane = iota((8, 128), 1)
    sub = iota((8, 128), 0)
    low = lane < 64
    ni, nj, nk = lane >> 4 & 3, lane >> 2 & 3, lane & 3
    weights = [weight_ref[d] for d in range(3)]
    upper = [jnp.where(n == 3, w, 0.0) for n, w in zip((ni, nj, nk), weights)]
    lower = [jnp.where(n == 0, w, 0.0) for n, w in zip((ni, nj, nk), weights)]

    def widen(blocks):
        out = []
        for j in range(4):
            turned = pltpu.roll(blocks[j], 64, 1)
            out += [jnp.where(low, blocks[j], turned), jnp.where(low, turned, blocks[j])]
        return out

    def halves(u):
        return [jnp.where(low, u[2 * j], u[2 * j + 1]) for j in range(4)]

    flat = jnp.concatenate([r_ref[x] for x in range(4)], axis=0)
    right = widen([flat[:, 128 * j : 128 * j + 128] for j in range(4)])
    marks = jnp.concatenate([class_ref[x] for x in range(4)], axis=0)
    mark = [jnp.broadcast_to(marks[:, z : z + 1], (8, 128)) for z in range(8)]

    def by_class(rows):
        out = [jnp.broadcast_to(rows[0], (8, 128)) for _ in range(8)]
        for k in range(1, 16):
            out = [jnp.where(here == k, rows[k], old) for here, old in zip(mark, out)]
        return out

    def twice(row):
        return jnp.concatenate([row, row], axis=1)

    eye = iota((64, 64), 0) == iota((64, 64), 1)
    diag_rows = [
        twice(jnp.sum(jnp.where(eye, blocks_ref[k], 0.0), axis=0, keepdims=True)) for k in range(16)
    ]
    diagonal = by_class(diag_rows)
    inverse = [1.0 / d for d in diagonal]

    def prepare():
        rows = []
        for k in range(16):
            rest = jnp.where(eye, 0.0, blocks_ref[k])
            rest_hi = rest.astype(jnp.bfloat16).astype(f32)
            both = jnp.concatenate([rest_hi, rest - rest_hi], axis=1)
            w_ref[64 * k : 64 * k + 64, :] = both.astype(jnp.bfloat16)
            rows.append(twice(jnp.sum(rest, axis=0, keepdims=True)) + diag_rows[k])
        return by_class(rows), by_class([shift_ref[k] for k in range(16)])

    own_cell = (sub >> 2) * 64 + gy * 16 + gz * 4

    def cell_row(columns, scale):
        row = jnp.zeros((8, 128), f32)
        for j in range(4):
            row = row + jnp.where(lane == own_cell + j, columns[j], 0.0)
        return scale * jnp.sum(row, axis=0, keepdims=True)

    note_lane = iota((1, 128), 1)

    def dots(*pairs):
        row = jnp.zeros((1, 128), f32)
        for at, (a, b) in enumerate(pairs):
            acc = a[0] * b[0]
            for z in range(1, 8):
                acc = acc + a[z] * b[z]
            acc = jnp.sum(jnp.sum(acc, axis=0, keepdims=True), axis=1, keepdims=True)
            row = row + jnp.where(note_lane == at, 0.5 * acc, 0.0)
        return row

    widths = (128, 128, 256, 128)

    def note(ref, at, slot):
        return ref.at[at, slot, :, pl.ds(0, widths[at])]

    def tell(at, message):
        note_out[at, :, : widths[at]] = message
        note_in[at, me, :, : widths[at]] = message
        for to in others:
            pltpu.make_async_remote_copy(
                src_ref=note_out.at[at, :, pl.ds(0, widths[at])], dst_ref=note(note_in, at, me),
                send_sem=note_send.at[at], recv_sem=note_recv.at[at],
                device_id=to, device_id_type=MESH,
            ).start()

    def hear(at):
        span = note(note_in, at, pl.ds(0, DEVICES - 1))
        pltpu.make_async_copy(span, span, note_recv.at[at]).wait()
        cells = note_in[at, :, :, :128]
        cells = [jnp.sum(cells[:16], axis=0), jnp.sum(cells[16:], axis=0)]
        return jnp.concatenate(cells, axis=1)

    def end_tell(at):
        span = note(note_in, at, pl.ds(0, DEVICES - 1))
        pltpu.make_async_copy(span, span, note_send.at[at]).wait()

    routes = (
        (0, 1, gx < AXES[0] - 1, gx > 0, (gx + 1, gy, gz)),
        (1, 1, gx > 0, gx < AXES[0] - 1, (gx - 1, gy, gz)),
        (2, 2, gy < AXES[1] - 1, gy > 0, (gx, gy + 1, gz)),
        (4, 2, gy > 0, gy < AXES[1] - 1, (gx, gy - 1, gz)),
        (6, 1, gz < AXES[2] - 1, gz > 0, (gx, gy, gz + 1)),
        (7, 1, gz > 0, gz < AXES[2] - 1, (gx, gy, gz - 1)),
    )

    def halo_copy(at, way):
        tile, count, _, _, to = routes[way]
        span = pl.ds(3 * tile, 3 * count if at == 1 else count)
        return pltpu.make_async_remote_copy(
            src_ref=halo_out.at[at, span], dst_ref=halo_in.at[at, span],
            send_sem=halo_send.at[at, way], recv_sem=halo_recv.at[at, way],
            device_id=to, device_id_type=MESH,
        )

    odd = (sub & 1) == 1

    places = [(0, 1, 0), (1, 1, 0), (2, 2, 0), (2, 2, 1), (4, 2, 0), (4, 2, 1), (6, 1, 0), (7, 1, 0)]

    def send_halo(at, *fields):
        for f, u in enumerate(fields):
            half = halves(u)
            up = jnp.where(sub >= 6, half[3], 0.0)
            down = jnp.where(sub < 2, half[0], 0.0)
            for m in range(3):
                up = jnp.where((sub >> 1) == m, pltpu.roll(half[m], (2 * m + 2) % 8, 0), up)
            for m in range(1, 4):
                down = jnp.where((sub >> 1) == m, pltpu.roll(half[m], 2 * m, 0), down)
            tiles = [up, down]
            tiles += [jnp.where(odd, half[2 * j], pltpu.roll(half[2 * j + 1], 7, 0)) for j in range(2)]
            tiles += [jnp.where(odd, pltpu.roll(half[2 * j + 1], 1, 0), half[2 * j]) for j in range(2)]
            tiles += [u[7], u[0]]
            for (tile, count, j), value in zip(places, tiles):
                halo_out[at, 3 * tile + f * count + j] = value
        for way in range(6):
            @pl.when(routes[way][2])
            def _():
                halo_copy(at, way).start()

    def ghosts(at, f=0):
        return [halo_in[at, 3 * tile + f * count + j] for tile, count, j in places]

    def wait_halo(at):
        for way in range(6):
            @pl.when(routes[way][3])
            def _():
                halo_copy(at, way).wait_recv()

    def end_halo(at):
        for way in range(6):
            @pl.when(routes[way][2])
            def _():
                halo_copy(at, way).wait_send()

    def turn(tile, by):
        return pltpu.roll(tile, by % 8, 0) if by % 8 else tile

    def unpack_x(packed, row):
        return widen([turn(packed, row - 2 * m) for m in range(4)])

    def local_part(u):
        top = jnp.concatenate(u, axis=0)
        top_hi = top.astype(jnp.bfloat16).astype(f32)
        top_lo = top - top_hi
        top = jnp.concatenate([top_hi, top_lo], axis=0)
        classes = jnp.concatenate(mark + mark, axis=0)
        kind = classes - (iota((128, 128), 1) >> 6)
        parts = [jnp.where(kind == 2 * p, top, 0.0).astype(jnp.bfloat16) for p in range(8)]
        out = jnp.dot(jnp.concatenate(parts, axis=1), w_ref[...], preferred_element_type=f32)
        out = out[:64] + out[64:]
        out = out + pltpu.roll(out, 64, 1)
        return [out[8 * z : 8 * z + 8] + diagonal[z] * u[z] for z in range(8)]

    def couple(u, got):
        x_before, x_after = unpack_x(got[0], 0), unpack_x(got[1], 6)
        y_before = widen([pltpu.roll(got[2], 7, 0), got[2], pltpu.roll(got[3], 7, 0), got[3]])
        y_after = widen([pltpu.roll(got[4], 1, 0), got[4], pltpu.roll(got[5], 1, 0), got[5]])
        out = []
        for z in range(8):
            x_next = jnp.where(sub >= 6, x_after[z], pltpu.roll(u[z], 6, 0))
            x_last = jnp.where(sub < 2, x_before[z], pltpu.roll(u[z], 2, 0))
            y_next = jnp.where(odd, y_after[z], pltpu.roll(u[z], 7, 0))
            y_last = jnp.where(odd, pltpu.roll(u[z], 1, 0), y_before[z])
            z_next = u[z + 1] if z < 7 else got[7]
            z_last = u[z - 1] if z > 0 else got[6]
            acc = upper[0] * pltpu.roll(x_next, 48, 1) + lower[0] * pltpu.roll(x_last, 80, 1)
            acc = acc + upper[1] * pltpu.roll(y_next, 12, 1) + lower[1] * pltpu.roll(y_last, 116, 1)
            acc = acc + upper[2] * pltpu.roll(z_next, 3, 1) + lower[2] * pltpu.roll(z_last, 125, 1)
            out.append(acc)
        return out

    def minus(a, b):
        return [p - q for p, q in zip(a, b)]

    def cell_sums(left):
        sums = [jnp.sum(left[2 * j] + left[2 * j + 1], axis=1, keepdims=True) for j in range(4)]
        return cell_row(sums, 1.0 / 128.0)

    def correct(q, source, iterate, left, totals, at):
        picked = jnp.sum(cells_ref[...] * q, axis=1, keepdims=True)
        tiles = [jnp.broadcast_to(picked[8 * t : 8 * t + 8], (8, 128)) for t in range(78)]
        own, x_up, x_down, y_up, y_down = tiles[:6], tiles[6:10], tiles[10:14], tiles[14:18], tiles[18:22]
        rest, scaled = [], []
        for z in range(8):
            j = z // 2
            image = totals[z] * own[j + 1]
            image = image - upper[0] * x_up[j] - lower[0] * x_down[j]
            image = image - upper[1] * y_up[j] - lower[1] * y_down[j]
            image = image - upper[2] * own[(z + 1) // 2 + 1] - lower[2] * own[(z - 1) // 2 + 1]
            rest.append(left[z] - image)
            scaled.append(rest[z] * inverse[z])
        own_part = local_part(scaled)
        wait_halo(at)
        got = []
        for g, (sent, inv, tot) in enumerate(zip(ghosts(at), ghosts(1, 1), ghosts(1, 2))):
            mid, xu, xd, yu, yd, zu, zd = tiles[22 + 7 * g : 29 + 7 * g]
            if g < 6:
                zu, zd = jnp.where(low, mid, zu), jnp.where(low, zd, mid)
            pull = upper[0] * xu + lower[0] * xd + upper[1] * yu + lower[1] * yd
            pull = pull + upper[2] * zu + lower[2] * zd
            got.append(sent - tot * mid + inv * pull)
        near = couple(scaled, got)
        result = [iterate[z] + own[z // 2 + 1] + 0.6 * scaled[z] for z in range(8)]
        image = [source[z] - rest[z] + 0.6 * (own_part[z] - near[z]) for z in range(8)]
        return result, image

    def scale(a, b):
        return [p * q for p, q in zip(a, b)]

    def remainder(source, iterate, at):
        own_part = local_part(iterate)
        wait_halo(at)
        return minus(source, minus(own_part, couple(iterate, ghosts(at))))

    first = [0.6 * a for a in scale(right, inverse)]
    pl.semaphore_wait(barrier, DEVICES - 1)
    send_halo(0, first)
    totals, shifts = prepare()
    columns = [(shifts[2 * j] + shifts[2 * j + 1])[:, :1] for j in range(4)]
    tell(0, cell_row(columns, 0.125))
    left = remainder(right, first, 0)
    tell(1, cell_sums(left))
    send_halo(1, scale(left, inverse), inverse, scale(totals, inverse))
    coarse = coarse_matrix(hear(0), beside_ref[...])
    cells_ref[...] = exact_dot(pick_ref[...], coarse)
    z0, w0 = correct(hear(1), right, first, left, totals, 1)

    start = [0.6 * a for a in scale(w0, inverse)]
    send_halo(2, start)
    early_dots = dots((right, z0), (z0, w0))
    left = remainder(w0, start, 2)
    tell(2, jnp.concatenate([cell_sums(left), early_dots], axis=1))
    send_halo(3, scale(left, inverse))
    heard = hear(2)
    heard_dots = jnp.sum(note_in[2, :, :, 128:], axis=0)
    gamma, curve = heard_dots[:, 0:1], heard_dots[:, 1:2]
    alpha = gamma / curve
    u, v = correct(heard, w0, start, left, totals, 3)
    z1 = [a - alpha * b for a, b in zip(z0, u)]
    w1 = [a - alpha * b for a, b in zip(w0, v)]
    r1 = [a - alpha * b for a, b in zip(right, w0)]
    tell(3, dots((r1, z1), (z1, w1), (z1, w0), (z0, w1)))
    for at in range(HALO_ROUNDS):
        end_halo(at)
    for at in range(3):
        end_tell(at)
    heard = hear(3)
    heard = heard[:, :128] + heard[:, 128:]
    gamma_2 = heard[:, 0:1]
    beta = gamma_2 / gamma
    curve_2 = heard[:, 1:2] + beta * (heard[:, 2:3] + heard[:, 3:4]) + beta * beta * curve
    alpha_2 = gamma_2 / curve_2
    field = [alpha * a + alpha_2 * (b + beta * a) for a, b in zip(z0, z1)]
    rest = [a - alpha_2 * (b + beta * c) for a, b, c in zip(r1, w1, w0)]
    whole = jnp.concatenate(halves(field) + halves(rest), axis=1)
    for x in range(4):
        out_ref[x] = whole[2 * x : 2 * x + 2, :]
    end_tell(3)


def per_device_fused(right_side, element_class, class_blocks, class_shift, face_weights):
    vmem, hbm = pl.BlockSpec(memory_space=pltpu.VMEM), pl.BlockSpec(memory_space=pltpu.HBM)
    size_x, size_y, width = right_side.shape
    both = pl.pallas_call(
        fused,
        out_shape=jax.ShapeDtypeStruct((size_x, size_y, 2 * width), f32),
        in_specs=[hbm] * 5,
        out_specs=vmem,
        scratch_shapes=[
            pltpu.VMEM(right_side.shape, f32),
            pltpu.VMEM(element_class.shape, jnp.int32),
            pltpu.VMEM(class_blocks.shape, f32),
            pltpu.SMEM(class_shift.shape, f32),
            pltpu.SMEM(face_weights.shape, f32),
            pltpu.VMEM((HALO_ROUNDS, 24, 8, 128), f32),
            pltpu.VMEM((HALO_ROUNDS, 24, 8, 128), f32),
            pltpu.VMEM((HALO_ROUNDS, 1, MESSAGE), f32),
            pltpu.VMEM((HALO_ROUNDS, DEVICES, 1, MESSAGE), f32),
            pltpu.VMEM((1024, 128), jnp.bfloat16),
            pltpu.VMEM((624, CELLS), f32),
            pltpu.VMEM((624, CELLS), jnp.bfloat16),
            pltpu.VMEM((CELLS, CELLS), jnp.bfloat16),
            pltpu.SemaphoreType.DMA((5,)),
            pltpu.SemaphoreType.DMA((HALO_ROUNDS, 6)),
            pltpu.SemaphoreType.DMA((HALO_ROUNDS, 6)),
            pltpu.SemaphoreType.DMA((HALO_ROUNDS,)),
            pltpu.SemaphoreType.DMA((HALO_ROUNDS,)),
        ],
        compiler_params=pltpu.CompilerParams(
            collective_id=0, has_side_effects=True
        ),
    )(right_side, element_class, class_blocks, class_shift, face_weights)
    return both[:, :, :width], both[:, :, width:]


def solution(mesh):
    in_specs = (P("gx", "gy", "gz"), P("gx", "gy", "gz"), P(), P(), P())
    out_specs = (P("gx", "gy", "gz"), P("gx", "gy", "gz"))
    small = tuple(mesh.shape[axis] for axis in ("gx", "gy", "gz")) == AXES
    body = per_device_fused if small else per_device
    return jax.shard_map(
        body, mesh=mesh, in_specs=in_specs, out_specs=out_specs, check_vma=False
    )
```

```python
import jax
import jax.numpy as jnp
import numpy as np
from jax import lax
from jax.experimental import pallas as pl
from jax.experimental.pallas import tpu as pltpu
from jax.sharding import PartitionSpec as P

P_SIZE = 64
SWEEPS = 4


highest = lax.Precision.HIGHEST
relax_weight = 0.6


def with_halo(x, sides, width):
    for axis, dim in sides:
        size, length = (lax.axis_size(axis), x.shape[dim])
        up = [(i, (i + 1) % size) for i in range(size - 1)]
        down = [(j, i) for i, j in up]
        last = lax.slice_in_dim(x, length - width, length, axis=dim)
        first = lax.slice_in_dim(x, 0, width, axis=dim)
        before = lax.ppermute(last, axis, up)
        after = lax.ppermute(first, axis, down)
        x = jnp.concatenate([before, x, after], axis=dim)
    return x


def partner_2(x, axis, bit):
    return lax.ppermute(x, axis, [(i, i ^ 1 << bit) for i in range(lax.axis_size(axis))])


def face_tables():
    node_ids = np.arange(P_SIZE)
    digits = (node_ids // 16, node_ids // 4 % 4, node_ids % 4)
    strides = (48, 12, 3)
    lower_sets = [node_ids[digits[axis_dim] == 0] for axis_dim in range(3)]
    return (lower_sets, strides)


def full_matrix(face_weights):
    lower_sets, strides = face_tables()
    pieces = []
    for axis_dim in range(3):
        lower_ids = lower_sets[axis_dim]
        upper_ids = lower_ids + strides[axis_dim]
        from_next = np.zeros((P_SIZE, P_SIZE), np.float32)
        from_next[lower_ids, upper_ids] = 1.0
        from_prev = np.zeros((P_SIZE, P_SIZE), np.float32)
        from_prev[upper_ids, lower_ids] = 1.0
        pieces.append(face_weights[axis_dim] * jnp.asarray(from_next))
        pieces.append(face_weights[axis_dim] * jnp.asarray(from_prev))
    return jnp.concatenate(pieces, axis=0)


def couple_full(cubes, face_weights):
    count = cubes.shape[0] * cubes.shape[1] * cubes.shape[2]
    padded = with_halo(cubes, (("gx", 0), ("gy", 1), ("gz", 2)), 1)
    views = [
        padded[2:, 1:-1, 1:-1],
        padded[:-2, 1:-1, 1:-1],
        padded[1:-1, 2:, 1:-1],
        padded[1:-1, :-2, 1:-1],
        padded[1:-1, 1:-1, 2:],
        padded[1:-1, 1:-1, :-2],
    ]
    stacked = jnp.concatenate(views, axis=3).reshape(count, 6 * P_SIZE)
    return jnp.dot(stacked, full_matrix(face_weights), precision=highest)


def coarsen(values):
    size_x, size_y, size_z = values.shape
    return values.reshape(size_x // 2, 2, size_y // 2, 2, size_z // 2, 2).sum(axis=(1, 3, 5))


def refine(values):
    return jnp.repeat(jnp.repeat(jnp.repeat(values, 2, axis=0), 2, axis=1), 2, axis=2)


def section_apply(values, shift):
    padded = jnp.pad(values, ((1, 1), (1, 1), (1, 1)))
    beside = padded[2:, 1:-1, 1:-1] + padded[:-2, 1:-1, 1:-1]
    beside = beside + padded[1:-1, 2:, 1:-1] + padded[1:-1, :-2, 1:-1]
    beside = beside + padded[1:-1, 1:-1, 2:] + padded[1:-1, 1:-1, :-2]
    return (6.0 + shift) * values - beside


def assemble(stacked, depth, layout):
    undo_list = []
    for axis_dim, axis_count, bit_offset, my_index in layout:
        if axis_count >= 2**depth:
            partner = partner_2(stacked, ("gx", "gy", "gz"), bit_offset + depth - 1)
            upper_half = my_index >> depth - 1 & 1 == 1
            half_size = stacked.shape[axis_dim + 1]
            low_first = jnp.concatenate([stacked, partner], axis_dim + 1)
            high_first = jnp.concatenate([partner, stacked], axis_dim + 1)
            stacked = jnp.where(upper_half, high_first, low_first)
            undo_list.append((axis_dim, upper_half, half_size))
    return (stacked, undo_list)


def unpick(values, undo_list):
    for axis_dim, upper_half, half_size in reversed(undo_list):
        values = lax.dynamic_slice_in_dim(
            values, upper_half.astype(jnp.int32) * half_size, half_size, axis_dim
        )
    return values


def fine_apply(field, operator):
    onehot, wide_blocks, face_weights = operator
    size_x, size_y, width = field.shape
    size_z = width // P_SIZE
    count = size_x * size_y * size_z
    classes = onehot.shape[1]
    flat = field.reshape(count, P_SIZE)
    products = jnp.dot(flat, wide_blocks, precision=highest).reshape(count, classes, P_SIZE)
    local_part = jnp.einsum("ekn,ek->en", products, onehot, precision=highest)
    cubes = field.reshape(size_x, size_y, size_z, P_SIZE)
    nearby = couple_full(cubes, face_weights)
    return (local_part - nearby).reshape(size_x, size_y, width)


def section_cycle(source, shift, depth, layout):
    diagonal = 6.0 + shift
    if depth == 3:
        iterate = jnp.zeros_like(source)
        for sweep_index in range(SWEEPS):
            iterate = iterate + relax_weight * (source - section_apply(iterate, shift)) / diagonal
        return iterate
    iterate = relax_weight * source / diagonal
    remainder = source - section_apply(iterate, shift)
    gathered, undo_list = assemble(
        jnp.stack([0.25 * coarsen(remainder), 0.125 * coarsen(shift)]), depth + 1, layout
    )
    coarse = section_cycle(gathered[0], gathered[1], depth + 1, layout)
    iterate = iterate + refine(unpick(coarse, undo_list))
    return iterate + relax_weight * (source - section_apply(iterate, shift)) / diagonal


def precondition(source, context):
    operator, fine_diagonal, shift_cells, row_totals, layout = context
    iterate = relax_weight * source / fine_diagonal
    remainder = source - fine_apply(iterate, operator)
    size_x, size_y, width = source.shape
    sums = remainder.reshape(size_x, size_y, width // P_SIZE, P_SIZE).sum(axis=3)
    gathered, undo_list = assemble(
        jnp.stack([coarsen(sums) / float(P_SIZE), 0.125 * coarsen(shift_cells)]), 1, layout
    )
    coarse = section_cycle(gathered[0], gathered[1], 1, layout)
    correction = refine(unpick(coarse, undo_list))
    iterate = iterate + jnp.repeat(correction, P_SIZE, axis=2)
    update = source - fine_apply(iterate, operator)
    return iterate + relax_weight * update / fine_diagonal


def total(terms):
    return lax.psum(terms, ("gx", "gy", "gz"))


def per_device(right_side, element_class, class_blocks, class_shift, face_weights):
    size_x, size_y, width = right_side.shape
    size_z = width // P_SIZE
    classes = class_blocks.shape[0]
    element_count = size_x * size_y * size_z
    onehot = (
        element_class.reshape(element_count, 1) == jnp.arange(classes, dtype=jnp.int32)[None, :]
    ).astype(jnp.float32)
    wide_blocks = jnp.transpose(class_blocks, (2, 0, 1)).reshape(P_SIZE, classes * P_SIZE)
    operator = (onehot, wide_blocks, face_weights)
    diag_table = jnp.diagonal(class_blocks, axis1=1, axis2=2)
    fine_diagonal = jnp.dot(onehot, diag_table, precision=highest).reshape(size_x, size_y, width)
    shift_cells = jnp.dot(onehot, class_shift[:, None], precision=highest).reshape(
        size_x, size_y, size_z
    )
    row_totals = None
    bits_z = lax.axis_size("gz").bit_length() - 1
    bits_y = lax.axis_size("gy").bit_length() - 1
    layout = (
        (0, lax.axis_size("gx"), bits_z + bits_y, lax.axis_index("gx")),
        (1, lax.axis_size("gy"), bits_z, lax.axis_index("gy")),
        (2, lax.axis_size("gz"), 0, lax.axis_index("gz")),
    )
    context = (operator, fine_diagonal, shift_cells, row_totals, layout)
    residual = right_side
    smoothed = precondition(residual, context)
    gamma_now = total((jnp.sum(residual * smoothed),))[0]
    direction = smoothed
    image = fine_apply(direction, operator)
    step_size = gamma_now / total((jnp.sum(direction * image),))[0]
    solution_field = step_size * direction
    residual = residual - step_size * image
    smoothed = precondition(residual, context)
    gamma_next = total((jnp.sum(residual * smoothed),))[0]
    direction = smoothed + gamma_next / gamma_now * direction
    image = fine_apply(direction, operator)
    step_size = gamma_next / total((jnp.sum(direction * image),))[0]
    solution_field = solution_field + step_size * direction
    residual = residual - step_size * image
    return (solution_field, residual)


AXES = (2, 4, 4)
CELLS = 256
DEVICES = 32
MESSAGE = 384
NOTE_ROUNDS = 3
HALO_ROUNDS = 4
MESH = pl.DeviceIdType.MESH
f32 = jnp.float32


def iota(shape, dim):
    return lax.broadcasted_iota(jnp.int32, shape, dim)


def exact_dot(a, b, parts=2):
    a = a.astype(jnp.bfloat16)
    total_dot = None
    for _ in range(parts):
        part = b.astype(jnp.bfloat16)
        b = b - part.astype(f32)
        term = jnp.dot(a, part, preferred_element_type=f32)
        total_dot = term if total_dot is None else total_dot + term
    return total_dot


def neighbours(count, bits_y, bits_z, section_y, section_z):
    i, j = iota((count, count), 0), iota((count, count), 1)

    def split(k):
        return k >> bits_y + bits_z, k >> bits_z & (1 << bits_y) - 1, k & (1 << bits_z) - 1

    (xi, yi, zi), (xj, yj, zj) = split(i), split(j)
    apart = jnp.abs(xi - xj) + jnp.abs(yi - yj) + jnp.abs(zi - zj)
    same = ((yi >> section_y) == (yj >> section_y)) & ((zi >> section_z) == (zj >> section_z))
    return jnp.where((apart == 1) & same, 1.0, 0.0).astype(f32)


def coarse_matrix(shift_row, beside_1):
    i, j = iota((CELLS, CELLS), 0), iota((CELLS, CELLS), 1)
    eye = jnp.where(i == j, 1.0, 0.0).astype(f32)
    beside_2 = neighbours(32, 1, 3, 1, 3)
    j2, cell = iota((32, CELLS), 0), iota((32, CELLS), 1)
    parent = (cell >> 7) * 16 + (cell >> 5 & 1) * 8 + (cell >> 1 & 7)
    down_1 = jnp.where(parent == j2, 1.0, 0.0).astype(f32)
    ci, cj = iota((CELLS, 32), 0), iota((CELLS, 32), 1)
    up_1 = jnp.where((ci >> 7) * 16 + (ci >> 5 & 1) * 8 + (ci >> 1 & 7) == cj, 1.0, 0.0).astype(f32)
    j3, k3 = iota((8, 32), 0), iota((8, 32), 1)
    down_2 = jnp.where((k3 >> 1 & 3) == j3, 1.0, 0.0).astype(f32)
    k2, i2 = iota((32, 8), 0), iota((32, 8), 1)
    up_2 = jnp.where((k2 >> 1 & 3) == i2, 1.0, 0.0).astype(f32)
    d1_row = 6.0 + shift_row
    d1 = jnp.sum(eye * d1_row, axis=1, keepdims=True)
    d2 = 6.0 + 0.125 * jnp.sum(down_1 * shift_row, axis=1, keepdims=True)
    j3w, cellw = iota((8, CELLS), 0), iota((8, CELLS), 1)
    d3 = 6.0 + 0.015625 * jnp.sum(
        jnp.where((cellw >> 2 & 3) == j3w, shift_row, 0.0), axis=1, keepdims=True
    )
    q2 = 0.25 * exact_dot(down_1, 0.4 * eye + 0.6 * beside_1.astype(f32) / d1_row)
    x2 = 0.6 * q2 / d2
    q3 = 0.25 * exact_dot(down_2, 0.4 * q2 + exact_dot(beside_2, x2))
    x3 = 0.6 * q3 / d3
    row = iota((8, CELLS), 0)
    for _ in range(SWEEPS - 1):
        after = jnp.where(row < 3, pltpu.roll(x3, 7, 0), 0.0)
        before = jnp.where((row > 0) & (row < 4), pltpu.roll(x3, 1, 0), 0.0)
        x3 = 0.4 * x3 + 0.6 * (q3 + after + before) / d3
    x2 = x2 + exact_dot(up_2, x3)
    x2 = 0.4 * x2 + 0.6 * (q2 + exact_dot(beside_2, x2)) / d2
    x1 = 0.6 * eye / d1 + exact_dot(up_1, x2)
    return 0.4 * x1 + 0.6 * (eye + exact_dot(beside_1, x1)) / d1


def pick_cells(gx, gy, gz):
    rows = []
    s, cell = iota((8, CELLS), 0), iota((8, CELLS), 1)
    cx, cy, cz = cell >> 6, cell >> 4 & 3, cell & 15

    def pick(x, y, z):
        hit = (cx == ((gx * 4 + x) >> 1)) & (cy == ((gy * 2 + y) >> 1)) & (cz == gz * 4 + z)
        rows.append(jnp.where(hit, 1.0, 0.0).astype(f32))

    x, y = s >> 1, s & 1
    for dx, dy, zs in ((0, 0, range(-1, 5)), (1, 0, range(4)), (-1, 0, range(4)), (0, 1, range(4)), (0, -1, range(4))):
        for z in zs:
            pick(x + dx, y + dy, z)
    pairs = ((-1, y, s >> 1), (4, y, s >> 1))
    pairs += ((x, -1, 1 - y), (x, -1, 3 - y), (x, 2, y), (x, 2, y + 2), (x, y, -1), (x, y, 4))
    for gone_x, gone_y, gone_z in pairs:
        pick(gone_x, gone_y, gone_z)
        for dx, dy, dz in ((1, 0, 0), (-1, 0, 0), (0, 1, 0), (0, -1, 0), (0, 0, 1), (0, 0, -1)):
            pick(gone_x + dx, gone_y + dy, gone_z + dz)
    return jnp.concatenate(rows, axis=0)


def fused(
    r_hbm, class_hbm, blocks_hbm, shift_hbm, weight_hbm, out_ref,
    r_ref, class_ref, blocks_ref, shift_ref, weight_ref,
    halo_out, halo_in, note_out, note_in, w_ref, cells_ref, coarse_ref, pick_ref, beside_ref,
    load_sem, halo_send, halo_recv, note_send, note_recv,
):
    loads = (
        (blocks_hbm, blocks_ref), (r_hbm, r_ref), (class_hbm, class_ref),
        (shift_hbm, shift_ref), (weight_hbm, weight_ref),
    )
    loads = [pltpu.make_async_copy(a, b, load_sem.at[i]) for i, (a, b) in enumerate(loads)]
    for load in loads:
        load.start()
    gx, gy, gz = lax.axis_index("gx"), lax.axis_index("gy"), lax.axis_index("gz")

    me = gx * 16 + gy * 4 + gz
    ring_y = [gy] + [lax.rem(gy + k, 4) for k in range(1, 4)]
    ring_z = [gz] + [lax.rem(gz + k, 4) for k in range(1, 4)]
    others = [(x, y, z) for y in ring_y for x in (gx, 1 - gx) for z in ring_z][:0:-1]
    barrier = pltpu.get_barrier_semaphore()
    halo_in[...] = jnp.zeros_like(halo_in)
    for to in others:
        pl.semaphore_signal(barrier, inc=1, device_id=to, device_id_type=MESH)
    pick_ref[...] = pick_cells(gx, gy, gz).astype(jnp.bfloat16)
    beside_ref[...] = neighbours(CELLS, 2, 4, 1, 3).astype(jnp.bfloat16)

    for load in loads:
        load.wait()

    lane = iota((8, 128), 1)
    sub = iota((8, 128), 0)
    low = lane < 64
    ni, nj, nk = lane >> 4 & 3, lane >> 2 & 3, lane & 3
    weights = [weight_ref[d] for d in range(3)]
    upper = [jnp.where(n == 3, w, 0.0) for n, w in zip((ni, nj, nk), weights)]
    lower = [jnp.where(n == 0, w, 0.0) for n, w in zip((ni, nj, nk), weights)]

    def widen(blocks):
        out = []
        for j in range(4):
            turned = pltpu.roll(blocks[j], 64, 1)
            out += [jnp.where(low, blocks[j], turned), jnp.where(low, turned, blocks[j])]
        return out

    def halves(u):
        return [jnp.where(low, u[2 * j], u[2 * j + 1]) for j in range(4)]

    flat = jnp.concatenate([r_ref[x] for x in range(4)], axis=0)
    right = widen([flat[:, 128 * j : 128 * j + 128] for j in range(4)])
    marks = jnp.concatenate([class_ref[x] for x in range(4)], axis=0)
    mark = [jnp.broadcast_to(marks[:, z : z + 1], (8, 128)) for z in range(8)]

    def by_class(rows):
        out = [jnp.broadcast_to(rows[0], (8, 128)) for _ in range(8)]
        for k in range(1, 16):
            out = [jnp.where(here == k, rows[k], old) for here, old in zip(mark, out)]
        return out

    def twice(row):
        return jnp.concatenate([row, row], axis=1)

    eye = iota((64, 64), 0) == iota((64, 64), 1)
    diag_rows = [
        twice(jnp.sum(jnp.where(eye, blocks_ref[k], 0.0), axis=0, keepdims=True)) for k in range(16)
    ]
    diagonal = by_class(diag_rows)
    inverse = [1.0 / d for d in diagonal]

    def prepare():
        rows = []
        for k in range(16):
            rest = jnp.where(eye, 0.0, blocks_ref[k])
            rest_hi = rest.astype(jnp.bfloat16).astype(f32)
            both = jnp.concatenate([rest_hi, rest - rest_hi], axis=1)
            w_ref[64 * k : 64 * k + 64, :] = both.astype(jnp.bfloat16)
            rows.append(twice(jnp.sum(rest, axis=0, keepdims=True)) + diag_rows[k])
        return by_class(rows), by_class([shift_ref[k] for k in range(16)])

    own_cell = (sub >> 2) * 64 + gy * 16 + gz * 4

    def cell_row(columns, scale):
        row = jnp.zeros((8, 128), f32)
        for j in range(4):
            row = row + jnp.where(lane == own_cell + j, columns[j], 0.0)
        return scale * jnp.sum(row, axis=0, keepdims=True)

    note_lane = iota((1, 128), 1)

    def dots(*pairs):
        row = jnp.zeros((1, 128), f32)
        for at, (a, b) in enumerate(pairs):
            acc = a[0] * b[0]
            for z in range(1, 8):
                acc = acc + a[z] * b[z]
            acc = jnp.sum(jnp.sum(acc, axis=0, keepdims=True), axis=1, keepdims=True)
            row = row + jnp.where(note_lane == at, 0.5 * acc, 0.0)
        return row

    widths = (384, 384, 128)

    def note(ref, at, slot):
        return ref.at[at, slot, :, pl.ds(0, widths[at])]

    def tell(at, message):
        note_out[at, :, : widths[at]] = message
        note_in[at, me, :, : widths[at]] = message
        for to in others:
            pltpu.make_async_remote_copy(
                src_ref=note_out.at[at, :, pl.ds(0, widths[at])], dst_ref=note(note_in, at, me),
                send_sem=note_send.at[at], recv_sem=note_recv.at[at],
                device_id=to, device_id_type=MESH,
            ).start()

    def hear(at):
        span = note(note_in, at, pl.ds(0, DEVICES - 1))
        pltpu.make_async_copy(span, span, note_recv.at[at]).wait()
        return note_in[at, :, :, : widths[at]]

    def end_tell(at):
        span = note(note_in, at, pl.ds(0, DEVICES - 1))
        pltpu.make_async_copy(span, span, note_send.at[at]).wait()

    routes = (
        (0, 1, gx < AXES[0] - 1, gx > 0, (gx + 1, gy, gz)),
        (1, 1, gx > 0, gx < AXES[0] - 1, (gx - 1, gy, gz)),
        (2, 2, gy < AXES[1] - 1, gy > 0, (gx, gy + 1, gz)),
        (4, 2, gy > 0, gy < AXES[1] - 1, (gx, gy - 1, gz)),
        (6, 1, gz < AXES[2] - 1, gz > 0, (gx, gy, gz + 1)),
        (7, 1, gz > 0, gz < AXES[2] - 1, (gx, gy, gz - 1)),
    )

    def halo_copy(at, way):
        tile, count, _, _, to = routes[way]
        span = pl.ds(3 * tile, 3 * count if at == 1 else count)
        return pltpu.make_async_remote_copy(
            src_ref=halo_out.at[at, span], dst_ref=halo_in.at[at, span],
            send_sem=halo_send.at[at, way], recv_sem=halo_recv.at[at, way],
            device_id=to, device_id_type=MESH,
        )

    odd = (sub & 1) == 1

    places = [(0, 1, 0), (1, 1, 0), (2, 2, 0), (2, 2, 1), (4, 2, 0), (4, 2, 1), (6, 1, 0), (7, 1, 0)]

    def send_halo(at, *fields):
        for f, u in enumerate(fields):
            half = halves(u)
            up = jnp.where(sub >= 6, half[3], 0.0)
            down = jnp.where(sub < 2, half[0], 0.0)
            for m in range(3):
                up = jnp.where((sub >> 1) == m, pltpu.roll(half[m], (2 * m + 2) % 8, 0), up)
            for m in range(1, 4):
                down = jnp.where((sub >> 1) == m, pltpu.roll(half[m], 2 * m, 0), down)
            tiles = [up, down]
            tiles += [jnp.where(odd, half[2 * j], pltpu.roll(half[2 * j + 1], 7, 0)) for j in range(2)]
            tiles += [jnp.where(odd, pltpu.roll(half[2 * j + 1], 1, 0), half[2 * j]) for j in range(2)]
            tiles += [u[7], u[0]]
            for (tile, count, j), value in zip(places, tiles):
                halo_out[at, 3 * tile + f * count + j] = value
        for way in range(6):
            @pl.when(routes[way][2])
            def _():
                halo_copy(at, way).start()

    def ghosts(at, f=0):
        return [halo_in[at, 3 * tile + f * count + j] for tile, count, j in places]

    def wait_halo(at):
        for way in range(6):
            @pl.when(routes[way][3])
            def _():
                halo_copy(at, way).wait_recv()

    def end_halo(at):
        for way in range(6):
            @pl.when(routes[way][2])
            def _():
                halo_copy(at, way).wait_send()

    def turn(tile, by):
        return pltpu.roll(tile, by % 8, 0) if by % 8 else tile

    def unpack_x(packed, row):
        return widen([turn(packed, row - 2 * m) for m in range(4)])

    def local_part(u):
        top = jnp.concatenate(u, axis=0)
        top_hi = top.astype(jnp.bfloat16).astype(f32)
        top_lo = top - top_hi
        top = jnp.concatenate([top_hi, top_lo], axis=0)
        classes = jnp.concatenate(mark + mark, axis=0)
        kind = classes - (iota((128, 128), 1) >> 6)
        parts = [jnp.where(kind == 2 * p, top, 0.0).astype(jnp.bfloat16) for p in range(8)]
        out = jnp.dot(jnp.concatenate(parts, axis=1), w_ref[...], preferred_element_type=f32)
        out = out[:64] + out[64:]
        out = out + pltpu.roll(out, 64, 1)
        return [out[8 * z : 8 * z + 8] + diagonal[z] * u[z] for z in range(8)]

    def couple(u, got):
        x_before, x_after = unpack_x(got[0], 0), unpack_x(got[1], 6)
        y_before = widen([pltpu.roll(got[2], 7, 0), got[2], pltpu.roll(got[3], 7, 0), got[3]])
        y_after = widen([pltpu.roll(got[4], 1, 0), got[4], pltpu.roll(got[5], 1, 0), got[5]])
        out = []
        for z in range(8):
            x_next = jnp.where(sub >= 6, x_after[z], pltpu.roll(u[z], 6, 0))
            x_last = jnp.where(sub < 2, x_before[z], pltpu.roll(u[z], 2, 0))
            y_next = jnp.where(odd, y_after[z], pltpu.roll(u[z], 7, 0))
            y_last = jnp.where(odd, pltpu.roll(u[z], 1, 0), y_before[z])
            z_next = u[z + 1] if z < 7 else got[7]
            z_last = u[z - 1] if z > 0 else got[6]
            acc = upper[0] * pltpu.roll(x_next, 48, 1) + lower[0] * pltpu.roll(x_last, 80, 1)
            acc = acc + upper[1] * pltpu.roll(y_next, 12, 1) + lower[1] * pltpu.roll(y_last, 116, 1)
            acc = acc + upper[2] * pltpu.roll(z_next, 3, 1) + lower[2] * pltpu.roll(z_last, 125, 1)
            out.append(acc)
        return out

    def minus(a, b):
        return [p - q for p, q in zip(a, b)]

    def cell_message(w, v, totals):
        cell, s = iota((8, CELLS), 1), iota((8, CELLS), 0)

        def offset(dx, dy):
            x, y = (gx * 4 + (s >> 1) + dx) >> 1, (gy * 2 + (s & 1) + dy) >> 1
            inside = (x >= 0) & (x < 4) & (y >= 0) & (y < 4)
            return jnp.where(inside, cell - (x * 64 + y * 16 + gz * 4), 4096)

        def place(values, off, z):
            return jnp.where(off == z, jnp.sum(values, axis=1, keepdims=True), 0.0)

        pair = [0.6 * (v[2 * j] + v[2 * j + 1]) for j in range(4)]
        here = offset(0, 0)
        row = place(0.6 * lower[2] * v[0], here, jnp.where(gz > 0, -1, 8192))
        row = row + place(0.6 * upper[2] * v[7], here, jnp.where(gz < AXES[2] - 1, 4, 8192))
        for j in range(4):
            own = w[2 * j] + w[2 * j + 1] - 0.6 * (totals[2 * j] * v[2 * j] + totals[2 * j + 1] * v[2 * j + 1])
            to_next = v[2 * j] + v[2 * j - 1] if j > 0 else v[2 * j]
            to_last = v[2 * j + 1] + v[2 * j + 2] if j < 3 else v[2 * j + 1]
            row = row + place(own + 0.6 * (upper[2] * to_next + lower[2] * to_last), here, j)
        for d, up, down in ((0, offset(1, 0), offset(-1, 0)), (1, offset(0, 1), offset(0, -1))):
            for j in range(4):
                row = row + place(upper[d] * pair[j], up, j) + place(lower[d] * pair[j], down, j)
        return jnp.sum(row, axis=0, keepdims=True) * (1.0 / 128.0)

    def correct(picked, source, iterate, left, totals, at):
        tiles = [jnp.broadcast_to(picked[8 * t : 8 * t + 8], (8, 128)) for t in range(78)]
        own, x_up, x_down, y_up, y_down = tiles[:6], tiles[6:10], tiles[10:14], tiles[14:18], tiles[18:22]
        rest, scaled = [], []
        for z in range(8):
            j = z // 2
            image = totals[z] * own[j + 1]
            image = image - upper[0] * x_up[j] - lower[0] * x_down[j]
            image = image - upper[1] * y_up[j] - lower[1] * y_down[j]
            image = image - upper[2] * own[(z + 1) // 2 + 1] - lower[2] * own[(z - 1) // 2 + 1]
            rest.append(left[z] - image)
            scaled.append(rest[z] * inverse[z])
        own_part = local_part(scaled)
        wait_halo(at)
        got = []
        for g, (sent, inv, tot) in enumerate(zip(ghosts(at), ghosts(1, 1), ghosts(1, 2))):
            mid, xu, xd, yu, yd, zu, zd = tiles[22 + 7 * g : 29 + 7 * g]
            if g < 6:
                zu, zd = jnp.where(low, mid, zu), jnp.where(low, zd, mid)
            pull = upper[0] * xu + lower[0] * xd + upper[1] * yu + lower[1] * yd
            pull = pull + upper[2] * zu + lower[2] * zd
            got.append(sent - tot * mid + inv * pull)
        near = couple(scaled, got)
        result = [iterate[z] + own[z // 2 + 1] + 0.6 * scaled[z] for z in range(8)]
        image = [source[z] - rest[z] + 0.6 * (own_part[z] - near[z]) for z in range(8)]
        return result, image

    def scale(a, b):
        return [p * q for p, q in zip(a, b)]

    def remainder(source, own_part, iterate, at):
        wait_halo(at)
        return minus(source, minus(own_part, couple(iterate, ghosts(at))))

    totals, shifts = prepare()
    spread = scale(right, inverse)
    first = [0.6 * a for a in spread]
    columns = [(shifts[2 * j] + shifts[2 * j + 1])[:, :1] for j in range(4)]
    message = [cell_row(columns, 0.125), cell_message(right, spread, totals)]
    own_part = local_part(first)
    pl.semaphore_wait(barrier, DEVICES - 1)
    send_halo(0, first)
    tell(0, jnp.concatenate(message, axis=1))
    left = remainder(right, own_part, first, 0)
    send_halo(1, scale(left, inverse), inverse, scale(totals, inverse))
    heard = hear(0)
    shift_row = [jnp.sum(heard[:16, :, :128], axis=0), jnp.sum(heard[16:, :, :128], axis=0)]
    cells = jnp.sum(heard[:, :, 128:], axis=0)
    coarse = coarse_matrix(jnp.concatenate(shift_row, axis=1), beside_ref[...])
    coarse_ref[...] = coarse
    column = jnp.sum(coarse * cells, axis=1, keepdims=True)
    same = iota((CELLS, CELLS), 0) == iota((CELLS, CELLS), 1)
    row = jnp.sum(jnp.where(same, column, 0.0), axis=0, keepdims=True)
    picked = jnp.sum(pick_ref[...].astype(f32) * row, axis=1, keepdims=True)
    z0, w0 = correct(picked, right, first, left, totals, 1)

    spread = scale(w0, inverse)
    start = [0.6 * a for a in spread]
    send_halo(2, start)
    message = [cell_message(w0, spread, totals), dots((right, z0), (z0, w0))]
    tell(1, jnp.concatenate(message, axis=1))
    own_part = local_part(start)
    left = remainder(w0, own_part, start, 2)
    send_halo(3, scale(left, inverse))
    cells_ref[...] = exact_dot(pick_ref[...], coarse_ref[...], 3)
    heard = jnp.sum(hear(1), axis=0)
    gamma, curve = heard[:, CELLS : CELLS + 1], heard[:, CELLS + 1 : CELLS + 2]
    alpha = gamma / curve
    picked = jnp.sum(cells_ref[...] * heard[:, :CELLS], axis=1, keepdims=True)
    u, v = correct(picked, w0, start, left, totals, 3)
    z1 = [a - alpha * b for a, b in zip(z0, u)]
    w1 = [a - alpha * b for a, b in zip(w0, v)]
    r1 = [a - alpha * b for a, b in zip(right, w0)]
    tell(2, dots((r1, z1), (z1, w1), (z1, w0), (z0, w1)))
    for at in range(HALO_ROUNDS):
        end_halo(at)
    for at in range(2):
        end_tell(at)
    heard = jnp.sum(hear(2), axis=0)
    gamma_2 = heard[:, 0:1]
    beta = gamma_2 / gamma
    curve_2 = heard[:, 1:2] + beta * (heard[:, 2:3] + heard[:, 3:4]) + beta * beta * curve
    alpha_2 = gamma_2 / curve_2
    field = [alpha * a + alpha_2 * (b + beta * a) for a, b in zip(z0, z1)]
    rest = [a - alpha_2 * (b + beta * c) for a, b, c in zip(r1, w1, w0)]
    whole = jnp.concatenate(halves(field) + halves(rest), axis=1)
    for x in range(4):
        out_ref[x] = whole[2 * x : 2 * x + 2, :]
    end_tell(2)


def per_device_fused(right_side, element_class, class_blocks, class_shift, face_weights):
    vmem, hbm = pl.BlockSpec(memory_space=pltpu.VMEM), pl.BlockSpec(memory_space=pltpu.HBM)
    size_x, size_y, width = right_side.shape
    both = pl.pallas_call(
        fused,
        out_shape=jax.ShapeDtypeStruct((size_x, size_y, 2 * width), f32),
        in_specs=[hbm] * 5,
        out_specs=vmem,
        scratch_shapes=[
            pltpu.VMEM(right_side.shape, f32),
            pltpu.VMEM(element_class.shape, jnp.int32),
            pltpu.VMEM(class_blocks.shape, f32),
            pltpu.SMEM(class_shift.shape, f32),
            pltpu.SMEM(face_weights.shape, f32),
            pltpu.VMEM((HALO_ROUNDS, 24, 8, 128), f32),
            pltpu.VMEM((HALO_ROUNDS, 24, 8, 128), f32),
            pltpu.VMEM((NOTE_ROUNDS, 1, MESSAGE), f32),
            pltpu.VMEM((NOTE_ROUNDS, DEVICES, 1, MESSAGE), f32),
            pltpu.VMEM((1024, 128), jnp.bfloat16),
            pltpu.VMEM((624, CELLS), f32),
            pltpu.VMEM((CELLS, CELLS), f32),
            pltpu.VMEM((624, CELLS), jnp.bfloat16),
            pltpu.VMEM((CELLS, CELLS), jnp.bfloat16),
            pltpu.SemaphoreType.DMA((5,)),
            pltpu.SemaphoreType.DMA((HALO_ROUNDS, 6)),
            pltpu.SemaphoreType.DMA((HALO_ROUNDS, 6)),
            pltpu.SemaphoreType.DMA((NOTE_ROUNDS,)),
            pltpu.SemaphoreType.DMA((NOTE_ROUNDS,)),
        ],
        compiler_params=pltpu.CompilerParams(
            collective_id=0, has_side_effects=True
        ),
    )(right_side, element_class, class_blocks, class_shift, face_weights)
    return both[:, :, :width], both[:, :, width:]


def solution(mesh):
    in_specs = (P("gx", "gy", "gz"), P("gx", "gy", "gz"), P(), P(), P())
    out_specs = (P("gx", "gy", "gz"), P("gx", "gy", "gz"))
    small = tuple(mesh.shape[axis] for axis in ("gx", "gy", "gz")) == AXES
    body = per_device_fused if small else per_device
    return jax.shard_map(
        body, mesh=mesh, in_specs=in_specs, out_specs=out_specs, check_vma=False
    )
```

```python
import jax
import jax.numpy as jnp
import numpy as np
from jax import lax
from jax.experimental import pallas as pl
from jax.experimental.pallas import tpu as pltpu
from jax.sharding import PartitionSpec as P

P_SIZE = 64
SWEEPS = 4


highest = lax.Precision.HIGHEST
relax_weight = 0.6


def with_halo(x, sides, width):
    for axis, dim in sides:
        size, length = (lax.axis_size(axis), x.shape[dim])
        up = [(i, (i + 1) % size) for i in range(size - 1)]
        down = [(j, i) for i, j in up]
        last = lax.slice_in_dim(x, length - width, length, axis=dim)
        first = lax.slice_in_dim(x, 0, width, axis=dim)
        before = lax.ppermute(last, axis, up)
        after = lax.ppermute(first, axis, down)
        x = jnp.concatenate([before, x, after], axis=dim)
    return x


def partner_2(x, axis, bit):
    return lax.ppermute(x, axis, [(i, i ^ 1 << bit) for i in range(lax.axis_size(axis))])


def face_tables():
    node_ids = np.arange(P_SIZE)
    digits = (node_ids // 16, node_ids // 4 % 4, node_ids % 4)
    strides = (48, 12, 3)
    lower_sets = [node_ids[digits[axis_dim] == 0] for axis_dim in range(3)]
    return (lower_sets, strides)


def full_matrix(face_weights):
    lower_sets, strides = face_tables()
    pieces = []
    for axis_dim in range(3):
        lower_ids = lower_sets[axis_dim]
        upper_ids = lower_ids + strides[axis_dim]
        from_next = np.zeros((P_SIZE, P_SIZE), np.float32)
        from_next[lower_ids, upper_ids] = 1.0
        from_prev = np.zeros((P_SIZE, P_SIZE), np.float32)
        from_prev[upper_ids, lower_ids] = 1.0
        pieces.append(face_weights[axis_dim] * jnp.asarray(from_next))
        pieces.append(face_weights[axis_dim] * jnp.asarray(from_prev))
    return jnp.concatenate(pieces, axis=0)


def couple_full(cubes, face_weights):
    count = cubes.shape[0] * cubes.shape[1] * cubes.shape[2]
    padded = with_halo(cubes, (("gx", 0), ("gy", 1), ("gz", 2)), 1)
    views = [
        padded[2:, 1:-1, 1:-1],
        padded[:-2, 1:-1, 1:-1],
        padded[1:-1, 2:, 1:-1],
        padded[1:-1, :-2, 1:-1],
        padded[1:-1, 1:-1, 2:],
        padded[1:-1, 1:-1, :-2],
    ]
    stacked = jnp.concatenate(views, axis=3).reshape(count, 6 * P_SIZE)
    return jnp.dot(stacked, full_matrix(face_weights), precision=highest)


def coarsen(values):
    size_x, size_y, size_z = values.shape
    return values.reshape(size_x // 2, 2, size_y // 2, 2, size_z // 2, 2).sum(axis=(1, 3, 5))


def refine(values):
    return jnp.repeat(jnp.repeat(jnp.repeat(values, 2, axis=0), 2, axis=1), 2, axis=2)


def section_apply(values, shift):
    padded = jnp.pad(values, ((1, 1), (1, 1), (1, 1)))
    beside = padded[2:, 1:-1, 1:-1] + padded[:-2, 1:-1, 1:-1]
    beside = beside + padded[1:-1, 2:, 1:-1] + padded[1:-1, :-2, 1:-1]
    beside = beside + padded[1:-1, 1:-1, 2:] + padded[1:-1, 1:-1, :-2]
    return (6.0 + shift) * values - beside


def assemble(stacked, depth, layout):
    undo_list = []
    for axis_dim, axis_count, bit_offset, my_index in layout:
        if axis_count >= 2**depth:
            partner = partner_2(stacked, ("gx", "gy", "gz"), bit_offset + depth - 1)
            upper_half = my_index >> depth - 1 & 1 == 1
            half_size = stacked.shape[axis_dim + 1]
            low_first = jnp.concatenate([stacked, partner], axis_dim + 1)
            high_first = jnp.concatenate([partner, stacked], axis_dim + 1)
            stacked = jnp.where(upper_half, high_first, low_first)
            undo_list.append((axis_dim, upper_half, half_size))
    return (stacked, undo_list)


def unpick(values, undo_list):
    for axis_dim, upper_half, half_size in reversed(undo_list):
        values = lax.dynamic_slice_in_dim(
            values, upper_half.astype(jnp.int32) * half_size, half_size, axis_dim
        )
    return values


def fine_apply(field, operator):
    onehot, wide_blocks, face_weights = operator
    size_x, size_y, width = field.shape
    size_z = width // P_SIZE
    count = size_x * size_y * size_z
    classes = onehot.shape[1]
    flat = field.reshape(count, P_SIZE)
    products = jnp.dot(flat, wide_blocks, precision=highest).reshape(count, classes, P_SIZE)
    local_part = jnp.einsum("ekn,ek->en", products, onehot, precision=highest)
    cubes = field.reshape(size_x, size_y, size_z, P_SIZE)
    nearby = couple_full(cubes, face_weights)
    return (local_part - nearby).reshape(size_x, size_y, width)


def section_cycle(source, shift, depth, layout):
    diagonal = 6.0 + shift
    if depth == 3:
        iterate = jnp.zeros_like(source)
        for sweep_index in range(SWEEPS):
            iterate = iterate + relax_weight * (source - section_apply(iterate, shift)) / diagonal
        return iterate
    iterate = relax_weight * source / diagonal
    remainder = source - section_apply(iterate, shift)
    gathered, undo_list = assemble(
        jnp.stack([0.25 * coarsen(remainder), 0.125 * coarsen(shift)]), depth + 1, layout
    )
    coarse = section_cycle(gathered[0], gathered[1], depth + 1, layout)
    iterate = iterate + refine(unpick(coarse, undo_list))
    return iterate + relax_weight * (source - section_apply(iterate, shift)) / diagonal


def precondition(source, context):
    operator, fine_diagonal, shift_cells, row_totals, layout = context
    iterate = relax_weight * source / fine_diagonal
    remainder = source - fine_apply(iterate, operator)
    size_x, size_y, width = source.shape
    sums = remainder.reshape(size_x, size_y, width // P_SIZE, P_SIZE).sum(axis=3)
    gathered, undo_list = assemble(
        jnp.stack([coarsen(sums) / float(P_SIZE), 0.125 * coarsen(shift_cells)]), 1, layout
    )
    coarse = section_cycle(gathered[0], gathered[1], 1, layout)
    correction = refine(unpick(coarse, undo_list))
    iterate = iterate + jnp.repeat(correction, P_SIZE, axis=2)
    update = source - fine_apply(iterate, operator)
    return iterate + relax_weight * update / fine_diagonal


def total(terms):
    return lax.psum(terms, ("gx", "gy", "gz"))


def per_device(right_side, element_class, class_blocks, class_shift, face_weights):
    size_x, size_y, width = right_side.shape
    size_z = width // P_SIZE
    classes = class_blocks.shape[0]
    element_count = size_x * size_y * size_z
    onehot = (
        element_class.reshape(element_count, 1) == jnp.arange(classes, dtype=jnp.int32)[None, :]
    ).astype(jnp.float32)
    wide_blocks = jnp.transpose(class_blocks, (2, 0, 1)).reshape(P_SIZE, classes * P_SIZE)
    operator = (onehot, wide_blocks, face_weights)
    diag_table = jnp.diagonal(class_blocks, axis1=1, axis2=2)
    fine_diagonal = jnp.dot(onehot, diag_table, precision=highest).reshape(size_x, size_y, width)
    shift_cells = jnp.dot(onehot, class_shift[:, None], precision=highest).reshape(
        size_x, size_y, size_z
    )
    row_totals = None
    bits_z = lax.axis_size("gz").bit_length() - 1
    bits_y = lax.axis_size("gy").bit_length() - 1
    layout = (
        (0, lax.axis_size("gx"), bits_z + bits_y, lax.axis_index("gx")),
        (1, lax.axis_size("gy"), bits_z, lax.axis_index("gy")),
        (2, lax.axis_size("gz"), 0, lax.axis_index("gz")),
    )
    context = (operator, fine_diagonal, shift_cells, row_totals, layout)
    residual = right_side
    smoothed = precondition(residual, context)
    gamma_now = total((jnp.sum(residual * smoothed),))[0]
    direction = smoothed
    image = fine_apply(direction, operator)
    step_size = gamma_now / total((jnp.sum(direction * image),))[0]
    solution_field = step_size * direction
    residual = residual - step_size * image
    smoothed = precondition(residual, context)
    gamma_next = total((jnp.sum(residual * smoothed),))[0]
    direction = smoothed + gamma_next / gamma_now * direction
    image = fine_apply(direction, operator)
    step_size = gamma_next / total((jnp.sum(direction * image),))[0]
    solution_field = solution_field + step_size * direction
    residual = residual - step_size * image
    return (solution_field, residual)


AXES = (2, 4, 4)
CELLS = 256
DEVICES = 32
MESSAGE = 384
NOTE_ROUNDS = 3
HALO_ROUNDS = 4
MESH = pl.DeviceIdType.MESH
f32 = jnp.float32


def iota(shape, dim):
    return lax.broadcasted_iota(jnp.int32, shape, dim)


def exact_dot(a, b, parts=2):
    a = a.astype(jnp.bfloat16)
    total_dot = None
    for _ in range(parts):
        part = b.astype(jnp.bfloat16)
        b = b - part.astype(f32)
        term = jnp.dot(a, part, preferred_element_type=f32)
        total_dot = term if total_dot is None else total_dot + term
    return total_dot


def neighbours(count, bits_y, bits_z, section_y, section_z):
    i, j = iota((count, count), 0), iota((count, count), 1)

    def split(k):
        return k >> bits_y + bits_z, k >> bits_z & (1 << bits_y) - 1, k & (1 << bits_z) - 1

    (xi, yi, zi), (xj, yj, zj) = split(i), split(j)
    apart = jnp.abs(xi - xj) + jnp.abs(yi - yj) + jnp.abs(zi - zj)
    same = ((yi >> section_y) == (yj >> section_y)) & ((zi >> section_z) == (zj >> section_z))
    return jnp.where((apart == 1) & same, 1.0, 0.0).astype(f32)


def where_one(hit):
    return jnp.where(hit, 1.0, 0.0).astype(f32)


def coarse_constants():
    beside_1 = neighbours(CELLS, 2, 4, 1, 3)
    beside_2 = neighbours(32, 1, 3, 1, 3)
    j2, cell = iota((32, CELLS), 0), iota((32, CELLS), 1)
    down_1 = where_one((cell >> 7) * 16 + (cell >> 5 & 1) * 8 + (cell >> 1 & 7) == j2)
    ci, cj = iota((CELLS, 32), 0), iota((CELLS, 32), 1)
    up_1 = where_one((ci >> 7) * 16 + (ci >> 5 & 1) * 8 + (ci >> 1 & 7) == cj)
    j3, k3 = iota((8, 32), 0), iota((8, 32), 1)
    down_2 = where_one((k3 >> 1 & 3) == j3)
    k2, i2 = iota((32, 8), 0), iota((32, 8), 1)
    up_2 = where_one((k2 >> 1 & 3) == i2)
    return (
        beside_1, beside_2, down_1, exact_dot(down_1, beside_1, 1),
        jnp.concatenate([up_1, exact_dot(beside_1, up_1, 1)], axis=0),
        jnp.concatenate([down_2, exact_dot(down_2, beside_2, 1)], axis=1),
        jnp.concatenate([up_2, exact_dot(beside_2, up_2, 1)], axis=0),
    )


def coarse_matrix(shift_row, constants):
    beside_1, beside_2, down_1, down_beside_1, up_1, down_2, up_2 = constants
    i, j = iota((CELLS, CELLS), 0), iota((CELLS, CELLS), 1)
    eye = where_one(i == j)
    d1_row = 6.0 + shift_row
    d1 = jnp.sum(eye * d1_row, axis=1, keepdims=True)
    d2 = 6.0 + 0.125 * jnp.sum(down_1 * shift_row, axis=1, keepdims=True)
    j3w, cellw = iota((8, CELLS), 0), iota((8, CELLS), 1)
    d3 = 6.0 + 0.015625 * jnp.sum(
        jnp.where((cellw >> 2 & 3) == j3w, shift_row, 0.0), axis=1, keepdims=True
    )
    q2 = 0.1 * down_1 + 0.15 * down_beside_1 / d1_row
    x2 = 0.6 * q2 / d2
    q3 = 0.25 * exact_dot(down_2, jnp.concatenate([0.4 * q2, x2], axis=0))
    beside_x2 = exact_dot(beside_2, x2)
    x3 = 0.6 * q3 / d3
    row = iota((8, CELLS), 0)
    for _ in range(SWEEPS - 1):
        after = jnp.where(row < 3, pltpu.roll(x3, 7, 0), 0.0)
        before = jnp.where((row > 0) & (row < 4), pltpu.roll(x3, 1, 0), 0.0)
        x3 = 0.4 * x3 + 0.6 * (q3 + after + before) / d3
    fine = exact_dot(up_2, x3)
    x2 = 0.4 * (x2 + fine[:32]) + 0.6 * (q2 + beside_x2 + fine[32:]) / d2
    fine = exact_dot(up_1, x2)
    x1 = 0.6 * eye / d1 + fine[:CELLS]
    beside_x1 = 0.6 * beside_1 / d1_row + fine[CELLS:]
    return 0.4 * x1 + 0.6 * (eye + beside_x1) / d1


def pick_cells(gx, gy, gz):
    rows = []
    s, cell = iota((8, CELLS), 0), iota((8, CELLS), 1)
    cx, cy, cz = cell >> 6, cell >> 4 & 3, cell & 15

    def pick(x, y, z):
        hit = (cx == ((gx * 4 + x) >> 1)) & (cy == ((gy * 2 + y) >> 1)) & (cz == gz * 4 + z)
        rows.append(jnp.where(hit, 1.0, 0.0).astype(f32))

    x, y = s >> 1, s & 1
    for dx, dy, zs in ((0, 0, range(-1, 5)), (1, 0, range(4)), (-1, 0, range(4)), (0, 1, range(4)), (0, -1, range(4))):
        for z in zs:
            pick(x + dx, y + dy, z)
    pairs = ((-1, y, s >> 1), (4, y, s >> 1))
    pairs += ((x, -1, 1 - y), (x, -1, 3 - y), (x, 2, y), (x, 2, y + 2), (x, y, -1), (x, y, 4))
    for gone_x, gone_y, gone_z in pairs:
        pick(gone_x, gone_y, gone_z)
        for dx, dy, dz in ((1, 0, 0), (-1, 0, 0), (0, 1, 0), (0, -1, 0), (0, 0, 1), (0, 0, -1)):
            pick(gone_x + dx, gone_y + dy, gone_z + dz)
    return jnp.concatenate(rows, axis=0)


def fused(
    r_hbm, class_hbm, blocks_hbm, shift_hbm, weight_hbm, out_ref,
    r_ref, class_ref, blocks_ref, shift_ref, weight_ref,
    halo_out, halo_in, note_out, note_in, w_ref, cells_ref, coarse_ref, pick_ref,
    load_sem, halo_send, halo_recv, note_send, note_recv, *const_refs,
):
    loads = (
        (blocks_hbm, blocks_ref), (r_hbm, r_ref), (class_hbm, class_ref),
        (shift_hbm, shift_ref), (weight_hbm, weight_ref),
    )
    loads = [pltpu.make_async_copy(a, b, load_sem.at[i]) for i, (a, b) in enumerate(loads)]
    for load in loads:
        load.start()
    gx, gy, gz = lax.axis_index("gx"), lax.axis_index("gy"), lax.axis_index("gz")

    me = gx * 16 + gy * 4 + gz
    ring_y = [gy] + [lax.rem(gy + k, 4) for k in range(1, 4)]
    ring_z = [gz] + [lax.rem(gz + k, 4) for k in range(1, 4)]
    others = [(x, y, z) for y in ring_y for x in (gx, 1 - gx) for z in ring_z][:0:-1]
    barrier = pltpu.get_barrier_semaphore()
    halo_in[...] = jnp.zeros_like(halo_in)
    for to in others:
        pl.semaphore_signal(barrier, inc=1, device_id=to, device_id_type=MESH)
    pick_ref[...] = pick_cells(gx, gy, gz).astype(jnp.bfloat16)
    for ref, value in zip(const_refs, coarse_constants()):
        ref[...] = value

    for load in loads:
        load.wait()

    lane = iota((8, 128), 1)
    sub = iota((8, 128), 0)
    low = lane < 64
    ni, nj, nk = lane >> 4 & 3, lane >> 2 & 3, lane & 3
    weights = [weight_ref[d] for d in range(3)]
    upper = [jnp.where(n == 3, w, 0.0) for n, w in zip((ni, nj, nk), weights)]
    lower = [jnp.where(n == 0, w, 0.0) for n, w in zip((ni, nj, nk), weights)]

    def widen(blocks):
        out = []
        for j in range(4):
            turned = pltpu.roll(blocks[j], 64, 1)
            out += [jnp.where(low, blocks[j], turned), jnp.where(low, turned, blocks[j])]
        return out

    def halves(u):
        return [jnp.where(low, u[2 * j], u[2 * j + 1]) for j in range(4)]

    flat = jnp.concatenate([r_ref[x] for x in range(4)], axis=0)
    right = widen([flat[:, 128 * j : 128 * j + 128] for j in range(4)])
    marks = jnp.concatenate([class_ref[x] for x in range(4)], axis=0)
    mark = [jnp.broadcast_to(marks[:, z : z + 1], (8, 128)) for z in range(8)]

    def by_class(rows):
        out = [jnp.broadcast_to(rows[0], (8, 128)) for _ in range(8)]
        for k in range(1, 16):
            out = [jnp.where(here == k, rows[k], old) for here, old in zip(mark, out)]
        return out

    def twice(row):
        return jnp.concatenate([row, row], axis=1)

    eye = iota((64, 64), 0) == iota((64, 64), 1)
    diag_rows = [
        twice(jnp.sum(jnp.where(eye, blocks_ref[k], 0.0), axis=0, keepdims=True)) for k in range(16)
    ]
    diagonal = by_class(diag_rows)
    inverse = [1.0 / d for d in diagonal]

    totals = by_class([twice(jnp.sum(blocks_ref[k], axis=0, keepdims=True)) for k in range(16)])
    shifts = by_class([shift_ref[k] for k in range(16)])

    def split_blocks():
        for k in range(16):
            rest = jnp.where(eye, 0.0, blocks_ref[k])
            rest_hi = rest.astype(jnp.bfloat16).astype(f32)
            both = jnp.concatenate([rest_hi, rest - rest_hi], axis=1)
            w_ref[64 * k : 64 * k + 64, :] = both.astype(jnp.bfloat16)

    own_cell = (sub >> 2) * 64 + gy * 16 + gz * 4

    def cell_row(columns, scale):
        row = jnp.zeros((8, 128), f32)
        for j in range(4):
            row = row + jnp.where(lane == own_cell + j, columns[j], 0.0)
        return scale * jnp.sum(row, axis=0, keepdims=True)

    note_lane = iota((1, 128), 1)

    def dots(*pairs):
        row = jnp.zeros((1, 128), f32)
        for at, (a, b) in enumerate(pairs):
            acc = a[0] * b[0]
            for z in range(1, 8):
                acc = acc + a[z] * b[z]
            acc = jnp.sum(jnp.sum(acc, axis=0, keepdims=True), axis=1, keepdims=True)
            row = row + jnp.where(note_lane == at, 0.5 * acc, 0.0)
        return row

    widths = (384, 384, 128)

    def note(ref, at, slot):
        return ref.at[at, slot, :, pl.ds(0, widths[at])]

    def tell(at, message):
        note_out[at, :, : widths[at]] = message
        note_in[at, me, :, : widths[at]] = message
        for to in others:
            pltpu.make_async_remote_copy(
                src_ref=note_out.at[at, :, pl.ds(0, widths[at])], dst_ref=note(note_in, at, me),
                send_sem=note_send.at[at], recv_sem=note_recv.at[at],
                device_id=to, device_id_type=MESH,
            ).start()

    def hear(at):
        span = note(note_in, at, pl.ds(0, DEVICES - 1))
        pltpu.make_async_copy(span, span, note_recv.at[at]).wait()
        return note_in[at, :, :, : widths[at]]

    def end_tell(at):
        span = note(note_in, at, pl.ds(0, DEVICES - 1))
        pltpu.make_async_copy(span, span, note_send.at[at]).wait()

    routes = (
        (0, 1, gx < AXES[0] - 1, gx > 0, (gx + 1, gy, gz)),
        (1, 1, gx > 0, gx < AXES[0] - 1, (gx - 1, gy, gz)),
        (2, 2, gy < AXES[1] - 1, gy > 0, (gx, gy + 1, gz)),
        (4, 2, gy > 0, gy < AXES[1] - 1, (gx, gy - 1, gz)),
        (6, 1, gz < AXES[2] - 1, gz > 0, (gx, gy, gz + 1)),
        (7, 1, gz > 0, gz < AXES[2] - 1, (gx, gy, gz - 1)),
    )

    def halo_copy(at, way):
        tile, count, _, _, to = routes[way]
        span = pl.ds(3 * tile, 3 * count if at == 1 else count)
        return pltpu.make_async_remote_copy(
            src_ref=halo_out.at[at, span], dst_ref=halo_in.at[at, span],
            send_sem=halo_send.at[at, way], recv_sem=halo_recv.at[at, way],
            device_id=to, device_id_type=MESH,
        )

    odd = (sub & 1) == 1

    places = [(0, 1, 0), (1, 1, 0), (2, 2, 0), (2, 2, 1), (4, 2, 0), (4, 2, 1), (6, 1, 0), (7, 1, 0)]

    def send_halo(at, *fields):
        for f, u in enumerate(fields):
            half = halves(u)
            up = jnp.where(sub >= 6, half[3], 0.0)
            down = jnp.where(sub < 2, half[0], 0.0)
            for m in range(3):
                up = jnp.where((sub >> 1) == m, pltpu.roll(half[m], (2 * m + 2) % 8, 0), up)
            for m in range(1, 4):
                down = jnp.where((sub >> 1) == m, pltpu.roll(half[m], 2 * m, 0), down)
            tiles = [up, down]
            tiles += [jnp.where(odd, half[2 * j], pltpu.roll(half[2 * j + 1], 7, 0)) for j in range(2)]
            tiles += [jnp.where(odd, pltpu.roll(half[2 * j + 1], 1, 0), half[2 * j]) for j in range(2)]
            tiles += [u[7], u[0]]
            for (tile, count, j), value in zip(places, tiles):
                halo_out[at, 3 * tile + f * count + j] = value
        for way in range(6):
            @pl.when(routes[way][2])
            def _():
                halo_copy(at, way).start()

    def ghosts(at, f=0):
        return [halo_in[at, 3 * tile + f * count + j] for tile, count, j in places]

    def wait_halo(at):
        for way in range(6):
            @pl.when(routes[way][3])
            def _():
                halo_copy(at, way).wait_recv()

    def end_halo(at):
        for way in range(6):
            @pl.when(routes[way][2])
            def _():
                halo_copy(at, way).wait_send()

    def turn(tile, by):
        return pltpu.roll(tile, by % 8, 0) if by % 8 else tile

    def unpack_x(packed, row):
        return widen([turn(packed, row - 2 * m) for m in range(4)])

    def local_part(u):
        top = jnp.concatenate(u, axis=0)
        top_hi = top.astype(jnp.bfloat16).astype(f32)
        top_lo = top - top_hi
        top = jnp.concatenate([top_hi, top_lo], axis=0)
        classes = jnp.concatenate(mark + mark, axis=0)
        kind = classes - (iota((128, 128), 1) >> 6)
        parts = [jnp.where(kind == 2 * p, top, 0.0).astype(jnp.bfloat16) for p in range(8)]
        out = jnp.dot(jnp.concatenate(parts, axis=1), w_ref[...], preferred_element_type=f32)
        out = out[:64] + out[64:]
        out = out + pltpu.roll(out, 64, 1)
        return [out[8 * z : 8 * z + 8] + diagonal[z] * u[z] for z in range(8)]

    def couple(u, got):
        x_before, x_after = unpack_x(got[0], 0), unpack_x(got[1], 6)
        y_before = widen([pltpu.roll(got[2], 7, 0), got[2], pltpu.roll(got[3], 7, 0), got[3]])
        y_after = widen([pltpu.roll(got[4], 1, 0), got[4], pltpu.roll(got[5], 1, 0), got[5]])
        out = []
        for z in range(8):
            x_next = jnp.where(sub >= 6, x_after[z], pltpu.roll(u[z], 6, 0))
            x_last = jnp.where(sub < 2, x_before[z], pltpu.roll(u[z], 2, 0))
            y_next = jnp.where(odd, y_after[z], pltpu.roll(u[z], 7, 0))
            y_last = jnp.where(odd, pltpu.roll(u[z], 1, 0), y_before[z])
            z_next = u[z + 1] if z < 7 else got[7]
            z_last = u[z - 1] if z > 0 else got[6]
            acc = upper[0] * pltpu.roll(x_next, 48, 1) + lower[0] * pltpu.roll(x_last, 80, 1)
            acc = acc + upper[1] * pltpu.roll(y_next, 12, 1) + lower[1] * pltpu.roll(y_last, 116, 1)
            acc = acc + upper[2] * pltpu.roll(z_next, 3, 1) + lower[2] * pltpu.roll(z_last, 125, 1)
            out.append(acc)
        return out

    def minus(a, b):
        return [p - q for p, q in zip(a, b)]

    def cell_message(w, v, totals):
        cell, s = iota((8, CELLS), 1), iota((8, CELLS), 0)

        def offset(dx, dy):
            x, y = (gx * 4 + (s >> 1) + dx) >> 1, (gy * 2 + (s & 1) + dy) >> 1
            inside = (x >= 0) & (x < 4) & (y >= 0) & (y < 4)
            return jnp.where(inside, cell - (x * 64 + y * 16 + gz * 4), 4096)

        def place(values, off, z):
            return jnp.where(off == z, jnp.sum(values, axis=1, keepdims=True), 0.0)

        pair = [0.6 * (v[2 * j] + v[2 * j + 1]) for j in range(4)]
        here = offset(0, 0)
        row = place(0.6 * lower[2] * v[0], here, jnp.where(gz > 0, -1, 8192))
        row = row + place(0.6 * upper[2] * v[7], here, jnp.where(gz < AXES[2] - 1, 4, 8192))
        for j in range(4):
            own = w[2 * j] + w[2 * j + 1] - 0.6 * (totals[2 * j] * v[2 * j] + totals[2 * j + 1] * v[2 * j + 1])
            to_next = v[2 * j] + v[2 * j - 1] if j > 0 else v[2 * j]
            to_last = v[2 * j + 1] + v[2 * j + 2] if j < 3 else v[2 * j + 1]
            row = row + place(own + 0.6 * (upper[2] * to_next + lower[2] * to_last), here, j)
        for d, up, down in ((0, offset(1, 0), offset(-1, 0)), (1, offset(0, 1), offset(0, -1))):
            for j in range(4):
                row = row + place(upper[d] * pair[j], up, j) + place(lower[d] * pair[j], down, j)
        return jnp.sum(row, axis=0, keepdims=True) * (1.0 / 128.0)

    def correct(picked, source, iterate, left, totals, at):
        tiles = [jnp.broadcast_to(picked[8 * t : 8 * t + 8], (8, 128)) for t in range(78)]
        own, x_up, x_down, y_up, y_down = tiles[:6], tiles[6:10], tiles[10:14], tiles[14:18], tiles[18:22]
        rest, scaled = [], []
        for z in range(8):
            j = z // 2
            image = totals[z] * own[j + 1]
            image = image - upper[0] * x_up[j] - lower[0] * x_down[j]
            image = image - upper[1] * y_up[j] - lower[1] * y_down[j]
            image = image - upper[2] * own[(z + 1) // 2 + 1] - lower[2] * own[(z - 1) // 2 + 1]
            rest.append(left[z] - image)
            scaled.append(rest[z] * inverse[z])
        own_part = local_part(scaled)
        wait_halo(at)
        got = []
        for g, (sent, inv, tot) in enumerate(zip(ghosts(at), ghosts(1, 1), ghosts(1, 2))):
            mid, xu, xd, yu, yd, zu, zd = tiles[22 + 7 * g : 29 + 7 * g]
            if g < 6:
                zu, zd = jnp.where(low, mid, zu), jnp.where(low, zd, mid)
            pull = upper[0] * xu + lower[0] * xd + upper[1] * yu + lower[1] * yd
            pull = pull + upper[2] * zu + lower[2] * zd
            got.append(sent - tot * mid + inv * pull)
        near = couple(scaled, got)
        result = [iterate[z] + own[z // 2 + 1] + 0.6 * scaled[z] for z in range(8)]
        image = [source[z] - rest[z] + 0.6 * (own_part[z] - near[z]) for z in range(8)]
        return result, image

    def scale(a, b):
        return [p * q for p, q in zip(a, b)]

    def remainder(source, own_part, iterate, at):
        wait_halo(at)
        return minus(source, minus(own_part, couple(iterate, ghosts(at))))

    spread = scale(right, inverse)
    first = [0.6 * a for a in spread]
    columns = [(shifts[2 * j] + shifts[2 * j + 1])[:, :1] for j in range(4)]
    message = [cell_row(columns, 0.125), cell_message(right, spread, totals)]
    pl.semaphore_wait(barrier, DEVICES - 1)
    send_halo(0, first)
    tell(0, jnp.concatenate(message, axis=1))
    split_blocks()
    own_part = local_part(first)
    left = remainder(right, own_part, first, 0)
    send_halo(1, scale(left, inverse), inverse, scale(totals, inverse))
    heard = hear(0)
    shift_row = [jnp.sum(heard[:16, :, :128], axis=0), jnp.sum(heard[16:, :, :128], axis=0)]
    cells = jnp.sum(heard[:, :, 128:], axis=0)
    same = iota((CELLS, CELLS), 0) == iota((CELLS, CELLS), 1)
    column = jnp.sum(jnp.where(same, cells, 0.0), axis=1, keepdims=True)
    coarse = coarse_matrix(jnp.concatenate(shift_row, axis=1), [ref[...] for ref in const_refs])
    coarse_ref[...] = coarse
    row = jnp.sum(coarse * column, axis=0, keepdims=True)
    picked = jnp.sum(pick_ref[...].astype(f32) * row, axis=1, keepdims=True)
    z0, w0 = correct(picked, right, first, left, totals, 1)

    spread = scale(w0, inverse)
    start = [0.6 * a for a in spread]
    send_halo(2, start)
    message = [cell_message(w0, spread, totals), dots((right, z0), (z0, w0))]
    tell(1, jnp.concatenate(message, axis=1))
    own_part = local_part(start)
    left = remainder(w0, own_part, start, 2)
    send_halo(3, scale(left, inverse))
    cells_ref[...] = exact_dot(pick_ref[...], coarse_ref[...], 3)
    heard = jnp.sum(hear(1), axis=0)
    gamma, curve = heard[:, CELLS : CELLS + 1], heard[:, CELLS + 1 : CELLS + 2]
    alpha = gamma / curve
    picked = jnp.sum(cells_ref[...] * heard[:, :CELLS], axis=1, keepdims=True)
    u, v = correct(picked, w0, start, left, totals, 3)
    z1 = [a - alpha * b for a, b in zip(z0, u)]
    w1 = [a - alpha * b for a, b in zip(w0, v)]
    r1 = [a - alpha * b for a, b in zip(right, w0)]
    tell(2, dots((r1, z1), (z1, w1), (z1, w0), (z0, w1)))
    for at in range(HALO_ROUNDS):
        end_halo(at)
    for at in range(2):
        end_tell(at)
    heard = jnp.sum(hear(2), axis=0)
    gamma_2 = heard[:, 0:1]
    beta = gamma_2 / gamma
    curve_2 = heard[:, 1:2] + beta * (heard[:, 2:3] + heard[:, 3:4]) + beta * beta * curve
    alpha_2 = gamma_2 / curve_2
    field = [alpha * a + alpha_2 * (b + beta * a) for a, b in zip(z0, z1)]
    rest = [a - alpha_2 * (b + beta * c) for a, b, c in zip(r1, w1, w0)]
    whole = jnp.concatenate(halves(field) + halves(rest), axis=1)
    for x in range(4):
        out_ref[x] = whole[2 * x : 2 * x + 2, :]
    end_tell(2)


def per_device_fused(right_side, element_class, class_blocks, class_shift, face_weights):
    vmem, hbm = pl.BlockSpec(memory_space=pltpu.VMEM), pl.BlockSpec(memory_space=pltpu.HBM)
    size_x, size_y, width = right_side.shape
    both = pl.pallas_call(
        fused,
        out_shape=jax.ShapeDtypeStruct((size_x, size_y, 2 * width), f32),
        in_specs=[hbm] * 5,
        out_specs=vmem,
        scratch_shapes=[
            pltpu.VMEM(right_side.shape, f32),
            pltpu.VMEM(element_class.shape, jnp.int32),
            pltpu.VMEM(class_blocks.shape, f32),
            pltpu.SMEM(class_shift.shape, f32),
            pltpu.SMEM(face_weights.shape, f32),
            pltpu.VMEM((HALO_ROUNDS, 24, 8, 128), f32),
            pltpu.VMEM((HALO_ROUNDS, 24, 8, 128), f32),
            pltpu.VMEM((NOTE_ROUNDS, 1, MESSAGE), f32),
            pltpu.VMEM((NOTE_ROUNDS, DEVICES, 1, MESSAGE), f32),
            pltpu.VMEM((1024, 128), jnp.bfloat16),
            pltpu.VMEM((624, CELLS), f32),
            pltpu.VMEM((CELLS, CELLS), f32),
            pltpu.VMEM((624, CELLS), jnp.bfloat16),
            pltpu.SemaphoreType.DMA((5,)),
            pltpu.SemaphoreType.DMA((HALO_ROUNDS, 6)),
            pltpu.SemaphoreType.DMA((HALO_ROUNDS, 6)),
            pltpu.SemaphoreType.DMA((NOTE_ROUNDS,)),
            pltpu.SemaphoreType.DMA((NOTE_ROUNDS,)),
            pltpu.VMEM((CELLS, CELLS), f32),
            pltpu.VMEM((32, 32), f32),
            pltpu.VMEM((32, CELLS), f32),
            pltpu.VMEM((32, CELLS), f32),
            pltpu.VMEM((2 * CELLS, 32), f32),
            pltpu.VMEM((8, 64), f32),
            pltpu.VMEM((64, 8), f32),
        ],
        compiler_params=pltpu.CompilerParams(
            collective_id=0, has_side_effects=True
        ),
    )(right_side, element_class, class_blocks, class_shift, face_weights)
    return both[:, :, :width], both[:, :, width:]


def solution(mesh):
    in_specs = (P("gx", "gy", "gz"), P("gx", "gy", "gz"), P(), P(), P())
    out_specs = (P("gx", "gy", "gz"), P("gx", "gy", "gz"))
    small = tuple(mesh.shape[axis] for axis in ("gx", "gy", "gz")) == AXES
    body = per_device_fused if small else per_device
    return jax.shard_map(
        body, mesh=mesh, in_specs=in_specs, out_specs=out_specs, check_vma=False
    )
```

```python
import jax
import jax.numpy as jnp
import numpy as np
from jax import lax
from jax.experimental import pallas as pl
from jax.experimental.pallas import tpu as pltpu
from jax.sharding import PartitionSpec as P

P_SIZE = 64
SWEEPS = 4


highest = lax.Precision.HIGHEST
relax_weight = 0.6


def with_halo(x, sides, width):
    for axis, dim in sides:
        size, length = (lax.axis_size(axis), x.shape[dim])
        up = [(i, (i + 1) % size) for i in range(size - 1)]
        down = [(j, i) for i, j in up]
        last = lax.slice_in_dim(x, length - width, length, axis=dim)
        first = lax.slice_in_dim(x, 0, width, axis=dim)
        before = lax.ppermute(last, axis, up)
        after = lax.ppermute(first, axis, down)
        x = jnp.concatenate([before, x, after], axis=dim)
    return x


def partner_2(x, axis, bit):
    return lax.ppermute(x, axis, [(i, i ^ 1 << bit) for i in range(lax.axis_size(axis))])


def face_tables():
    node_ids = np.arange(P_SIZE)
    digits = (node_ids // 16, node_ids // 4 % 4, node_ids % 4)
    strides = (48, 12, 3)
    lower_sets = [node_ids[digits[axis_dim] == 0] for axis_dim in range(3)]
    return (lower_sets, strides)


def full_matrix(face_weights):
    lower_sets, strides = face_tables()
    pieces = []
    for axis_dim in range(3):
        lower_ids = lower_sets[axis_dim]
        upper_ids = lower_ids + strides[axis_dim]
        from_next = np.zeros((P_SIZE, P_SIZE), np.float32)
        from_next[lower_ids, upper_ids] = 1.0
        from_prev = np.zeros((P_SIZE, P_SIZE), np.float32)
        from_prev[upper_ids, lower_ids] = 1.0
        pieces.append(face_weights[axis_dim] * jnp.asarray(from_next))
        pieces.append(face_weights[axis_dim] * jnp.asarray(from_prev))
    return jnp.concatenate(pieces, axis=0)


def couple_full(cubes, face_weights):
    count = cubes.shape[0] * cubes.shape[1] * cubes.shape[2]
    padded = with_halo(cubes, (("gx", 0), ("gy", 1), ("gz", 2)), 1)
    views = [
        padded[2:, 1:-1, 1:-1],
        padded[:-2, 1:-1, 1:-1],
        padded[1:-1, 2:, 1:-1],
        padded[1:-1, :-2, 1:-1],
        padded[1:-1, 1:-1, 2:],
        padded[1:-1, 1:-1, :-2],
    ]
    stacked = jnp.concatenate(views, axis=3).reshape(count, 6 * P_SIZE)
    return jnp.dot(stacked, full_matrix(face_weights), precision=highest)


def coarsen(values):
    size_x, size_y, size_z = values.shape
    return values.reshape(size_x // 2, 2, size_y // 2, 2, size_z // 2, 2).sum(axis=(1, 3, 5))


def refine(values):
    return jnp.repeat(jnp.repeat(jnp.repeat(values, 2, axis=0), 2, axis=1), 2, axis=2)


def section_apply(values, shift):
    padded = jnp.pad(values, ((1, 1), (1, 1), (1, 1)))
    beside = padded[2:, 1:-1, 1:-1] + padded[:-2, 1:-1, 1:-1]
    beside = beside + padded[1:-1, 2:, 1:-1] + padded[1:-1, :-2, 1:-1]
    beside = beside + padded[1:-1, 1:-1, 2:] + padded[1:-1, 1:-1, :-2]
    return (6.0 + shift) * values - beside


def assemble(stacked, depth, layout):
    undo_list = []
    for axis_dim, axis_count, bit_offset, my_index in layout:
        if axis_count >= 2**depth:
            partner = partner_2(stacked, ("gx", "gy", "gz"), bit_offset + depth - 1)
            upper_half = my_index >> depth - 1 & 1 == 1
            half_size = stacked.shape[axis_dim + 1]
            low_first = jnp.concatenate([stacked, partner], axis_dim + 1)
            high_first = jnp.concatenate([partner, stacked], axis_dim + 1)
            stacked = jnp.where(upper_half, high_first, low_first)
            undo_list.append((axis_dim, upper_half, half_size))
    return (stacked, undo_list)


def unpick(values, undo_list):
    for axis_dim, upper_half, half_size in reversed(undo_list):
        values = lax.dynamic_slice_in_dim(
            values, upper_half.astype(jnp.int32) * half_size, half_size, axis_dim
        )
    return values


def fine_apply(field, operator):
    onehot, wide_blocks, face_weights = operator
    size_x, size_y, width = field.shape
    size_z = width // P_SIZE
    count = size_x * size_y * size_z
    classes = onehot.shape[1]
    flat = field.reshape(count, P_SIZE)
    products = jnp.dot(flat, wide_blocks, precision=highest).reshape(count, classes, P_SIZE)
    local_part = jnp.einsum("ekn,ek->en", products, onehot, precision=highest)
    cubes = field.reshape(size_x, size_y, size_z, P_SIZE)
    nearby = couple_full(cubes, face_weights)
    return (local_part - nearby).reshape(size_x, size_y, width)


def section_cycle(source, shift, depth, layout):
    diagonal = 6.0 + shift
    if depth == 3:
        iterate = jnp.zeros_like(source)
        for sweep_index in range(SWEEPS):
            iterate = iterate + relax_weight * (source - section_apply(iterate, shift)) / diagonal
        return iterate
    iterate = relax_weight * source / diagonal
    remainder = source - section_apply(iterate, shift)
    gathered, undo_list = assemble(
        jnp.stack([0.25 * coarsen(remainder), 0.125 * coarsen(shift)]), depth + 1, layout
    )
    coarse = section_cycle(gathered[0], gathered[1], depth + 1, layout)
    iterate = iterate + refine(unpick(coarse, undo_list))
    return iterate + relax_weight * (source - section_apply(iterate, shift)) / diagonal


def precondition(source, context):
    operator, fine_diagonal, shift_cells, row_totals, layout = context
    iterate = relax_weight * source / fine_diagonal
    remainder = source - fine_apply(iterate, operator)
    size_x, size_y, width = source.shape
    sums = remainder.reshape(size_x, size_y, width // P_SIZE, P_SIZE).sum(axis=3)
    gathered, undo_list = assemble(
        jnp.stack([coarsen(sums) / float(P_SIZE), 0.125 * coarsen(shift_cells)]), 1, layout
    )
    coarse = section_cycle(gathered[0], gathered[1], 1, layout)
    correction = refine(unpick(coarse, undo_list))
    iterate = iterate + jnp.repeat(correction, P_SIZE, axis=2)
    update = source - fine_apply(iterate, operator)
    return iterate + relax_weight * update / fine_diagonal


def total(terms):
    return lax.psum(terms, ("gx", "gy", "gz"))


def per_device(right_side, element_class, class_blocks, class_shift, face_weights):
    size_x, size_y, width = right_side.shape
    size_z = width // P_SIZE
    classes = class_blocks.shape[0]
    element_count = size_x * size_y * size_z
    onehot = (
        element_class.reshape(element_count, 1) == jnp.arange(classes, dtype=jnp.int32)[None, :]
    ).astype(jnp.float32)
    wide_blocks = jnp.transpose(class_blocks, (2, 0, 1)).reshape(P_SIZE, classes * P_SIZE)
    operator = (onehot, wide_blocks, face_weights)
    diag_table = jnp.diagonal(class_blocks, axis1=1, axis2=2)
    fine_diagonal = jnp.dot(onehot, diag_table, precision=highest).reshape(size_x, size_y, width)
    shift_cells = jnp.dot(onehot, class_shift[:, None], precision=highest).reshape(
        size_x, size_y, size_z
    )
    row_totals = None
    bits_z = lax.axis_size("gz").bit_length() - 1
    bits_y = lax.axis_size("gy").bit_length() - 1
    layout = (
        (0, lax.axis_size("gx"), bits_z + bits_y, lax.axis_index("gx")),
        (1, lax.axis_size("gy"), bits_z, lax.axis_index("gy")),
        (2, lax.axis_size("gz"), 0, lax.axis_index("gz")),
    )
    context = (operator, fine_diagonal, shift_cells, row_totals, layout)
    residual = right_side
    smoothed = precondition(residual, context)
    gamma_now = total((jnp.sum(residual * smoothed),))[0]
    direction = smoothed
    image = fine_apply(direction, operator)
    step_size = gamma_now / total((jnp.sum(direction * image),))[0]
    solution_field = step_size * direction
    residual = residual - step_size * image
    smoothed = precondition(residual, context)
    gamma_next = total((jnp.sum(residual * smoothed),))[0]
    direction = smoothed + gamma_next / gamma_now * direction
    image = fine_apply(direction, operator)
    step_size = gamma_next / total((jnp.sum(direction * image),))[0]
    solution_field = solution_field + step_size * direction
    residual = residual - step_size * image
    return (solution_field, residual)


AXES = (2, 4, 4)
CELLS = 256
DEVICES = 32
MESSAGE = 384
NOTE_ROUNDS = 3
HALO_ROUNDS = 4
MESH = pl.DeviceIdType.MESH
f32 = jnp.float32


def iota(shape, dim):
    return lax.broadcasted_iota(jnp.int32, shape, dim)


def exact_dot(a, b, parts=2):
    a = a.astype(jnp.bfloat16)
    total_dot = None
    for _ in range(parts):
        part = b.astype(jnp.bfloat16)
        b = b - part.astype(f32)
        term = jnp.dot(a, part, preferred_element_type=f32)
        total_dot = term if total_dot is None else total_dot + term
    return total_dot


def neighbours(count, bits_y, bits_z, section_y, section_z):
    i, j = iota((count, count), 0), iota((count, count), 1)

    def split(k):
        return k >> bits_y + bits_z, k >> bits_z & (1 << bits_y) - 1, k & (1 << bits_z) - 1

    (xi, yi, zi), (xj, yj, zj) = split(i), split(j)
    apart = jnp.abs(xi - xj) + jnp.abs(yi - yj) + jnp.abs(zi - zj)
    same = ((yi >> section_y) == (yj >> section_y)) & ((zi >> section_z) == (zj >> section_z))
    return jnp.where((apart == 1) & same, 1.0, 0.0).astype(f32)


def where_one(hit):
    return jnp.where(hit, 1.0, 0.0).astype(f32)


def coarse_constants():
    beside_1 = neighbours(CELLS, 2, 4, 1, 3)
    beside_2 = neighbours(32, 1, 3, 1, 3)
    j2, cell = iota((32, CELLS), 0), iota((32, CELLS), 1)
    down_1 = where_one((cell >> 7) * 16 + (cell >> 5 & 1) * 8 + (cell >> 1 & 7) == j2)
    ci, cj = iota((CELLS, 32), 0), iota((CELLS, 32), 1)
    up_1 = where_one((ci >> 7) * 16 + (ci >> 5 & 1) * 8 + (ci >> 1 & 7) == cj)
    j3, k3 = iota((8, 32), 0), iota((8, 32), 1)
    down_2 = where_one((k3 >> 1 & 3) == j3)
    k2, i2 = iota((32, 8), 0), iota((32, 8), 1)
    up_2 = where_one((k2 >> 1 & 3) == i2)
    return (
        beside_1, beside_2, down_1, exact_dot(down_1, beside_1, 1),
        jnp.concatenate([up_1, exact_dot(beside_1, up_1, 1)], axis=0),
        jnp.concatenate([down_2, exact_dot(down_2, beside_2, 1)], axis=1),
        jnp.concatenate([up_2, exact_dot(beside_2, up_2, 1)], axis=0),
    )


def coarse_matrix(shift_row, constants):
    beside_1, beside_2, down_1, down_beside_1, up_1, down_2, up_2 = constants
    i, j = iota((CELLS, CELLS), 0), iota((CELLS, CELLS), 1)
    eye = where_one(i == j)
    d1_row = 6.0 + shift_row
    d1 = jnp.sum(eye * d1_row, axis=1, keepdims=True)
    d2 = 6.0 + 0.125 * jnp.sum(down_1 * shift_row, axis=1, keepdims=True)
    j3w, cellw = iota((8, CELLS), 0), iota((8, CELLS), 1)
    d3 = 6.0 + 0.015625 * jnp.sum(
        jnp.where((cellw >> 2 & 3) == j3w, shift_row, 0.0), axis=1, keepdims=True
    )
    q2 = 0.1 * down_1 + 0.15 * down_beside_1 / d1_row
    x2 = 0.6 * q2 / d2
    q3 = 0.25 * exact_dot(down_2, jnp.concatenate([0.4 * q2, x2], axis=0))
    beside_x2 = exact_dot(beside_2, x2)
    x3 = 0.6 * q3 / d3
    row = iota((8, CELLS), 0)
    for _ in range(SWEEPS - 1):
        after = jnp.where(row < 3, pltpu.roll(x3, 7, 0), 0.0)
        before = jnp.where((row > 0) & (row < 4), pltpu.roll(x3, 1, 0), 0.0)
        x3 = 0.4 * x3 + 0.6 * (q3 + after + before) / d3
    fine = exact_dot(up_2, x3)
    x2 = 0.4 * (x2 + fine[:32]) + 0.6 * (q2 + beside_x2 + fine[32:]) / d2
    fine = exact_dot(up_1, x2)
    x1 = 0.6 * eye / d1 + fine[:CELLS]
    beside_x1 = 0.6 * beside_1 / d1_row + fine[CELLS:]
    return 0.4 * x1 + 0.6 * (eye + beside_x1) / d1


def pick_cells(gx, gy, gz):
    rows = []
    s, cell = iota((8, CELLS), 0), iota((8, CELLS), 1)
    cx, cy, cz = cell >> 6, cell >> 4 & 3, cell & 15

    def pick(x, y, z):
        hit = (cx == ((gx * 4 + x) >> 1)) & (cy == ((gy * 2 + y) >> 1)) & (cz == gz * 4 + z)
        rows.append(jnp.where(hit, 1.0, 0.0).astype(f32))

    x, y = s >> 1, s & 1
    for dx, dy, zs in ((0, 0, range(-1, 5)), (1, 0, range(4)), (-1, 0, range(4)), (0, 1, range(4)), (0, -1, range(4))):
        for z in zs:
            pick(x + dx, y + dy, z)
    pairs = ((-1, y, s >> 1), (4, y, s >> 1))
    pairs += ((x, -1, 1 - y), (x, -1, 3 - y), (x, 2, y), (x, 2, y + 2), (x, y, -1), (x, y, 4))
    for gone_x, gone_y, gone_z in pairs:
        pick(gone_x, gone_y, gone_z)
        for dx, dy, dz in ((1, 0, 0), (-1, 0, 0), (0, 1, 0), (0, -1, 0), (0, 0, 1), (0, 0, -1)):
            pick(gone_x + dx, gone_y + dy, gone_z + dz)
    return jnp.concatenate(rows, axis=0)


def fused(
    r_hbm, class_hbm, blocks_hbm, shift_hbm, weight_hbm, out_ref,
    r_ref, class_ref, blocks_ref, shift_ref, weight_ref,
    halo_out, halo_in, note_out, note_in, w_ref, cells_ref, coarse_ref, pick_ref,
    load_sem, halo_send, halo_recv, note_send, note_recv, *const_refs,
):
    gx, gy, gz = lax.axis_index("gx"), lax.axis_index("gy"), lax.axis_index("gz")

    me = gx * 16 + gy * 4 + gz
    flip, chip, core = gy // 2, gz // 2, gz % 2
    near = gy + flip * (3 - 2 * gy)
    far_y = [k + flip * (3 - 2 * k) for k in (3, 2, 1 - near)] + [gy]
    far_z = [2 * (1 - chip) + 1 - core, 2 * (1 - chip) + core, 2 * chip + 1 - core, gz]
    others = [(x, y, z) for y in far_y for x in (1 - gx, gx) for z in far_z][:-1]
    barrier = pltpu.get_barrier_semaphore()
    halo_in[...] = jnp.zeros_like(halo_in)
    for to in others:
        pl.semaphore_signal(barrier, inc=1, device_id=to, device_id_type=MESH)
    loads = (
        (blocks_hbm, blocks_ref), (r_hbm, r_ref), (class_hbm, class_ref),
        (shift_hbm, shift_ref), (weight_hbm, weight_ref),
    )
    loads = [pltpu.make_async_copy(a, b, load_sem.at[i]) for i, (a, b) in enumerate(loads)]
    for load in loads:
        load.start()
    pick_ref[...] = pick_cells(gx, gy, gz).astype(jnp.bfloat16)
    for ref, value in zip(const_refs, coarse_constants()):
        ref[...] = value

    for load in loads:
        load.wait()

    lane = iota((8, 128), 1)
    sub = iota((8, 128), 0)
    low = lane < 64
    ni, nj, nk = lane >> 4 & 3, lane >> 2 & 3, lane & 3
    weights = [weight_ref[d] for d in range(3)]
    upper = [jnp.where(n == 3, w, 0.0) for n, w in zip((ni, nj, nk), weights)]
    lower = [jnp.where(n == 0, w, 0.0) for n, w in zip((ni, nj, nk), weights)]

    def widen(blocks):
        out = []
        for j in range(4):
            turned = pltpu.roll(blocks[j], 64, 1)
            out += [jnp.where(low, blocks[j], turned), jnp.where(low, turned, blocks[j])]
        return out

    def halves(u):
        return [jnp.where(low, u[2 * j], u[2 * j + 1]) for j in range(4)]

    flat = jnp.concatenate([r_ref[x] for x in range(4)], axis=0)
    right = widen([flat[:, 128 * j : 128 * j + 128] for j in range(4)])
    marks = jnp.concatenate([class_ref[x] for x in range(4)], axis=0)
    mark = [jnp.broadcast_to(marks[:, z : z + 1], (8, 128)) for z in range(8)]

    def by_class(rows):
        out = [jnp.broadcast_to(rows[0], (8, 128)) for _ in range(8)]
        for k in range(1, 16):
            out = [jnp.where(here == k, rows[k], old) for here, old in zip(mark, out)]
        return out

    def twice(row):
        return jnp.concatenate([row, row], axis=1)

    eye = iota((64, 64), 0) == iota((64, 64), 1)
    diag_rows = [
        twice(jnp.sum(jnp.where(eye, blocks_ref[k], 0.0), axis=0, keepdims=True)) for k in range(16)
    ]
    diagonal = by_class(diag_rows)
    inverse = [1.0 / d for d in diagonal]

    totals = by_class([twice(jnp.sum(blocks_ref[k], axis=0, keepdims=True)) for k in range(16)])
    shifts = by_class([shift_ref[k] for k in range(16)])

    def split_blocks():
        for k in range(16):
            rest = jnp.where(eye, 0.0, blocks_ref[k])
            rest_hi = rest.astype(jnp.bfloat16).astype(f32)
            both = jnp.concatenate([rest_hi, rest - rest_hi], axis=1)
            w_ref[64 * k : 64 * k + 64, :] = both.astype(jnp.bfloat16)

    own_cell = (sub >> 2) * 64 + gy * 16 + gz * 4

    def cell_row(columns, scale):
        row = jnp.zeros((8, 128), f32)
        for j in range(4):
            row = row + jnp.where(lane == own_cell + j, columns[j], 0.0)
        return scale * jnp.sum(row, axis=0, keepdims=True)

    note_lane = iota((1, 128), 1)

    def dots(*pairs):
        row = jnp.zeros((1, 128), f32)
        for at, (a, b) in enumerate(pairs):
            acc = a[0] * b[0]
            for z in range(1, 8):
                acc = acc + a[z] * b[z]
            acc = jnp.sum(jnp.sum(acc, axis=0, keepdims=True), axis=1, keepdims=True)
            row = row + jnp.where(note_lane == at, 0.5 * acc, 0.0)
        return row

    widths = (384, 384, 128)

    def note(ref, at, slot):
        return ref.at[at, slot, :, pl.ds(0, widths[at])]

    def tell(at, message):
        note_out[at, :, : widths[at]] = message
        note_in[at, me, :, : widths[at]] = message
        for to in others:
            pltpu.make_async_remote_copy(
                src_ref=note_out.at[at, :, pl.ds(0, widths[at])], dst_ref=note(note_in, at, me),
                send_sem=note_send.at[at], recv_sem=note_recv.at[at],
                device_id=to, device_id_type=MESH,
            ).start()

    def hear(at):
        span = note(note_in, at, pl.ds(0, DEVICES - 1))
        pltpu.make_async_copy(span, span, note_recv.at[at]).wait()
        return note_in[at, :, :, : widths[at]]

    def end_tell(at):
        span = note(note_in, at, pl.ds(0, DEVICES - 1))
        pltpu.make_async_copy(span, span, note_send.at[at]).wait()

    routes = (
        (0, 1, gx < AXES[0] - 1, gx > 0, (gx + 1, gy, gz)),
        (1, 1, gx > 0, gx < AXES[0] - 1, (gx - 1, gy, gz)),
        (2, 2, gy < AXES[1] - 1, gy > 0, (gx, gy + 1, gz)),
        (4, 2, gy > 0, gy < AXES[1] - 1, (gx, gy - 1, gz)),
        (6, 1, gz < AXES[2] - 1, gz > 0, (gx, gy, gz + 1)),
        (7, 1, gz > 0, gz < AXES[2] - 1, (gx, gy, gz - 1)),
    )

    def halo_copy(at, way):
        tile, count, _, _, to = routes[way]
        span = pl.ds(3 * tile, 3 * count if at == 1 else count)
        return pltpu.make_async_remote_copy(
            src_ref=halo_out.at[at, span], dst_ref=halo_in.at[at, span],
            send_sem=halo_send.at[at, way], recv_sem=halo_recv.at[at, way],
            device_id=to, device_id_type=MESH,
        )

    odd = (sub & 1) == 1

    places = [(0, 1, 0), (1, 1, 0), (2, 2, 0), (2, 2, 1), (4, 2, 0), (4, 2, 1), (6, 1, 0), (7, 1, 0)]

    def send_halo(at, *fields):
        for f, u in enumerate(fields):
            half = halves(u)
            up = jnp.where(sub >= 6, half[3], 0.0)
            down = jnp.where(sub < 2, half[0], 0.0)
            for m in range(3):
                up = jnp.where((sub >> 1) == m, pltpu.roll(half[m], (2 * m + 2) % 8, 0), up)
            for m in range(1, 4):
                down = jnp.where((sub >> 1) == m, pltpu.roll(half[m], 2 * m, 0), down)
            tiles = [up, down]
            tiles += [jnp.where(odd, half[2 * j], pltpu.roll(half[2 * j + 1], 7, 0)) for j in range(2)]
            tiles += [jnp.where(odd, pltpu.roll(half[2 * j + 1], 1, 0), half[2 * j]) for j in range(2)]
            tiles += [u[7], u[0]]
            for (tile, count, j), value in zip(places, tiles):
                halo_out[at, 3 * tile + f * count + j] = value
        for way in range(6):
            @pl.when(routes[way][2])
            def _():
                halo_copy(at, way).start()

    def ghosts(at, f=0):
        return [halo_in[at, 3 * tile + f * count + j] for tile, count, j in places]

    def wait_halo(at):
        for way in range(6):
            @pl.when(routes[way][3])
            def _():
                halo_copy(at, way).wait_recv()

    def end_halo(at):
        for way in range(6):
            @pl.when(routes[way][2])
            def _():
                halo_copy(at, way).wait_send()

    def turn(tile, by):
        return pltpu.roll(tile, by % 8, 0) if by % 8 else tile

    def unpack_x(packed, row):
        return widen([turn(packed, row - 2 * m) for m in range(4)])

    def local_part(u):
        top = jnp.concatenate(u, axis=0)
        top_hi = top.astype(jnp.bfloat16).astype(f32)
        top_lo = top - top_hi
        top = jnp.concatenate([top_hi, top_lo], axis=0)
        classes = jnp.concatenate(mark + mark, axis=0)
        kind = classes - (iota((128, 128), 1) >> 6)
        parts = [jnp.where(kind == 2 * p, top, 0.0).astype(jnp.bfloat16) for p in range(8)]
        out = jnp.dot(jnp.concatenate(parts, axis=1), w_ref[...], preferred_element_type=f32)
        out = out[:64] + out[64:]
        out = out + pltpu.roll(out, 64, 1)
        return [out[8 * z : 8 * z + 8] + diagonal[z] * u[z] for z in range(8)]

    def couple(u, got):
        x_before, x_after = unpack_x(got[0], 0), unpack_x(got[1], 6)
        y_before = widen([pltpu.roll(got[2], 7, 0), got[2], pltpu.roll(got[3], 7, 0), got[3]])
        y_after = widen([pltpu.roll(got[4], 1, 0), got[4], pltpu.roll(got[5], 1, 0), got[5]])
        out = []
        for z in range(8):
            x_next = jnp.where(sub >= 6, x_after[z], pltpu.roll(u[z], 6, 0))
            x_last = jnp.where(sub < 2, x_before[z], pltpu.roll(u[z], 2, 0))
            y_next = jnp.where(odd, y_after[z], pltpu.roll(u[z], 7, 0))
            y_last = jnp.where(odd, pltpu.roll(u[z], 1, 0), y_before[z])
            z_next = u[z + 1] if z < 7 else got[7]
            z_last = u[z - 1] if z > 0 else got[6]
            acc = upper[0] * pltpu.roll(x_next, 48, 1) + lower[0] * pltpu.roll(x_last, 80, 1)
            acc = acc + upper[1] * pltpu.roll(y_next, 12, 1) + lower[1] * pltpu.roll(y_last, 116, 1)
            acc = acc + upper[2] * pltpu.roll(z_next, 3, 1) + lower[2] * pltpu.roll(z_last, 125, 1)
            out.append(acc)
        return out

    def minus(a, b):
        return [p - q for p, q in zip(a, b)]

    def cell_message(w, v, totals):
        cell, s = iota((8, CELLS), 1), iota((8, CELLS), 0)

        def offset(dx, dy):
            x, y = (gx * 4 + (s >> 1) + dx) >> 1, (gy * 2 + (s & 1) + dy) >> 1
            inside = (x >= 0) & (x < 4) & (y >= 0) & (y < 4)
            return jnp.where(inside, cell - (x * 64 + y * 16 + gz * 4), 4096)

        def place(values, off, z):
            return jnp.where(off == z, jnp.sum(values, axis=1, keepdims=True), 0.0)

        pair = [0.6 * (v[2 * j] + v[2 * j + 1]) for j in range(4)]
        here = offset(0, 0)
        row = place(0.6 * lower[2] * v[0], here, jnp.where(gz > 0, -1, 8192))
        row = row + place(0.6 * upper[2] * v[7], here, jnp.where(gz < AXES[2] - 1, 4, 8192))
        for j in range(4):
            own = w[2 * j] + w[2 * j + 1] - 0.6 * (totals[2 * j] * v[2 * j] + totals[2 * j + 1] * v[2 * j + 1])
            to_next = v[2 * j] + v[2 * j - 1] if j > 0 else v[2 * j]
            to_last = v[2 * j + 1] + v[2 * j + 2] if j < 3 else v[2 * j + 1]
            row = row + place(own + 0.6 * (upper[2] * to_next + lower[2] * to_last), here, j)
        for d, up, down in ((0, offset(1, 0), offset(-1, 0)), (1, offset(0, 1), offset(0, -1))):
            for j in range(4):
                row = row + place(upper[d] * pair[j], up, j) + place(lower[d] * pair[j], down, j)
        return jnp.sum(row, axis=0, keepdims=True) * (1.0 / 128.0)

    def correct(picked, source, iterate, left, totals, at):
        tiles = [jnp.broadcast_to(picked[8 * t : 8 * t + 8], (8, 128)) for t in range(78)]
        own, x_up, x_down, y_up, y_down = tiles[:6], tiles[6:10], tiles[10:14], tiles[14:18], tiles[18:22]
        rest, scaled = [], []
        for z in range(8):
            j = z // 2
            image = totals[z] * own[j + 1]
            image = image - upper[0] * x_up[j] - lower[0] * x_down[j]
            image = image - upper[1] * y_up[j] - lower[1] * y_down[j]
            image = image - upper[2] * own[(z + 1) // 2 + 1] - lower[2] * own[(z - 1) // 2 + 1]
            rest.append(left[z] - image)
            scaled.append(rest[z] * inverse[z])
        own_part = local_part(scaled)
        wait_halo(at)
        got = []
        for g, (sent, inv, tot) in enumerate(zip(ghosts(at), ghosts(1, 1), ghosts(1, 2))):
            mid, xu, xd, yu, yd, zu, zd = tiles[22 + 7 * g : 29 + 7 * g]
            if g < 6:
                zu, zd = jnp.where(low, mid, zu), jnp.where(low, zd, mid)
            pull = upper[0] * xu + lower[0] * xd + upper[1] * yu + lower[1] * yd
            pull = pull + upper[2] * zu + lower[2] * zd
            got.append(sent - tot * mid + inv * pull)
        near = couple(scaled, got)
        result = [iterate[z] + own[z // 2 + 1] + 0.6 * scaled[z] for z in range(8)]
        image = [source[z] - rest[z] + 0.6 * (own_part[z] - near[z]) for z in range(8)]
        return result, image

    def scale(a, b):
        return [p * q for p, q in zip(a, b)]

    def remainder(source, own_part, iterate, at):
        wait_halo(at)
        return minus(source, minus(own_part, couple(iterate, ghosts(at))))

    spread = scale(right, inverse)
    first = [0.6 * a for a in spread]
    columns = [(shifts[2 * j] + shifts[2 * j + 1])[:, :1] for j in range(4)]
    message = [cell_row(columns, 0.125), cell_message(right, spread, totals)]
    pl.semaphore_wait(barrier, DEVICES - 1)
    send_halo(0, first)
    tell(0, jnp.concatenate(message, axis=1))
    split_blocks()
    own_part = local_part(first)
    left = remainder(right, own_part, first, 0)
    send_halo(1, scale(left, inverse), inverse, scale(totals, inverse))
    heard = hear(0)
    shift_row = [jnp.sum(heard[:16, :, :128], axis=0), jnp.sum(heard[16:, :, :128], axis=0)]
    cells = jnp.sum(heard[:, :, 128:], axis=0)
    same = iota((CELLS, CELLS), 0) == iota((CELLS, CELLS), 1)
    column = jnp.sum(jnp.where(same, cells, 0.0), axis=1, keepdims=True)
    coarse = coarse_matrix(jnp.concatenate(shift_row, axis=1), [ref[...] for ref in const_refs])
    coarse_ref[...] = coarse
    row = jnp.sum(coarse * column, axis=0, keepdims=True)
    picked = jnp.sum(pick_ref[...].astype(f32) * row, axis=1, keepdims=True)
    z0, w0 = correct(picked, right, first, left, totals, 1)

    spread = scale(w0, inverse)
    start = [0.6 * a for a in spread]
    send_halo(2, start)
    message = [cell_message(w0, spread, totals), dots((right, z0), (z0, w0))]
    tell(1, jnp.concatenate(message, axis=1))
    own_part = local_part(start)
    left = remainder(w0, own_part, start, 2)
    send_halo(3, scale(left, inverse))
    cells_ref[...] = exact_dot(pick_ref[...], coarse_ref[...], 3)
    heard = jnp.sum(hear(1), axis=0)
    gamma, curve = heard[:, CELLS : CELLS + 1], heard[:, CELLS + 1 : CELLS + 2]
    alpha = gamma / curve
    picked = jnp.sum(cells_ref[...] * heard[:, :CELLS], axis=1, keepdims=True)
    u, v = correct(picked, w0, start, left, totals, 3)
    z1 = [a - alpha * b for a, b in zip(z0, u)]
    w1 = [a - alpha * b for a, b in zip(w0, v)]
    r1 = [a - alpha * b for a, b in zip(right, w0)]
    tell(2, dots((r1, z1), (z1, w1), (z1, w0), (z0, w1)))
    for at in range(HALO_ROUNDS):
        end_halo(at)
    for at in range(2):
        end_tell(at)
    heard = jnp.sum(hear(2), axis=0)
    gamma_2 = heard[:, 0:1]
    beta = gamma_2 / gamma
    curve_2 = heard[:, 1:2] + beta * (heard[:, 2:3] + heard[:, 3:4]) + beta * beta * curve
    alpha_2 = gamma_2 / curve_2
    field = [alpha * a + alpha_2 * (b + beta * a) for a, b in zip(z0, z1)]
    rest = [a - alpha_2 * (b + beta * c) for a, b, c in zip(r1, w1, w0)]
    whole = jnp.concatenate(halves(field) + halves(rest), axis=1)
    for x in range(4):
        out_ref[x] = whole[2 * x : 2 * x + 2, :]
    end_tell(2)


def per_device_fused(right_side, element_class, class_blocks, class_shift, face_weights):
    vmem, hbm = pl.BlockSpec(memory_space=pltpu.VMEM), pl.BlockSpec(memory_space=pltpu.HBM)
    size_x, size_y, width = right_side.shape
    both = pl.pallas_call(
        fused,
        out_shape=jax.ShapeDtypeStruct((size_x, size_y, 2 * width), f32),
        in_specs=[hbm] * 5,
        out_specs=vmem,
        scratch_shapes=[
            pltpu.VMEM(right_side.shape, f32),
            pltpu.VMEM(element_class.shape, jnp.int32),
            pltpu.VMEM(class_blocks.shape, f32),
            pltpu.SMEM(class_shift.shape, f32),
            pltpu.SMEM(face_weights.shape, f32),
            pltpu.VMEM((HALO_ROUNDS, 24, 8, 128), f32),
            pltpu.VMEM((HALO_ROUNDS, 24, 8, 128), f32),
            pltpu.VMEM((NOTE_ROUNDS, 1, MESSAGE), f32),
            pltpu.VMEM((NOTE_ROUNDS, DEVICES, 1, MESSAGE), f32),
            pltpu.VMEM((1024, 128), jnp.bfloat16),
            pltpu.VMEM((624, CELLS), f32),
            pltpu.VMEM((CELLS, CELLS), f32),
            pltpu.VMEM((624, CELLS), jnp.bfloat16),
            pltpu.SemaphoreType.DMA((5,)),
            pltpu.SemaphoreType.DMA((HALO_ROUNDS, 6)),
            pltpu.SemaphoreType.DMA((HALO_ROUNDS, 6)),
            pltpu.SemaphoreType.DMA((NOTE_ROUNDS,)),
            pltpu.SemaphoreType.DMA((NOTE_ROUNDS,)),
            pltpu.VMEM((CELLS, CELLS), f32),
            pltpu.VMEM((32, 32), f32),
            pltpu.VMEM((32, CELLS), f32),
            pltpu.VMEM((32, CELLS), f32),
            pltpu.VMEM((2 * CELLS, 32), f32),
            pltpu.VMEM((8, 64), f32),
            pltpu.VMEM((64, 8), f32),
        ],
        compiler_params=pltpu.CompilerParams(
            collective_id=0, has_side_effects=True
        ),
    )(right_side, element_class, class_blocks, class_shift, face_weights)
    return both[:, :, :width], both[:, :, width:]


def solution(mesh):
    in_specs = (P("gx", "gy", "gz"), P("gx", "gy", "gz"), P(), P(), P())
    out_specs = (P("gx", "gy", "gz"), P("gx", "gy", "gz"))
    small = tuple(mesh.shape[axis] for axis in ("gx", "gy", "gz")) == AXES
    body = per_device_fused if small else per_device
    return jax.shard_map(
        body, mesh=mesh, in_specs=in_specs, out_specs=out_specs, check_vma=False
    )
```

```python
import jax
import jax.numpy as jnp
import numpy as np
from jax import lax
from jax.experimental import pallas as pl
from jax.experimental.pallas import tpu as pltpu
from jax.sharding import PartitionSpec as P

P_SIZE = 64
SWEEPS = 4


highest = lax.Precision.HIGHEST
relax_weight = 0.6


def with_halo(x, sides, width):
    for axis, dim in sides:
        size, length = (lax.axis_size(axis), x.shape[dim])
        up = [(i, (i + 1) % size) for i in range(size - 1)]
        down = [(j, i) for i, j in up]
        last = lax.slice_in_dim(x, length - width, length, axis=dim)
        first = lax.slice_in_dim(x, 0, width, axis=dim)
        before = lax.ppermute(last, axis, up)
        after = lax.ppermute(first, axis, down)
        x = jnp.concatenate([before, x, after], axis=dim)
    return x


def partner_2(x, axis, bit):
    return lax.ppermute(x, axis, [(i, i ^ 1 << bit) for i in range(lax.axis_size(axis))])


def face_tables():
    node_ids = np.arange(P_SIZE)
    digits = (node_ids // 16, node_ids // 4 % 4, node_ids % 4)
    strides = (48, 12, 3)
    lower_sets = [node_ids[digits[axis_dim] == 0] for axis_dim in range(3)]
    return (lower_sets, strides)


def full_matrix(face_weights):
    lower_sets, strides = face_tables()
    pieces = []
    for axis_dim in range(3):
        lower_ids = lower_sets[axis_dim]
        upper_ids = lower_ids + strides[axis_dim]
        from_next = np.zeros((P_SIZE, P_SIZE), np.float32)
        from_next[lower_ids, upper_ids] = 1.0
        from_prev = np.zeros((P_SIZE, P_SIZE), np.float32)
        from_prev[upper_ids, lower_ids] = 1.0
        pieces.append(face_weights[axis_dim] * jnp.asarray(from_next))
        pieces.append(face_weights[axis_dim] * jnp.asarray(from_prev))
    return jnp.concatenate(pieces, axis=0)


def couple_full(cubes, face_weights):
    count = cubes.shape[0] * cubes.shape[1] * cubes.shape[2]
    padded = with_halo(cubes, (("gx", 0), ("gy", 1), ("gz", 2)), 1)
    views = [
        padded[2:, 1:-1, 1:-1],
        padded[:-2, 1:-1, 1:-1],
        padded[1:-1, 2:, 1:-1],
        padded[1:-1, :-2, 1:-1],
        padded[1:-1, 1:-1, 2:],
        padded[1:-1, 1:-1, :-2],
    ]
    stacked = jnp.concatenate(views, axis=3).reshape(count, 6 * P_SIZE)
    return jnp.dot(stacked, full_matrix(face_weights), precision=highest)


def coarsen(values):
    size_x, size_y, size_z = values.shape
    return values.reshape(size_x // 2, 2, size_y // 2, 2, size_z // 2, 2).sum(axis=(1, 3, 5))


def refine(values):
    return jnp.repeat(jnp.repeat(jnp.repeat(values, 2, axis=0), 2, axis=1), 2, axis=2)


def section_apply(values, shift):
    padded = jnp.pad(values, ((1, 1), (1, 1), (1, 1)))
    beside = padded[2:, 1:-1, 1:-1] + padded[:-2, 1:-1, 1:-1]
    beside = beside + padded[1:-1, 2:, 1:-1] + padded[1:-1, :-2, 1:-1]
    beside = beside + padded[1:-1, 1:-1, 2:] + padded[1:-1, 1:-1, :-2]
    return (6.0 + shift) * values - beside


def assemble(stacked, depth, layout):
    undo_list = []
    for axis_dim, axis_count, bit_offset, my_index in layout:
        if axis_count >= 2**depth:
            partner = partner_2(stacked, ("gx", "gy", "gz"), bit_offset + depth - 1)
            upper_half = my_index >> depth - 1 & 1 == 1
            half_size = stacked.shape[axis_dim + 1]
            low_first = jnp.concatenate([stacked, partner], axis_dim + 1)
            high_first = jnp.concatenate([partner, stacked], axis_dim + 1)
            stacked = jnp.where(upper_half, high_first, low_first)
            undo_list.append((axis_dim, upper_half, half_size))
    return (stacked, undo_list)


def unpick(values, undo_list):
    for axis_dim, upper_half, half_size in reversed(undo_list):
        values = lax.dynamic_slice_in_dim(
            values, upper_half.astype(jnp.int32) * half_size, half_size, axis_dim
        )
    return values


def fine_apply(field, operator):
    onehot, wide_blocks, face_weights = operator
    size_x, size_y, width = field.shape
    size_z = width // P_SIZE
    count = size_x * size_y * size_z
    classes = onehot.shape[1]
    flat = field.reshape(count, P_SIZE)
    products = jnp.dot(flat, wide_blocks, precision=highest).reshape(count, classes, P_SIZE)
    local_part = jnp.einsum("ekn,ek->en", products, onehot, precision=highest)
    cubes = field.reshape(size_x, size_y, size_z, P_SIZE)
    nearby = couple_full(cubes, face_weights)
    return (local_part - nearby).reshape(size_x, size_y, width)


def section_cycle(source, shift, depth, layout):
    diagonal = 6.0 + shift
    if depth == 3:
        iterate = jnp.zeros_like(source)
        for sweep_index in range(SWEEPS):
            iterate = iterate + relax_weight * (source - section_apply(iterate, shift)) / diagonal
        return iterate
    iterate = relax_weight * source / diagonal
    remainder = source - section_apply(iterate, shift)
    gathered, undo_list = assemble(
        jnp.stack([0.25 * coarsen(remainder), 0.125 * coarsen(shift)]), depth + 1, layout
    )
    coarse = section_cycle(gathered[0], gathered[1], depth + 1, layout)
    iterate = iterate + refine(unpick(coarse, undo_list))
    return iterate + relax_weight * (source - section_apply(iterate, shift)) / diagonal


def precondition(source, context):
    operator, fine_diagonal, shift_cells, row_totals, layout = context
    iterate = relax_weight * source / fine_diagonal
    remainder = source - fine_apply(iterate, operator)
    size_x, size_y, width = source.shape
    sums = remainder.reshape(size_x, size_y, width // P_SIZE, P_SIZE).sum(axis=3)
    gathered, undo_list = assemble(
        jnp.stack([coarsen(sums) / float(P_SIZE), 0.125 * coarsen(shift_cells)]), 1, layout
    )
    coarse = section_cycle(gathered[0], gathered[1], 1, layout)
    correction = refine(unpick(coarse, undo_list))
    iterate = iterate + jnp.repeat(correction, P_SIZE, axis=2)
    update = source - fine_apply(iterate, operator)
    return iterate + relax_weight * update / fine_diagonal


def total(terms):
    return lax.psum(terms, ("gx", "gy", "gz"))


def per_device(right_side, element_class, class_blocks, class_shift, face_weights):
    size_x, size_y, width = right_side.shape
    size_z = width // P_SIZE
    classes = class_blocks.shape[0]
    element_count = size_x * size_y * size_z
    onehot = (
        element_class.reshape(element_count, 1) == jnp.arange(classes, dtype=jnp.int32)[None, :]
    ).astype(jnp.float32)
    wide_blocks = jnp.transpose(class_blocks, (2, 0, 1)).reshape(P_SIZE, classes * P_SIZE)
    operator = (onehot, wide_blocks, face_weights)
    diag_table = jnp.diagonal(class_blocks, axis1=1, axis2=2)
    fine_diagonal = jnp.dot(onehot, diag_table, precision=highest).reshape(size_x, size_y, width)
    shift_cells = jnp.dot(onehot, class_shift[:, None], precision=highest).reshape(
        size_x, size_y, size_z
    )
    row_totals = None
    bits_z = lax.axis_size("gz").bit_length() - 1
    bits_y = lax.axis_size("gy").bit_length() - 1
    layout = (
        (0, lax.axis_size("gx"), bits_z + bits_y, lax.axis_index("gx")),
        (1, lax.axis_size("gy"), bits_z, lax.axis_index("gy")),
        (2, lax.axis_size("gz"), 0, lax.axis_index("gz")),
    )
    context = (operator, fine_diagonal, shift_cells, row_totals, layout)
    residual = right_side
    smoothed = precondition(residual, context)
    gamma_now = total((jnp.sum(residual * smoothed),))[0]
    direction = smoothed
    image = fine_apply(direction, operator)
    step_size = gamma_now / total((jnp.sum(direction * image),))[0]
    solution_field = step_size * direction
    residual = residual - step_size * image
    smoothed = precondition(residual, context)
    gamma_next = total((jnp.sum(residual * smoothed),))[0]
    direction = smoothed + gamma_next / gamma_now * direction
    image = fine_apply(direction, operator)
    step_size = gamma_next / total((jnp.sum(direction * image),))[0]
    solution_field = solution_field + step_size * direction
    residual = residual - step_size * image
    return (solution_field, residual)


AXES = (2, 4, 4)
CELLS = 256
DEVICES = 32
MESSAGE = 384
NOTE_ROUNDS = 3
HALO_ROUNDS = 4
MESH = pl.DeviceIdType.MESH
f32 = jnp.float32


def iota(shape, dim):
    return lax.broadcasted_iota(jnp.int32, shape, dim)


def exact_dot(a, b, parts=2):
    a = a.astype(jnp.bfloat16)
    total_dot = None
    for _ in range(parts):
        part = b.astype(jnp.bfloat16)
        b = b - part.astype(f32)
        term = jnp.dot(a, part, preferred_element_type=f32)
        total_dot = term if total_dot is None else total_dot + term
    return total_dot


def neighbours(count, bits_y, bits_z, section_y, section_z):
    i, j = iota((count, count), 0), iota((count, count), 1)

    def split(k):
        return k >> bits_y + bits_z, k >> bits_z & (1 << bits_y) - 1, k & (1 << bits_z) - 1

    (xi, yi, zi), (xj, yj, zj) = split(i), split(j)
    apart = jnp.abs(xi - xj) + jnp.abs(yi - yj) + jnp.abs(zi - zj)
    same = ((yi >> section_y) == (yj >> section_y)) & ((zi >> section_z) == (zj >> section_z))
    return jnp.where((apart == 1) & same, 1.0, 0.0).astype(f32)


def where_one(hit):
    return jnp.where(hit, 1.0, 0.0).astype(f32)


def coarse_constants():
    beside_1 = neighbours(CELLS, 2, 4, 1, 3)
    beside_2 = neighbours(32, 1, 3, 1, 3)
    j2, cell = iota((32, CELLS), 0), iota((32, CELLS), 1)
    down_1 = where_one((cell >> 7) * 16 + (cell >> 5 & 1) * 8 + (cell >> 1 & 7) == j2)
    ci, cj = iota((CELLS, 32), 0), iota((CELLS, 32), 1)
    up_1 = where_one((ci >> 7) * 16 + (ci >> 5 & 1) * 8 + (ci >> 1 & 7) == cj)
    j3, k3 = iota((8, 32), 0), iota((8, 32), 1)
    down_2 = where_one((k3 >> 1 & 3) == j3)
    k2, i2 = iota((32, 8), 0), iota((32, 8), 1)
    up_2 = where_one((k2 >> 1 & 3) == i2)
    return (
        beside_1, beside_2, down_1, exact_dot(down_1, beside_1, 1),
        jnp.concatenate([up_1, exact_dot(beside_1, up_1, 1)], axis=0),
        jnp.concatenate([down_2, exact_dot(down_2, beside_2, 1)], axis=1),
        jnp.concatenate([up_2, exact_dot(beside_2, up_2, 1)], axis=0),
    )


def coarse_matrix(shift_row, constants):
    beside_1, beside_2, down_1, down_beside_1, up_1, down_2, up_2 = constants
    i, j = iota((CELLS, CELLS), 0), iota((CELLS, CELLS), 1)
    eye = where_one(i == j)
    d1_row = 6.0 + shift_row
    d1 = jnp.sum(eye * d1_row, axis=1, keepdims=True)
    d2 = 6.0 + 0.125 * jnp.sum(down_1 * shift_row, axis=1, keepdims=True)
    j3w, cellw = iota((8, CELLS), 0), iota((8, CELLS), 1)
    d3 = 6.0 + 0.015625 * jnp.sum(
        jnp.where((cellw >> 2 & 3) == j3w, shift_row, 0.0), axis=1, keepdims=True
    )
    q2 = 0.1 * down_1 + 0.15 * down_beside_1 / d1_row
    x2 = 0.6 * q2 / d2
    q3 = 0.25 * exact_dot(down_2, jnp.concatenate([0.4 * q2, x2], axis=0))
    beside_x2 = exact_dot(beside_2, x2)
    x3 = 0.6 * q3 / d3
    row = iota((8, CELLS), 0)
    for _ in range(SWEEPS - 1):
        after = jnp.where(row < 3, pltpu.roll(x3, 7, 0), 0.0)
        before = jnp.where((row > 0) & (row < 4), pltpu.roll(x3, 1, 0), 0.0)
        x3 = 0.4 * x3 + 0.6 * (q3 + after + before) / d3
    fine = exact_dot(up_2, x3)
    x2 = 0.4 * (x2 + fine[:32]) + 0.6 * (q2 + beside_x2 + fine[32:]) / d2
    fine = exact_dot(up_1, x2)
    x1 = 0.6 * eye / d1 + fine[:CELLS]
    beside_x1 = 0.6 * beside_1 / d1_row + fine[CELLS:]
    return 0.4 * x1 + 0.6 * (eye + beside_x1) / d1


def pick_cells(gx, gy, gz):
    rows = []
    s, cell = iota((8, CELLS), 0), iota((8, CELLS), 1)
    cx, cy, cz = cell >> 6, cell >> 4 & 3, cell & 15

    def pick(x, y, z):
        hit = (cx == ((gx * 4 + x) >> 1)) & (cy == ((gy * 2 + y) >> 1)) & (cz == gz * 4 + z)
        rows.append(jnp.where(hit, 1.0, 0.0).astype(f32))

    x, y = s >> 1, s & 1
    for dx, dy, zs in ((0, 0, range(-1, 5)), (1, 0, range(4)), (-1, 0, range(4)), (0, 1, range(4)), (0, -1, range(4))):
        for z in zs:
            pick(x + dx, y + dy, z)
    pairs = ((-1, y, s >> 1), (4, y, s >> 1))
    pairs += ((x, -1, 1 - y), (x, -1, 3 - y), (x, 2, y), (x, 2, y + 2), (x, y, -1), (x, y, 4))
    for gone_x, gone_y, gone_z in pairs:
        pick(gone_x, gone_y, gone_z)
        for dx, dy, dz in ((1, 0, 0), (-1, 0, 0), (0, 1, 0), (0, -1, 0), (0, 0, 1), (0, 0, -1)):
            pick(gone_x + dx, gone_y + dy, gone_z + dz)
    return jnp.concatenate(rows, axis=0)


def fused(
    r_hbm, class_hbm, blocks_hbm, shift_hbm, weight_hbm, out_ref,
    r_ref, class_ref, blocks_ref, shift_ref, weight_ref,
    halo_out, halo_in, note_out, note_in, w_ref, cells_ref, coarse_ref, pick_ref,
    load_sem, halo_send, halo_recv, note_send, note_recv, *const_refs,
):
    gx, gy, gz = lax.axis_index("gx"), lax.axis_index("gy"), lax.axis_index("gz")

    me = gx * 16 + gy * 4 + gz
    flip, chip, core = gy // 2, gz // 2, gz % 2
    near = gy + flip * (3 - 2 * gy)
    far_y = [k + flip * (3 - 2 * k) for k in (3, 2, 1 - near)] + [gy]
    far_z = [2 * (1 - chip) + 1 - core, 2 * (1 - chip) + core, 2 * chip + 1 - core, gz]
    others = [(x, y, z) for y in far_y for x in (1 - gx, gx) for z in far_z][:-1]
    barrier = pltpu.get_barrier_semaphore()
    halo_in[...] = jnp.zeros_like(halo_in)
    for to in others:
        pl.semaphore_signal(barrier, inc=1, device_id=to, device_id_type=MESH)
    loads = (
        (blocks_hbm, blocks_ref), (r_hbm, r_ref), (class_hbm, class_ref),
        (shift_hbm, shift_ref), (weight_hbm, weight_ref),
    )
    loads = [pltpu.make_async_copy(a, b, load_sem.at[i]) for i, (a, b) in enumerate(loads)]
    for load in loads:
        load.start()
    pick_ref[...] = pick_cells(gx, gy, gz).astype(jnp.bfloat16)

    for load in loads:
        load.wait()

    lane = iota((8, 128), 1)
    sub = iota((8, 128), 0)
    low = lane < 64
    ni, nj, nk = lane >> 4 & 3, lane >> 2 & 3, lane & 3
    weights = [weight_ref[d] for d in range(3)]
    upper = [jnp.where(n == 3, w, 0.0) for n, w in zip((ni, nj, nk), weights)]
    lower = [jnp.where(n == 0, w, 0.0) for n, w in zip((ni, nj, nk), weights)]

    def widen(blocks):
        out = []
        for j in range(4):
            turned = pltpu.roll(blocks[j], 64, 1)
            out += [jnp.where(low, blocks[j], turned), jnp.where(low, turned, blocks[j])]
        return out

    def halves(u):
        return [jnp.where(low, u[2 * j], u[2 * j + 1]) for j in range(4)]

    flat = jnp.concatenate([r_ref[x] for x in range(4)], axis=0)
    right = widen([flat[:, 128 * j : 128 * j + 128] for j in range(4)])
    marks = jnp.concatenate([class_ref[x] for x in range(4)], axis=0)
    mark = [jnp.broadcast_to(marks[:, z : z + 1], (8, 128)) for z in range(8)]

    def by_class(rows):
        out = [jnp.broadcast_to(rows[0], (8, 128)) for _ in range(8)]
        for k in range(1, 16):
            out = [jnp.where(here == k, rows[k], old) for here, old in zip(mark, out)]
        return out

    def twice(row):
        return jnp.concatenate([row, row], axis=1)

    eye = iota((64, 64), 0) == iota((64, 64), 1)
    diag_rows = [
        twice(jnp.sum(jnp.where(eye, blocks_ref[k], 0.0), axis=0, keepdims=True)) for k in range(16)
    ]
    diagonal = by_class(diag_rows)
    inverse = [1.0 / d for d in diagonal]

    totals = by_class([twice(jnp.sum(blocks_ref[k], axis=0, keepdims=True)) for k in range(16)])
    shifts = by_class([shift_ref[k] for k in range(16)])

    def split_blocks():
        for k in range(16):
            rest = jnp.where(eye, 0.0, blocks_ref[k])
            rest_hi = rest.astype(jnp.bfloat16).astype(f32)
            both = jnp.concatenate([rest_hi, rest - rest_hi], axis=1)
            w_ref[64 * k : 64 * k + 64, :] = both.astype(jnp.bfloat16)

    own_cell = (sub >> 2) * 64 + gy * 16 + gz * 4

    def cell_row(columns, scale):
        row = jnp.zeros((8, 128), f32)
        for j in range(4):
            row = row + jnp.where(lane == own_cell + j, columns[j], 0.0)
        return scale * jnp.sum(row, axis=0, keepdims=True)

    note_lane = iota((1, 128), 1)

    def dots(*pairs):
        row = jnp.zeros((1, 128), f32)
        for at, (a, b) in enumerate(pairs):
            acc = a[0] * b[0]
            for z in range(1, 8):
                acc = acc + a[z] * b[z]
            acc = jnp.sum(jnp.sum(acc, axis=0, keepdims=True), axis=1, keepdims=True)
            row = row + jnp.where(note_lane == at, 0.5 * acc, 0.0)
        return row

    widths = (384, 384, 128)

    def note(ref, at, slot):
        return ref.at[at, slot, :, pl.ds(0, widths[at])]

    def tell(at, message):
        note_out[at, :, : widths[at]] = message
        note_in[at, me, :, : widths[at]] = message
        for to in others:
            pltpu.make_async_remote_copy(
                src_ref=note_out.at[at, :, pl.ds(0, widths[at])], dst_ref=note(note_in, at, me),
                send_sem=note_send.at[at], recv_sem=note_recv.at[at],
                device_id=to, device_id_type=MESH,
            ).start()

    def hear(at):
        span = note(note_in, at, pl.ds(0, DEVICES - 1))
        pltpu.make_async_copy(span, span, note_recv.at[at]).wait()
        return note_in[at, :, :, : widths[at]]

    def end_tell(at):
        span = note(note_in, at, pl.ds(0, DEVICES - 1))
        pltpu.make_async_copy(span, span, note_send.at[at]).wait()

    routes = (
        (0, 1, gx < AXES[0] - 1, gx > 0, (gx + 1, gy, gz)),
        (1, 1, gx > 0, gx < AXES[0] - 1, (gx - 1, gy, gz)),
        (2, 2, gy < AXES[1] - 1, gy > 0, (gx, gy + 1, gz)),
        (4, 2, gy > 0, gy < AXES[1] - 1, (gx, gy - 1, gz)),
        (6, 1, gz < AXES[2] - 1, gz > 0, (gx, gy, gz + 1)),
        (7, 1, gz > 0, gz < AXES[2] - 1, (gx, gy, gz - 1)),
    )

    def halo_copy(at, way):
        tile, count, _, _, to = routes[way]
        span = pl.ds(3 * tile, 3 * count if at == 1 else count)
        return pltpu.make_async_remote_copy(
            src_ref=halo_out.at[at, span], dst_ref=halo_in.at[at, span],
            send_sem=halo_send.at[at, way], recv_sem=halo_recv.at[at, way],
            device_id=to, device_id_type=MESH,
        )

    odd = (sub & 1) == 1

    places = [(0, 1, 0), (1, 1, 0), (2, 2, 0), (2, 2, 1), (4, 2, 0), (4, 2, 1), (6, 1, 0), (7, 1, 0)]

    def send_halo(at, *fields):
        for f, u in enumerate(fields):
            half = halves(u)
            up = jnp.where(sub >= 6, half[3], 0.0)
            down = jnp.where(sub < 2, half[0], 0.0)
            for m in range(3):
                up = jnp.where((sub >> 1) == m, pltpu.roll(half[m], (2 * m + 2) % 8, 0), up)
            for m in range(1, 4):
                down = jnp.where((sub >> 1) == m, pltpu.roll(half[m], 2 * m, 0), down)
            tiles = [up, down]
            tiles += [jnp.where(odd, half[2 * j], pltpu.roll(half[2 * j + 1], 7, 0)) for j in range(2)]
            tiles += [jnp.where(odd, pltpu.roll(half[2 * j + 1], 1, 0), half[2 * j]) for j in range(2)]
            tiles += [u[7], u[0]]
            for (tile, count, j), value in zip(places, tiles):
                halo_out[at, 3 * tile + f * count + j] = value
        for way in range(6):
            @pl.when(routes[way][2])
            def _():
                halo_copy(at, way).start()

    def ghosts(at, f=0):
        return [halo_in[at, 3 * tile + f * count + j] for tile, count, j in places]

    def wait_halo(at):
        for way in range(6):
            @pl.when(routes[way][3])
            def _():
                halo_copy(at, way).wait_recv()

    def end_halo(at):
        for way in range(6):
            @pl.when(routes[way][2])
            def _():
                halo_copy(at, way).wait_send()

    def turn(tile, by):
        return pltpu.roll(tile, by % 8, 0) if by % 8 else tile

    def unpack_x(packed, row):
        return widen([turn(packed, row - 2 * m) for m in range(4)])

    def local_part(u):
        top = jnp.concatenate(u, axis=0)
        top_hi = top.astype(jnp.bfloat16).astype(f32)
        top_lo = top - top_hi
        top = jnp.concatenate([top_hi, top_lo], axis=0)
        classes = jnp.concatenate(mark + mark, axis=0)
        kind = classes - (iota((128, 128), 1) >> 6)
        parts = [jnp.where(kind == 2 * p, top, 0.0).astype(jnp.bfloat16) for p in range(8)]
        out = jnp.dot(jnp.concatenate(parts, axis=1), w_ref[...], preferred_element_type=f32)
        out = out[:64] + out[64:]
        out = out + pltpu.roll(out, 64, 1)
        return [out[8 * z : 8 * z + 8] + diagonal[z] * u[z] for z in range(8)]

    def couple(u, got):
        x_before, x_after = unpack_x(got[0], 0), unpack_x(got[1], 6)
        y_before = widen([pltpu.roll(got[2], 7, 0), got[2], pltpu.roll(got[3], 7, 0), got[3]])
        y_after = widen([pltpu.roll(got[4], 1, 0), got[4], pltpu.roll(got[5], 1, 0), got[5]])
        out = []
        for z in range(8):
            x_next = jnp.where(sub >= 6, x_after[z], pltpu.roll(u[z], 6, 0))
            x_last = jnp.where(sub < 2, x_before[z], pltpu.roll(u[z], 2, 0))
            y_next = jnp.where(odd, y_after[z], pltpu.roll(u[z], 7, 0))
            y_last = jnp.where(odd, pltpu.roll(u[z], 1, 0), y_before[z])
            z_next = u[z + 1] if z < 7 else got[7]
            z_last = u[z - 1] if z > 0 else got[6]
            acc = upper[0] * pltpu.roll(x_next, 48, 1) + lower[0] * pltpu.roll(x_last, 80, 1)
            acc = acc + upper[1] * pltpu.roll(y_next, 12, 1) + lower[1] * pltpu.roll(y_last, 116, 1)
            acc = acc + upper[2] * pltpu.roll(z_next, 3, 1) + lower[2] * pltpu.roll(z_last, 125, 1)
            out.append(acc)
        return out

    def minus(a, b):
        return [p - q for p, q in zip(a, b)]

    def cell_message(w, v, totals):
        cell, s = iota((8, CELLS), 1), iota((8, CELLS), 0)

        def offset(dx, dy):
            x, y = (gx * 4 + (s >> 1) + dx) >> 1, (gy * 2 + (s & 1) + dy) >> 1
            inside = (x >= 0) & (x < 4) & (y >= 0) & (y < 4)
            return jnp.where(inside, cell - (x * 64 + y * 16 + gz * 4), 4096)

        def place(values, off, z):
            return jnp.where(off == z, jnp.sum(values, axis=1, keepdims=True), 0.0)

        pair = [0.6 * (v[2 * j] + v[2 * j + 1]) for j in range(4)]
        here = offset(0, 0)
        row = place(0.6 * lower[2] * v[0], here, jnp.where(gz > 0, -1, 8192))
        row = row + place(0.6 * upper[2] * v[7], here, jnp.where(gz < AXES[2] - 1, 4, 8192))
        for j in range(4):
            own = w[2 * j] + w[2 * j + 1] - 0.6 * (totals[2 * j] * v[2 * j] + totals[2 * j + 1] * v[2 * j + 1])
            to_next = v[2 * j] + v[2 * j - 1] if j > 0 else v[2 * j]
            to_last = v[2 * j + 1] + v[2 * j + 2] if j < 3 else v[2 * j + 1]
            row = row + place(own + 0.6 * (upper[2] * to_next + lower[2] * to_last), here, j)
        for d, up, down in ((0, offset(1, 0), offset(-1, 0)), (1, offset(0, 1), offset(0, -1))):
            for j in range(4):
                row = row + place(upper[d] * pair[j], up, j) + place(lower[d] * pair[j], down, j)
        return jnp.sum(row, axis=0, keepdims=True) * (1.0 / 128.0)

    def correct(picked, source, iterate, left, totals, at):
        tiles = [jnp.broadcast_to(picked[8 * t : 8 * t + 8], (8, 128)) for t in range(78)]
        own, x_up, x_down, y_up, y_down = tiles[:6], tiles[6:10], tiles[10:14], tiles[14:18], tiles[18:22]
        rest, scaled = [], []
        for z in range(8):
            j = z // 2
            image = totals[z] * own[j + 1]
            image = image - upper[0] * x_up[j] - lower[0] * x_down[j]
            image = image - upper[1] * y_up[j] - lower[1] * y_down[j]
            image = image - upper[2] * own[(z + 1) // 2 + 1] - lower[2] * own[(z - 1) // 2 + 1]
            rest.append(left[z] - image)
            scaled.append(rest[z] * inverse[z])
        own_part = local_part(scaled)
        wait_halo(at)
        got = []
        for g, (sent, inv, tot) in enumerate(zip(ghosts(at), ghosts(1, 1), ghosts(1, 2))):
            mid, xu, xd, yu, yd, zu, zd = tiles[22 + 7 * g : 29 + 7 * g]
            if g < 6:
                zu, zd = jnp.where(low, mid, zu), jnp.where(low, zd, mid)
            pull = upper[0] * xu + lower[0] * xd + upper[1] * yu + lower[1] * yd
            pull = pull + upper[2] * zu + lower[2] * zd
            got.append(sent - tot * mid + inv * pull)
        near = couple(scaled, got)
        result = [iterate[z] + own[z // 2 + 1] + 0.6 * scaled[z] for z in range(8)]
        image = [source[z] - rest[z] + 0.6 * (own_part[z] - near[z]) for z in range(8)]
        return result, image

    def scale(a, b):
        return [p * q for p, q in zip(a, b)]

    def remainder(source, own_part, iterate, at):
        wait_halo(at)
        return minus(source, minus(own_part, couple(iterate, ghosts(at))))

    spread = scale(right, inverse)
    first = [0.6 * a for a in spread]
    columns = [(shifts[2 * j] + shifts[2 * j + 1])[:, :1] for j in range(4)]
    message = [cell_row(columns, 0.125), cell_message(right, spread, totals)]
    pl.semaphore_wait(barrier, DEVICES - 1)
    send_halo(0, first)
    tell(0, jnp.concatenate(message, axis=1))
    split_blocks()
    own_part = local_part(first)
    for ref, value in zip(const_refs, coarse_constants()):
        ref[...] = value
    left = remainder(right, own_part, first, 0)
    send_halo(1, scale(left, inverse), inverse, scale(totals, inverse))
    heard = hear(0)
    shift_row = [jnp.sum(heard[:16, :, :128], axis=0), jnp.sum(heard[16:, :, :128], axis=0)]
    cells = jnp.sum(heard[:, :, 128:], axis=0)
    same = iota((CELLS, CELLS), 0) == iota((CELLS, CELLS), 1)
    column = jnp.sum(jnp.where(same, cells, 0.0), axis=1, keepdims=True)
    coarse = coarse_matrix(jnp.concatenate(shift_row, axis=1), [ref[...] for ref in const_refs])
    coarse_ref[...] = coarse
    row = jnp.sum(coarse * column, axis=0, keepdims=True)
    picked = jnp.sum(pick_ref[...].astype(f32) * row, axis=1, keepdims=True)
    z0, w0 = correct(picked, right, first, left, totals, 1)

    spread = scale(w0, inverse)
    start = [0.6 * a for a in spread]
    send_halo(2, start)
    message = [cell_message(w0, spread, totals), dots((right, z0), (z0, w0))]
    tell(1, jnp.concatenate(message, axis=1))
    own_part = local_part(start)
    left = remainder(w0, own_part, start, 2)
    send_halo(3, scale(left, inverse))
    cells_ref[...] = exact_dot(pick_ref[...], coarse_ref[...], 3)
    heard = jnp.sum(hear(1), axis=0)
    gamma, curve = heard[:, CELLS : CELLS + 1], heard[:, CELLS + 1 : CELLS + 2]
    alpha = gamma / curve
    picked = jnp.sum(cells_ref[...] * heard[:, :CELLS], axis=1, keepdims=True)
    u, v = correct(picked, w0, start, left, totals, 3)
    z1 = [a - alpha * b for a, b in zip(z0, u)]
    w1 = [a - alpha * b for a, b in zip(w0, v)]
    r1 = [a - alpha * b for a, b in zip(right, w0)]
    tell(2, dots((r1, z1), (z1, w1), (z1, w0)))
    for at in range(HALO_ROUNDS):
        end_halo(at)
    for at in range(2):
        end_tell(at)
    heard = jnp.sum(hear(2), axis=0)
    gamma_2 = heard[:, 0:1]
    beta = gamma_2 / gamma
    curve_2 = heard[:, 1:2] + beta * (2.0 * heard[:, 2:3] + beta * curve)
    alpha_2 = gamma_2 / curve_2
    field = [alpha * a + alpha_2 * (b + beta * a) for a, b in zip(z0, z1)]
    rest = [a - alpha_2 * (b + beta * c) for a, b, c in zip(r1, w1, w0)]
    whole = jnp.concatenate(halves(field) + halves(rest), axis=1)
    for x in range(4):
        out_ref[x] = whole[2 * x : 2 * x + 2, :]
    end_tell(2)


def per_device_fused(right_side, element_class, class_blocks, class_shift, face_weights):
    vmem, hbm = pl.BlockSpec(memory_space=pltpu.VMEM), pl.BlockSpec(memory_space=pltpu.HBM)
    size_x, size_y, width = right_side.shape
    both = pl.pallas_call(
        fused,
        out_shape=jax.ShapeDtypeStruct((size_x, size_y, 2 * width), f32),
        in_specs=[hbm] * 5,
        out_specs=vmem,
        scratch_shapes=[
            pltpu.VMEM(right_side.shape, f32),
            pltpu.VMEM(element_class.shape, jnp.int32),
            pltpu.VMEM(class_blocks.shape, f32),
            pltpu.SMEM(class_shift.shape, f32),
            pltpu.SMEM(face_weights.shape, f32),
            pltpu.VMEM((HALO_ROUNDS, 24, 8, 128), f32),
            pltpu.VMEM((HALO_ROUNDS, 24, 8, 128), f32),
            pltpu.VMEM((NOTE_ROUNDS, 1, MESSAGE), f32),
            pltpu.VMEM((NOTE_ROUNDS, DEVICES, 1, MESSAGE), f32),
            pltpu.VMEM((1024, 128), jnp.bfloat16),
            pltpu.VMEM((624, CELLS), f32),
            pltpu.VMEM((CELLS, CELLS), f32),
            pltpu.VMEM((624, CELLS), jnp.bfloat16),
            pltpu.SemaphoreType.DMA((5,)),
            pltpu.SemaphoreType.DMA((HALO_ROUNDS, 6)),
            pltpu.SemaphoreType.DMA((HALO_ROUNDS, 6)),
            pltpu.SemaphoreType.DMA((NOTE_ROUNDS,)),
            pltpu.SemaphoreType.DMA((NOTE_ROUNDS,)),
            pltpu.VMEM((CELLS, CELLS), f32),
            pltpu.VMEM((32, 32), f32),
            pltpu.VMEM((32, CELLS), f32),
            pltpu.VMEM((32, CELLS), f32),
            pltpu.VMEM((2 * CELLS, 32), f32),
            pltpu.VMEM((8, 64), f32),
            pltpu.VMEM((64, 8), f32),
        ],
        compiler_params=pltpu.CompilerParams(
            collective_id=0, has_side_effects=True
        ),
    )(right_side, element_class, class_blocks, class_shift, face_weights)
    return both[:, :, :width], both[:, :, width:]


def solution(mesh):
    in_specs = (P("gx", "gy", "gz"), P("gx", "gy", "gz"), P(), P(), P())
    out_specs = (P("gx", "gy", "gz"), P("gx", "gy", "gz"))
    small = tuple(mesh.shape[axis] for axis in ("gx", "gy", "gz")) == AXES
    body = per_device_fused if small else per_device
    return jax.shard_map(
        body, mesh=mesh, in_specs=in_specs, out_specs=out_specs, check_vma=False
    )
```
